512 devices in a mesh: section: 16 (over x, z_hi), mp: 8 (over y, core), dp: 4 (over z_lo).
Axes of the slice: x: 4, y: 4, z: 16 (z_hi: 4, z_lo: 4; z = z_hi * 4 + z_lo), core: 2. Of those that a mesh axis runs over, the one named last changes fastest.
Arguments:
- section_inputs: bfloat16 [16, 8, 64, 5120], P('section', None, 'dp'), may hold values from -480 to 480
- out_grads: bfloat16 [8, 64, 5120], P(None, 'dp'), may hold values from -6 to 6
- proj_weight: bfloat16 [16, 5120, 5120], P('section', 'mp', 'dp'), may hold values from -0.13975425 to 0.13975425
- norm_gain: float32 [16, 5120], P('section', 'mp'), may hold values from 0.1 to 1.9
- adapter_down: bfloat16 [16, 8, 5120, 16], P('section', None, 'mp'), may hold values from -0.078125 to 0.078125
- adapter_up: bfloat16 [16, 8, 16, 5120], P('section'), may hold values from -0.25 to 0.25
- tenant_ids: int32 [8], replicated, may hold values from 0 to 7, each once
- slot_table: int32 [16, 8], P('section'), may hold values from 0 to 7, each once within a row
Outputs:
- input_grads: bfloat16 [16, 8, 64, 5120], P('section', None, 'dp', 'mp')
- down_grads: float32 [16, 8, 5120, 16], P('section', None, 'mp')
- up_grads: float32 [16, 8, 16, 5120], P('section', None, None, 'mp')
The draws below stay inside these ranges and needn't reach their ends.
Inputs may be any that keep to these rules, and one draw needn't show every extreme that they name: `tenant_ids`: each micro-batch belongs to another tenant. `slot_table`: each row is a permutation.
All inputs are finite; a program needn't handle non-finite values.
Results may differ from the reference program's by a relative error of at most 0.015.
Values may be sent and summed in bfloat16 or wider, within the bound.
No kernel may reach another device: no remote copies, remote signals or barrier semaphores. Data moves between devices by JAX's collectives and lax.ppermute only.
A program may use at most 64 MiB of HBM per device.

```python
import math
import jax
import jax.numpy as jnp
from jax import lax

D = 5120
R = 16
MB = 8
SECTIONS = 16
TOKENS = 64


def shared_direction(key):
    common_key = jax.random.fold_in(key, 5)
    return jnp.clip(jax.random.normal(common_key, (SECTIONS, D), jnp.float32), -3.0, 3.0)


def draw_section_inputs(key, part):
    common = shared_direction(key)
    key = jax.random.fold_in(key, 11)
    first, second, third = jax.random.split(key, 3)
    full_shape = (SECTIONS, MB, TOKENS, D)
    common_rows = common.reshape(SECTIONS, 1, 1, D)
    base_vals = jnp.clip(jax.random.normal(first, full_shape, jnp.float32), -4.0, 4.0) + 0.8 * common_rows
    row_scale = jnp.exp(jax.random.uniform(second, (SECTIONS, MB, TOKENS, 1), jnp.float32, math.log(1.5), math.log(15.0)))
    feature_pos = jnp.arange(D, dtype=jnp.float32) / D
    rising = jnp.exp(math.log(0.25) + feature_pos * math.log(10.0)).reshape(1, 1, 1, D)
    col_scale = rising * jnp.exp(jax.random.uniform(third, (SECTIONS, 1, 1, D), jnp.float32, math.log(0.5), math.log(2.0)))
    return (base_vals * row_scale * col_scale).astype(jnp.bfloat16)


def draw_proj_weight(key, part):
    common = shared_direction(key)
    key = jax.random.fold_in(key, 23)
    first, second = jax.random.split(key, 2)
    outward = jnp.clip(jax.random.normal(second, (SECTIONS, D), jnp.float32), -3.0, 3.0)
    inv_root = 1.0 / math.sqrt(D)
    bound = 10.0 * inv_root

    def one_section(section_idx):
        noise_key = jax.random.fold_in(first, section_idx)
        noise = jnp.clip(jax.random.normal(noise_key, (D, D), jnp.float32), -4.0, 4.0)
        along = lax.dynamic_index_in_dim(common, section_idx, 0, keepdims=False)
        across = lax.dynamic_index_in_dim(outward, section_idx, 0, keepdims=False)
        full = (noise + along[:, None] * across[None, :]) * inv_root
        return jnp.clip(full, -bound, bound).astype(jnp.bfloat16)
    return lax.map(one_section, jnp.arange(SECTIONS, dtype=jnp.int32))


def block_scale(stream_key, shape, pieces, least, top_value):
    def one(axis_at, blocks):
        heights = jax.random.uniform(jax.random.fold_in(jax.random.fold_in(stream_key, 6), axis_at), (blocks,), jnp.float32, least / len(pieces), top_value / len(pieces))
        return jnp.repeat(jnp.exp(heights), shape[axis_at] // blocks).reshape((-1,) + (1,) * (len(shape) - axis_at - 1))

    factor_of = one(*pieces[0])
    for cut in pieces[1:]:
        factor_of = factor_of * one(*cut)
    return factor_of


def bell_draw(stream_key, dims, width, most, cuts=(), kind=jnp.bfloat16):
    values = width * jax.random.normal(stream_key, dims, jnp.float32)
    if cuts:
        values = values * block_scale(stream_key, dims, cuts, -0.22, 0.18)
    return jnp.clip(values, -most, most).astype(kind)


def setup_inputs(seed: int = 0) -> dict:
    seeds = jax.random.split(jax.random.key(seed), 9)
    section_inputs = draw_section_inputs(jax.random.fold_in(seeds[8], 71), 0)
    out_grads = bell_draw(seeds[1], (MB, TOKENS, D), 1.0, 6.0, ((1, 4),))
    proj_weight = draw_proj_weight(jax.random.fold_in(seeds[8], 71), 0)
    norm_gain = jnp.clip(1.0 + 0.18 * jax.random.normal(seeds[3], (SECTIONS, D), jnp.float32), 0.1, 1.9)
    adapter_down = bell_draw(seeds[4], (SECTIONS, MB, D, R), D ** -0.5, 0.078125, ((0, 16), (2, 8)))
    adapter_up = bell_draw(seeds[5], (SECTIONS, MB, R, D), (D // 8) ** -0.5, 0.25, ((0, 16),))
    tenant_ids = jax.random.permutation(seeds[6], MB).astype(jnp.int32)
    slot_table = jax.vmap(lambda own: jax.random.permutation(own, MB))(jax.random.split(seeds[7], SECTIONS)).reshape((SECTIONS, MB)).astype(jnp.int32)
    return {"section_inputs": section_inputs, "out_grads": out_grads, "proj_weight": proj_weight, "norm_gain": norm_gain, "adapter_down": adapter_down, "adapter_up": adapter_up, "tenant_ids": tenant_ids, "slot_table": slot_table}


norm_eps = 1e-05
low_rank_scale = 2.0

def reference(section_inputs, out_grads, proj_weight, norm_gain, adapter_down, adapter_up, tenant_ids, slot_table):
    grad_rows = out_grads
    gathered_tokens = out_grads.shape[1]
    multiplier = low_rank_scale / gathered_tokens
    input_list = []
    down_list = []
    up_list = []
    for section_pos in range(SECTIONS - 1, -1, -1):
        inputs = section_inputs[section_pos].astype(jnp.float32)
        inv_rms = lax.rsqrt(lax.optimization_barrier(jnp.mean(inputs * inputs, axis=-1, keepdims=True)) + norm_eps)
        normed = inputs * inv_rms
        hidden = (normed * norm_gain[section_pos]).astype(jnp.bfloat16)
        slot_ids = slot_table[section_pos][tenant_ids].astype(jnp.int32)
        selected_down_weight = adapter_down[section_pos][slot_ids].astype(jnp.float32)
        up_sel = adapter_up[section_pos][slot_ids].astype(jnp.float32)
        grads_f = grad_rows.astype(jnp.float32)
        hidden_f = hidden.astype(jnp.float32)
        low_in = jnp.einsum('mtd,mdr->mtr', hidden_f, selected_down_weight).astype(jnp.bfloat16)
        low_rank_output = jnp.einsum('mtd,mrd->mtr', grads_f, up_sel).astype(jnp.bfloat16)
        frozen_path_gradient = jnp.dot(grad_rows.reshape(-1, D), proj_weight[section_pos].T, preferred_element_type=jnp.float32)
        frozen_path_gradient = frozen_path_gradient.reshape(grad_rows.shape)
        hidden_state_gradient = frozen_path_gradient + low_rank_scale * jnp.einsum('aex,afx->aef', low_rank_output.astype(jnp.float32), selected_down_weight)
        normalized_gradient = (hidden_state_gradient * norm_gain[section_pos]).astype(jnp.bfloat16)
        norm_rows = normalized_gradient.astype(jnp.float32)
        row_stat = lax.optimization_barrier(jnp.mean(norm_rows * normed, axis=-1, keepdims=True))
        new_grads = (grads_f + inv_rms * (norm_rows - normed * row_stat)).astype(jnp.bfloat16)
        down_term = multiplier * jnp.einsum('mtd,mtr->mdr', hidden_f, low_rank_output.astype(jnp.float32))
        up_term = multiplier * jnp.einsum('mtr,mtd->mrd', low_in.astype(jnp.float32), grads_f)
        down_list.append(jnp.zeros_like(down_term).at[slot_ids].set(down_term))
        up_list.append(jnp.zeros_like(up_term).at[slot_ids].set(up_term))
        input_list.append(new_grads)
        grad_rows = new_grads
    input_order = input_list[::-1]
    down_order = down_list[::-1]
    up_order = up_list[::-1]
    return (jnp.stack(input_order), jnp.stack(down_order), jnp.stack(up_order))
```

```python
import jax
import jax.numpy as jnp
from jax import lax
from jax.sharding import Mesh, PartitionSpec as P

norm_eps = 1e-05
low_rank_scale = 2.0
CHUNKS = 2
TAIL = 128
SWAP = [(0, 1), (1, 0)]
ODD = [(s, s - 1) for s in range(15, 0, -2)]
EVEN = [(s, s - 1) for s in range(14, 0, -2)]
EVERY = [(s, s - 1) for s in range(15, 0, -1)]
f32 = jnp.float32
bf16 = jnp.bfloat16
contract_last = (((1,), (1,)), ((), ()))


def both_cores(value, axis):
    core = lax.axis_index("c")
    other = lax.ppermute(value, "c", SWAP)
    low = jnp.where(core == 0, value, other)
    high = jnp.where(core == 0, other, value)
    return jnp.concatenate([low, high], axis)


def half_sum(value, axis):
    core = lax.axis_index("c")
    width = value.shape[axis] // 2
    low = lax.slice_in_dim(value, 0, width, axis=axis)
    high = lax.slice_in_dim(value, width, 2 * width, axis=axis)
    mine = jnp.where(core == 0, low, high)
    theirs = jnp.where(core == 0, high, low)
    return mine + lax.ppermute(theirs, "c", SWAP)


def spread(value):
    sent = jnp.broadcast_to(value[None], (4,) + value.shape)
    return lax.all_to_all(sent, "y", 0, 0)


def local(
    section_inputs,
    out_grads,
    proj_weight,
    norm_gain,
    adapter_down,
    adapter_up,
    tenant_ids,
    slot_table,
):
    sec = lax.axis_index("s")
    ypos = lax.axis_index("y")
    core = lax.axis_index("c")
    micro = section_inputs.shape[1]
    width_all = section_inputs.shape[3]
    half = proj_weight.shape[1]
    width = 2 * half
    toks = section_inputs.shape[2] // 2
    rank = adapter_down.shape[3]
    rows_all = micro * toks
    group = micro // CHUNKS
    rows = group * toks
    multiplier = low_rank_scale / (toks * 2 * lax.axis_size("z"))

    w_own = lax.all_gather(proj_weight[0], "z", axis=1, tiled=True)
    w_other = lax.ppermute(w_own, "c", SWAP)

    x_full = section_inputs[0]
    x_mine = lax.dynamic_slice_in_dim(x_full, core * toks, toks, 1).reshape(rows_all, width_all)
    x_f = x_mine.astype(f32)
    inv_rms = lax.rsqrt(jnp.mean(x_f * x_f, axis=-1, keepdims=True) + norm_eps)
    x_y = lax.dynamic_slice_in_dim(x_mine, ypos * width, width, 1)
    normed_y = x_y.astype(f32) * inv_rms
    x_before = spread(lax.ppermute(x_y, "s", EVERY))
    gain_y = both_cores(norm_gain, 1)
    down_y = both_cores(adapter_down[0], 1)
    h_y = (normed_y * gain_y).astype(bf16)

    iota = jnp.arange(micro, dtype=jnp.int32)
    tenant_hot = tenant_ids[:, None] == iota[None, :]
    slot_ids = jnp.sum(jnp.where(tenant_hot, slot_table[0][None, :], 0), axis=1)
    down_sel = down_y[slot_ids]
    up_sel = adapter_up[0][slot_ids]
    low_in = jnp.einsum(
        "mtd,mdr->mtr", h_y.reshape(micro, toks, width), down_sel, preferred_element_type=f32
    )
    low_in = lax.psum(low_in, "y").astype(bf16)
    low_in_all = lax.all_gather(low_in, "z")
    h_all = lax.all_gather(h_y, "z")

    grads_top = lax.dynamic_slice_in_dim(out_grads, core * toks, toks, 1)
    grads_top = grads_top.reshape(CHUNKS, rows, width_all)
    x_before = x_before.reshape(4, CHUNKS, rows, width).transpose(1, 0, 2, 3)
    x_chunk = x_y.reshape(CHUNKS, rows, width)
    inv_chunk = inv_rms.reshape(CHUNKS, rows, 1)
    down_chunk = down_sel.reshape(CHUNKS, group, width, rank)
    up_chunk = up_sel.reshape(CHUNKS, group, rank, width_all)

    def pick(array, m):
        return lax.dynamic_index_in_dim(array, m, 0, keepdims=False)

    def gathered(box, m):
        parts = spread(box)
        tail = parts[:, :, width:].astype(f32)
        coef = jnp.sum(tail[:, :, 0:1] + tail[:, :, 1:2], axis=0)
        rows_u = parts[:, :, :width].astype(f32) - coef[None] * pick(x_before, m).astype(f32)
        return rows_u.astype(bf16).transpose(1, 0, 2).reshape(rows, width_all)

    def stage(m, box):
        grad = lax.cond(
            sec == 15, lambda box: pick(grads_top, m), lambda box: gathered(box, m), box
        )
        low = jnp.einsum(
            "mtd,mrd->mtr",
            grad.reshape(group, toks, width_all),
            pick(up_chunk, m),
            preferred_element_type=f32,
        ).astype(bf16)
        part_own = lax.dot_general(grad, w_own, contract_last, preferred_element_type=f32)
        part_other = lax.dot_general(grad, w_other, contract_last, preferred_element_type=f32)
        frozen = jnp.concatenate(
            [
                jnp.where(core == 0, part_own, part_other),
                jnp.where(core == 0, part_other, part_own),
            ],
            1,
        )
        adapt = jnp.einsum(
            "mtr,mdr->mtd", low, pick(down_chunk, m), preferred_element_type=f32
        ).reshape(rows, width)
        normed_grad = ((frozen + low_rank_scale * adapt) * gain_y).astype(bf16).astype(f32)
        inv = pick(inv_chunk, m)
        x_m = pick(x_chunk, m).astype(f32)
        grad_y = lax.dynamic_slice_in_dim(grad, ypos * width, width, 1)
        sent = (grad_y.astype(f32) + inv * normed_grad).astype(bf16)
        coef = jnp.sum(normed_grad * x_m, axis=1, keepdims=True) * (inv * inv * inv / width_all)
        high = lax.reduce_precision(coef, 8, 7)
        rest = coef - high
        lane = lax.broadcasted_iota(jnp.int32, (rows, TAIL), 1)
        tail = jnp.where(lane == 0, high, jnp.where(lane == 1, rest, 0.0)).astype(bf16)
        return jnp.concatenate([sent, tail], 1), low.reshape(rows, rank), grad_y, coef

    def put(array, value, m):
        return lax.dynamic_update_index_in_dim(array, value, m, 0)

    def step(u, state):
        box, sent_all, low_all, grad_all, coef_all = state
        t, m = u // CHUNKS, u % CHUNKS
        turn = 15 - t + m

        def work(args):
            sent_all, low_all, grad_all, coef_all = args
            sent, low, grad_y, coef = stage(m, box)
            return (
                put(sent_all, sent, m),
                put(low_all, low, m),
                put(grad_all, grad_y, m),
                put(coef_all, coef, m),
            )

        sent_all, low_all, grad_all, coef_all = lax.cond(
            sec == turn, work, lambda args: args, (sent_all, low_all, grad_all, coef_all)
        )
        part = ((sec == turn) | (sec == turn - 1)) & (turn >= 1) & (turn <= 15)
        kind = jnp.where(part, jnp.where(turn % 2 == 1, 1, 2), 0)
        outgoing = pick(sent_all, m)
        box = lax.switch(
            kind,
            [
                lambda box, out: box,
                lambda box, out: lax.ppermute(out, "s", ODD),
                lambda box, out: lax.ppermute(out, "s", EVEN),
            ],
            box,
            outgoing,
        )
        return box, sent_all, low_all, grad_all, coef_all

    start = (
        jnp.zeros((rows, width + TAIL), bf16),
        jnp.zeros((CHUNKS, rows, width + TAIL), bf16),
        jnp.zeros((CHUNKS, rows, rank), bf16),
        jnp.zeros((CHUNKS, rows, width), bf16),
        jnp.zeros((CHUNKS, rows, 1), f32),
    )
    _, sent_all, low_all, grad_all, coef_all = lax.fori_loop(0, 15 * CHUNKS + 2 * CHUNKS, step, start)

    coef_sum = lax.psum(coef_all, "y")
    new_grads = sent_all[:, :, :width].astype(f32) - coef_sum * x_chunk.astype(f32)
    new_grads = new_grads.astype(bf16).reshape(micro, toks, width)
    keep = jnp.where(core == 0, new_grads[:, :, :half], new_grads[:, :, half:])
    give = jnp.where(core == 0, new_grads[:, :, half:], new_grads[:, :, :half])
    got = lax.ppermute(give, "c", SWAP)
    kept = jnp.concatenate(
        [jnp.where(core == 0, keep, got), jnp.where(core == 0, got, keep)], 1
    )

    both = jnp.concatenate(
        [
            grad_all.reshape(rows_all, width),
            jnp.pad(low_all.reshape(rows_all, rank), ((0, 0), (0, TAIL - rank))),
        ],
        1,
    )
    both = lax.all_gather(both, "z").reshape(4, micro, toks, width + TAIL)
    grads_z = both[..., :width]
    low_z = both[..., width : width + rank]
    hidden_z = h_all.reshape(4, micro, toks, width)
    down_part = multiplier * jnp.einsum(
        "zmtd,zmtr->mdr", hidden_z, low_z, preferred_element_type=f32
    )
    up_part = multiplier * jnp.einsum(
        "zmtr,zmtd->mrd", low_in_all, grads_z, preferred_element_type=f32
    )
    down_acc = half_sum(down_part, 1)
    up_acc = half_sum(up_part, 2)
    slot_hot = slot_ids[None, :] == iota[:, None]
    down_out = jnp.sum(jnp.where(slot_hot[:, :, None, None], down_acc[None], 0.0), axis=1)
    up_out = jnp.sum(jnp.where(slot_hot[:, :, None, None], up_acc[None], 0.0), axis=1)
    return (kept[None], down_out[None], up_out[None])


def solution(mesh):
    fine = Mesh(mesh.devices.reshape(16, 4, 2, 4), ("s", "y", "c", "z"))
    mp = ("y", "c")
    placed = (
        P("s", None, "z", None),
        P(None, "z", None),
        P("s", mp, "z"),
        P("s", mp),
        P("s", None, mp, None),
        P("s", None, None, None),
        P(),
        P("s", None),
    )
    return jax.shard_map(
        local,
        mesh=fine,
        in_specs=placed,
        out_specs=(
            P("s", None, "z", mp),
            P("s", None, mp, None),
            P("s", None, None, mp),
        ),
        check_vma=False,
    )
```

```python
import functools

import jax
import jax.numpy as jnp
from jax import lax
from jax.experimental import pallas as pl
from jax.experimental.pallas import tpu as pltpu
from jax.sharding import Mesh, PartitionSpec as P

norm_eps = 1e-05
low_rank_scale = 2.0
CHUNKS = 2
TAIL = 128
SWAP = [(0, 1), (1, 0)]
ODD = [(s, s - 1) for s in range(15, 0, -2)]
EVEN = [(s, s - 1) for s in range(14, 0, -2)]
EVERY = [(s, s - 1) for s in range(15, 0, -1)]
f32 = jnp.float32
bf16 = jnp.bfloat16
contract_last = (((1,), (1,)), ((), ()))


def both_cores(value, axis):
    core = lax.axis_index("c")
    other = lax.ppermute(value, "c", SWAP)
    low = jnp.where(core == 0, value, other)
    high = jnp.where(core == 0, other, value)
    return jnp.concatenate([low, high], axis)


def half_sum(value, axis):
    core = lax.axis_index("c")
    width = value.shape[axis] // 2
    low = lax.slice_in_dim(value, 0, width, axis=axis)
    high = lax.slice_in_dim(value, width, 2 * width, axis=axis)
    mine = jnp.where(core == 0, low, high)
    theirs = jnp.where(core == 0, high, low)
    return mine + lax.ppermute(theirs, "c", SWAP)


def spread(value):
    sent = jnp.broadcast_to(value[None], (4,) + value.shape)
    return lax.all_to_all(sent, "y", 0, 0)


def stage_kernel(
    place_ref,
    parts_ref,
    before_ref,
    up_ref,
    down_ref,
    gain_ref,
    inv_ref,
    x_ref,
    own_ref,
    other_ref,
    sent_in,
    low_in,
    grad_in,
    coef_in,
    box_ref,
    sent_ref,
    low_ref,
    grad_ref,
    coef_ref,
    full,
    frozen,
    low_sc,
    *,
    group,
):
    del sent_in, low_in, grad_in, coef_in
    step = pl.program_id(0)
    ypos, core = place_ref[1], place_ref[2]
    rows, width = x_ref.shape[1], x_ref.shape[2]
    width_all = full.shape[1]
    half = width // 2
    block = own_ref.shape[0]
    toks = rows // group
    rank = up_ref.shape[1] // group

    @pl.when(step == 0)
    def _():
        tail = parts_ref[:, :, width:].astype(f32)
        coef = jnp.sum(jnp.sum(tail, axis=0), axis=1, keepdims=True)
        for part in range(4):
            fixed = parts_ref[part, :, :width].astype(f32) - coef * before_ref[0, part].astype(f32)
            full[:, part * width : (part + 1) * width] = fixed.astype(bf16)
        low = lax.dot_general(full[...], up_ref[0], contract_last, preferred_element_type=f32)
        row_group = lax.broadcasted_iota(jnp.int32, low.shape, 0) // toks
        col_group = lax.broadcasted_iota(jnp.int32, low.shape, 1) // rank
        low_sc[...] = jnp.where(row_group == col_group, low, 0.0).astype(bf16)

    grad = full[...]
    offset = step * block
    for ref, base in ((own_ref, core * half), (other_ref, (1 - core) * half)):
        frozen[:, pl.ds(pl.multiple_of(base + offset, 128), block)] = lax.dot_general(
            grad, ref[...], contract_last, preferred_element_type=f32
        )

    @pl.when(step == pl.num_programs(0) - 1)
    def _():
        low = low_sc[...]
        adapt = lax.dot_general(
            low, down_ref[0], (((1,), (0,)), ((), ())), preferred_element_type=f32
        )
        normed_grad = ((frozen[...] + low_rank_scale * adapt) * gain_ref[...]).astype(bf16)
        normed_grad = normed_grad.astype(f32)
        inv = inv_ref[0]
        grad_y = full[:, pl.ds(pl.multiple_of(ypos * width, 128), width)]
        sent = (grad_y.astype(f32) + inv * normed_grad).astype(bf16)
        coef = jnp.sum(normed_grad * x_ref[0].astype(f32), axis=1, keepdims=True)
        coef = coef * (inv * inv * inv / width_all)
        high = coef.astype(bf16).astype(f32)
        lane = lax.broadcasted_iota(jnp.int32, (rows, TAIL), 1)
        tail = jnp.where(lane == 0, high, jnp.where(lane == 1, coef - high, 0.0)).astype(bf16)
        box_ref[:, :width] = sent
        box_ref[:, width:] = tail
        sent_ref[0] = sent
        low_ref[0] = low
        grad_ref[0] = grad_y
        coef_ref[0] = jnp.where(lane == 0, coef, 0.0)


def run_stage(place, parts, before, up, down, gain, inv, x, own, other, kept):
    sent_all, low_all, grad_all, coef_all = kept
    _, rows, width = x.shape
    half, width_all = own.shape
    group = up.shape[1] // 16
    block = 128

    def whole(shape):
        return pl.BlockSpec(shape, lambda i, place: (0,) * len(shape))

    def chunk(array):
        shape = array.shape[1:]
        return pl.BlockSpec((1,) + shape, lambda i, place: (place[0],) + (0,) * len(shape))

    weight = pl.BlockSpec((block, width_all), lambda i, place: (i, 0))
    any_space = pl.BlockSpec(memory_space=pl.ANY)
    keeps = [sent_all, low_all, grad_all, coef_all]
    return pl.pallas_call(
        functools.partial(stage_kernel, group=group),
        grid_spec=pltpu.PrefetchScalarGridSpec(
            num_scalar_prefetch=1,
            grid=(half // block,),
            in_specs=[
                whole(parts.shape),
                chunk(before),
                chunk(up),
                chunk(down),
                whole(gain.shape),
                chunk(inv),
                chunk(x),
                weight,
                weight,
            ]
            + [any_space] * 4,
            out_specs=[whole((rows, width + TAIL))] + [chunk(k) for k in keeps],
            scratch_shapes=[
                pltpu.VMEM((rows, width_all), bf16),
                pltpu.VMEM((rows, width), f32),
                pltpu.VMEM((rows, up.shape[1]), bf16),
            ],
        ),
        out_shape=[jax.ShapeDtypeStruct((rows, width + TAIL), bf16)]
        + [jax.ShapeDtypeStruct(k.shape, k.dtype) for k in keeps],
        input_output_aliases={10: 1, 11: 2, 12: 3, 13: 4},
        compiler_params=pltpu.CompilerParams(
            dimension_semantics=("arbitrary",), vmem_limit_bytes=32 * 1024 * 1024
        ),
        cost_estimate=pl.CostEstimate(
            flops=2 * rows * width * width_all, bytes_accessed=2 * width * width_all, transcendentals=0
        ),
        name="stage",
    )(place, parts, before, up, down, gain, inv, x, own, other, *keeps)


def local(
    section_inputs,
    out_grads,
    proj_weight,
    norm_gain,
    adapter_down,
    adapter_up,
    tenant_ids,
    slot_table,
):
    sec = lax.axis_index("s")
    ypos = lax.axis_index("y")
    core = lax.axis_index("c")
    micro = section_inputs.shape[1]
    width_all = section_inputs.shape[3]
    half = proj_weight.shape[1]
    width = 2 * half
    toks = section_inputs.shape[2] // 2
    rank = adapter_down.shape[3]
    rows_all = micro * toks
    group = micro // CHUNKS
    rows = group * toks
    multiplier = low_rank_scale / (toks * 2 * lax.axis_size("z"))

    w_own = lax.all_gather(proj_weight[0], "z", axis=1, tiled=True)

    x_full = section_inputs[0]
    x_mine = lax.dynamic_slice_in_dim(x_full, core * toks, toks, 1).reshape(rows_all, width_all)
    x_f = x_mine.astype(f32)
    inv_rms = lax.rsqrt(jnp.mean(x_f * x_f, axis=-1, keepdims=True) + norm_eps)
    x_y = lax.dynamic_slice_in_dim(x_mine, ypos * width, width, 1)
    normed_y = x_y.astype(f32) * inv_rms
    x_before = spread(lax.ppermute(x_y, "s", EVERY))
    gain_y = both_cores(norm_gain, 1)
    down_y = both_cores(adapter_down[0], 1)
    h_y = (normed_y * gain_y).astype(bf16)

    iota = jnp.arange(micro, dtype=jnp.int32)
    tenant_hot = tenant_ids[:, None] == iota[None, :]
    slot_ids = jnp.sum(jnp.where(tenant_hot, slot_table[0][None, :], 0), axis=1)
    down_sel = down_y[slot_ids]
    up_sel = adapter_up[0][slot_ids]
    low_in = jnp.einsum(
        "mtd,mdr->mtr", h_y.reshape(micro, toks, width), down_sel, preferred_element_type=f32
    )
    low_in = lax.psum(low_in, "y").astype(bf16)
    low_in_all = lax.all_gather(low_in, "z")
    h_all = lax.all_gather(h_y, "z")

    grads_top = lax.dynamic_slice_in_dim(out_grads, core * toks, toks, 1)
    grads_top = grads_top.reshape(CHUNKS, rows, 4, width).transpose(0, 2, 1, 3)
    grads_top = jnp.pad(grads_top, ((0, 0), (0, 0), (0, 0), (0, TAIL)))
    x_before = x_before.reshape(4, CHUNKS, rows, width).transpose(1, 0, 2, 3)
    x_chunk = x_y.reshape(CHUNKS, rows, width)
    inv_chunk = inv_rms.reshape(CHUNKS, rows, 1)
    down_chunk = down_sel.transpose(0, 2, 1).reshape(CHUNKS, group * rank, width)
    up_chunk = up_sel.reshape(CHUNKS, group * rank, width_all)

    ready = (x_before, low_in_all, h_all, grads_top, down_chunk, up_chunk, inv_chunk, gain_y)
    w_own, ready = lax.optimization_barrier((w_own, ready))
    x_before, low_in_all, h_all, grads_top, down_chunk, up_chunk, inv_chunk, gain_y = ready
    w_other = lax.ppermute(w_own, "c", SWAP)

    def pick(array, m):
        return lax.dynamic_index_in_dim(array, m, 0, keepdims=False)

    def step(u, state):
        t, m = u // CHUNKS, u % CHUNKS
        turn = 15 - t + m

        def work(state):
            box, kept = state
            parts = lax.cond(sec == 15, lambda box: pick(grads_top, m), spread, box)
            place = jnp.stack([m, ypos, core]).astype(jnp.int32)
            box, *kept = run_stage(
                place,
                parts,
                x_before,
                up_chunk,
                down_chunk,
                gain_y,
                inv_chunk,
                x_chunk,
                w_own,
                w_other,
                kept,
            )
            return box, tuple(kept)

        box, kept = lax.cond(sec == turn, work, lambda state: state, state)
        part = ((sec == turn) | (sec == turn - 1)) & (turn >= 1) & (turn <= 15)
        kind = jnp.where(part, jnp.where(turn % 2 == 1, 1, 2), 0)
        box = lax.switch(
            kind,
            [
                lambda box: box,
                lambda box: lax.ppermute(box, "s", ODD),
                lambda box: lax.ppermute(box, "s", EVEN),
            ],
            box,
        )
        return box, kept

    start = (
        jnp.zeros((rows, width + TAIL), bf16),
        (
            jnp.zeros((CHUNKS, rows, width), bf16),
            jnp.zeros((CHUNKS, rows, group * rank), bf16),
            jnp.zeros((CHUNKS, rows, width), bf16),
            jnp.zeros((CHUNKS, rows, TAIL), f32),
        ),
    )
    _, kept = lax.fori_loop(0, 15 * CHUNKS + 2 * CHUNKS, step, start)
    sent_all, low_all, grad_all, coef_all = kept

    coef_sum = jnp.sum(spread(coef_all), axis=(0, -1))[..., None]
    new_grads = sent_all.astype(f32) - coef_sum * x_chunk.astype(f32)
    new_grads = new_grads.astype(bf16).reshape(micro, toks, width)
    keep = jnp.where(core == 0, new_grads[:, :, :half], new_grads[:, :, half:])
    give = jnp.where(core == 0, new_grads[:, :, half:], new_grads[:, :, :half])
    got = lax.ppermute(give, "c", SWAP)
    kept = jnp.concatenate(
        [jnp.where(core == 0, keep, got), jnp.where(core == 0, got, keep)], 1
    )

    both = jnp.concatenate(
        [
            grad_all.reshape(rows_all, width),
            jnp.pad(low_all.reshape(rows_all, group * rank), ((0, 0), (0, TAIL - group * rank))),
        ],
        1,
    )
    both = lax.all_gather(both, "z").reshape(4, micro, toks, width + TAIL)
    grads_z = both[..., :width]
    low_z = both[..., width : width + group * rank].reshape(4, micro, toks, group, rank)
    low_z = jnp.sum(low_z.astype(f32), axis=3).astype(bf16)
    hidden_z = h_all.reshape(4, micro, toks, width)
    down_part = multiplier * jnp.einsum(
        "zmtd,zmtr->mdr", hidden_z, low_z, preferred_element_type=f32
    )
    up_part = multiplier * jnp.einsum(
        "zmtr,zmtd->mrd", low_in_all, grads_z, preferred_element_type=f32
    )
    down_acc = half_sum(down_part, 1)
    up_acc = half_sum(up_part, 2)
    slot_hot = slot_ids[None, :] == iota[:, None]
    down_out = jnp.sum(jnp.where(slot_hot[:, :, None, None], down_acc[None], 0.0), axis=1)
    up_out = jnp.sum(jnp.where(slot_hot[:, :, None, None], up_acc[None], 0.0), axis=1)
    return (kept[None], down_out[None], up_out[None])


def solution(mesh):
    fine = Mesh(mesh.devices.reshape(16, 4, 2, 4), ("s", "y", "c", "z"))
    mp = ("y", "c")
    placed = (
        P("s", None, "z", None),
        P(None, "z", None),
        P("s", mp, "z"),
        P("s", mp),
        P("s", None, mp, None),
        P("s", None, None, None),
        P(),
        P("s", None),
    )
    return jax.shard_map(
        local,
        mesh=fine,
        in_specs=placed,
        out_specs=(
            P("s", None, "z", mp),
            P("s", None, mp, None),
            P("s", None, None, mp),
        ),
        check_vma=False,
    )
```

```python
import functools

import jax
import jax.numpy as jnp
from jax import lax
from jax.experimental import pallas as pl
from jax.experimental.pallas import tpu as pltpu
from jax.sharding import Mesh, PartitionSpec as P

norm_eps = 1e-05
low_rank_scale = 2.0
CHUNKS = 2
TAIL = 128
SWAP = [(0, 1), (1, 0)]
ODD = [(s, s - 1) for s in range(15, 0, -2)]
EVEN = [(s, s - 1) for s in range(14, 0, -2)]
EVERY = [(s, s - 1) for s in range(15, 0, -1)]
f32 = jnp.float32
bf16 = jnp.bfloat16
contract_last = (((1,), (1,)), ((), ()))


def both_cores(value, axis):
    core = lax.axis_index("c")
    other = lax.ppermute(value, "c", SWAP)
    low = jnp.where(core == 0, value, other)
    high = jnp.where(core == 0, other, value)
    return jnp.concatenate([low, high], axis)


def half_sum(value, axis):
    core = lax.axis_index("c")
    width = value.shape[axis] // 2
    low = lax.slice_in_dim(value, 0, width, axis=axis)
    high = lax.slice_in_dim(value, width, 2 * width, axis=axis)
    mine = jnp.where(core == 0, low, high)
    theirs = jnp.where(core == 0, high, low)
    return mine + lax.ppermute(theirs, "c", SWAP)


def spread(value):
    sent = jnp.broadcast_to(value[None], (4,) + value.shape)
    return lax.all_to_all(sent, "y", 0, 0)


def stage_kernel(
    place_ref,
    parts_ref,
    before_ref,
    up_ref,
    down_ref,
    gain_ref,
    inv_ref,
    x_ref,
    own_ref,
    other_ref,
    sent_in,
    low_in,
    grad_in,
    coef_in,
    box_ref,
    sent_ref,
    low_ref,
    grad_ref,
    coef_ref,
    full,
    weight,
    sems,
    *,
    group,
):
    del sent_in, low_in, grad_in, coef_in
    ypos, core = place_ref[1], place_ref[2]
    rows, width = x_ref.shape[1], x_ref.shape[2]
    width_all = full.shape[1]
    half = width // 2
    toks = rows // group
    rank = up_ref.shape[1] // group
    pieces = sems.shape[0]
    depth = width_all // pieces
    copies = []
    for piece in range(pieces):
        span = pl.ds(piece * depth, depth)
        pair = []
        for side, (ref, base) in enumerate(((own_ref, core * half), (other_ref, (1 - core) * half))):
            lanes = pl.ds(pl.multiple_of(base, 128), half)
            copy = pltpu.make_async_copy(
                ref.at[span], weight.at[span, lanes], sems.at[piece, side]
            )
            copy.start()
            pair.append(copy)
        copies.append(pair)

    tail = parts_ref[:, :, width:].astype(f32)
    coef = jnp.sum(jnp.sum(tail, axis=0), axis=1, keepdims=True)
    for part in range(4):
        fixed = parts_ref[part, :, :width].astype(f32) - coef * before_ref[0, part].astype(f32)
        full[:, part * width : (part + 1) * width] = fixed.astype(bf16)
    low = lax.dot_general(full[...], up_ref[0], contract_last, preferred_element_type=f32)
    row_group = lax.broadcasted_iota(jnp.int32, low.shape, 0) // toks
    col_group = lax.broadcasted_iota(jnp.int32, low.shape, 1) // rank
    low = jnp.where(row_group == col_group, low, 0.0).astype(bf16)
    total = low_rank_scale * lax.dot_general(
        low, down_ref[0], (((1,), (0,)), ((), ())), preferred_element_type=f32
    )
    for piece in range(pieces):
        for copy in copies[piece]:
            copy.wait()
        span = slice(piece * depth, (piece + 1) * depth)
        total = total + lax.dot_general(
            full[:, span], weight[span], (((1,), (0,)), ((), ())), preferred_element_type=f32
        )
    normed_grad = (total * gain_ref[...]).astype(bf16).astype(f32)
    inv = inv_ref[0]
    grad_y = full[:, pl.ds(pl.multiple_of(ypos * width, 128), width)]
    sent = (grad_y.astype(f32) + inv * normed_grad).astype(bf16)
    coef = jnp.sum(normed_grad * x_ref[0].astype(f32), axis=1, keepdims=True)
    coef = coef * (inv * inv * inv / width_all)
    lane = lax.broadcasted_iota(jnp.int32, (rows, TAIL), 1)
    high = coef.astype(bf16).astype(f32)
    tail = jnp.where(lane == 0, high, jnp.where(lane == 1, coef - high, 0.0)).astype(bf16)
    box_ref[:, :width] = sent
    box_ref[:, width:] = tail
    sent_ref[0] = sent
    low_ref[0] = low
    grad_ref[0] = grad_y
    coef_ref[0] = jnp.where(lane == 0, coef, 0.0)


def run_stage(place, parts, before, up, down, gain, inv, x, own, other, kept):
    _, rows, width = x.shape
    width_all = own.shape[0]
    group = up.shape[1] // 16
    pieces = 5

    def whole(shape):
        return pl.BlockSpec(shape, lambda i, place: (0,) * len(shape))

    def chunk(array):
        shape = array.shape[1:]
        return pl.BlockSpec((1,) + shape, lambda i, place: (place[0],) + (0,) * len(shape))

    any_space = pl.BlockSpec(memory_space=pl.ANY)
    keeps = list(kept)
    return pl.pallas_call(
        functools.partial(stage_kernel, group=group),
        grid_spec=pltpu.PrefetchScalarGridSpec(
            num_scalar_prefetch=1,
            grid=(1,),
            in_specs=[
                whole(parts.shape),
                chunk(before),
                chunk(up),
                chunk(down),
                whole(gain.shape),
                chunk(inv),
                chunk(x),
            ]
            + [any_space] * 6,
            out_specs=[whole((rows, width + TAIL))] + [chunk(k) for k in keeps],
            scratch_shapes=[
                pltpu.VMEM((rows, width_all), bf16),
                pltpu.VMEM((width_all, width), bf16),
                pltpu.SemaphoreType.DMA((pieces, 2)),
            ],
        ),
        out_shape=[jax.ShapeDtypeStruct((rows, width + TAIL), bf16)]
        + [jax.ShapeDtypeStruct(k.shape, k.dtype) for k in keeps],
        input_output_aliases={10: 1, 11: 2, 12: 3, 13: 4},
        compiler_params=pltpu.CompilerParams(
            dimension_semantics=("arbitrary",), vmem_limit_bytes=40 * 1024 * 1024
        ),
        cost_estimate=pl.CostEstimate(
            flops=2 * rows * width * width_all, bytes_accessed=2 * width * width_all, transcendentals=0
        ),
        name="stage",
    )(place, parts, before, up, down, gain, inv, x, own, other, *keeps)


def local(
    section_inputs,
    out_grads,
    proj_weight,
    norm_gain,
    adapter_down,
    adapter_up,
    tenant_ids,
    slot_table,
):
    sec = lax.axis_index("s")
    ypos = lax.axis_index("y")
    core = lax.axis_index("c")
    micro = section_inputs.shape[1]
    width_all = section_inputs.shape[3]
    half = proj_weight.shape[1]
    width = 2 * half
    toks = section_inputs.shape[2] // 2
    rank = adapter_down.shape[3]
    rows_all = micro * toks
    group = micro // CHUNKS
    rows = group * toks
    multiplier = low_rank_scale / (toks * 2 * lax.axis_size("z"))

    w_own = lax.all_gather(proj_weight[0].T, "z", axis=0, tiled=True)

    x_full = section_inputs[0]
    x_mine = lax.dynamic_slice_in_dim(x_full, core * toks, toks, 1).reshape(rows_all, width_all)
    x_f = x_mine.astype(f32)
    inv_rms = lax.rsqrt(jnp.mean(x_f * x_f, axis=-1, keepdims=True) + norm_eps)
    x_y = lax.dynamic_slice_in_dim(x_mine, ypos * width, width, 1)
    normed_y = x_y.astype(f32) * inv_rms
    x_before = spread(lax.ppermute(x_y, "s", EVERY))
    gain_y = both_cores(norm_gain, 1)
    down_y = both_cores(adapter_down[0], 1)
    h_y = (normed_y * gain_y).astype(bf16)

    iota = jnp.arange(micro, dtype=jnp.int32)
    tenant_hot = tenant_ids[:, None] == iota[None, :]
    slot_ids = jnp.sum(jnp.where(tenant_hot, slot_table[0][None, :], 0), axis=1)
    down_sel = down_y[slot_ids]
    up_sel = adapter_up[0][slot_ids]
    low_in = jnp.einsum(
        "mtd,mdr->mtr", h_y.reshape(micro, toks, width), down_sel, preferred_element_type=f32
    )
    low_in = lax.psum(low_in, "y").astype(bf16)
    low_in_all = lax.all_gather(low_in, "z")
    h_all = lax.all_gather(h_y, "z")

    grads_top = lax.dynamic_slice_in_dim(out_grads, core * toks, toks, 1)
    grads_top = grads_top.reshape(CHUNKS, rows, 4, width).transpose(0, 2, 1, 3)
    grads_top = jnp.pad(grads_top, ((0, 0), (0, 0), (0, 0), (0, TAIL)))
    x_before = x_before.reshape(4, CHUNKS, rows, width).transpose(1, 0, 2, 3)
    x_chunk = x_y.reshape(CHUNKS, rows, width)
    inv_chunk = inv_rms.reshape(CHUNKS, rows, 1)
    down_chunk = down_sel.transpose(0, 2, 1).reshape(CHUNKS, group * rank, width)
    up_chunk = up_sel.reshape(CHUNKS, group * rank, width_all)

    ready = (x_before, low_in_all, h_all, grads_top, down_chunk, up_chunk, inv_chunk, gain_y)
    w_own, ready = lax.optimization_barrier((w_own, ready))
    x_before, low_in_all, h_all, grads_top, down_chunk, up_chunk, inv_chunk, gain_y = ready
    w_other = lax.ppermute(w_own, "c", SWAP)

    def pick(array, m):
        return lax.dynamic_index_in_dim(array, m, 0, keepdims=False)

    def step(u, state):
        t, m = u // CHUNKS, u % CHUNKS
        turn = 15 - t + m

        def work(state):
            box, kept = state
            parts = lax.cond(sec == 15, lambda box: pick(grads_top, m), spread, box)
            place = jnp.stack([m, ypos, core]).astype(jnp.int32)
            box, *kept = run_stage(
                place,
                parts,
                x_before,
                up_chunk,
                down_chunk,
                gain_y,
                inv_chunk,
                x_chunk,
                w_own,
                w_other,
                kept,
            )
            return box, tuple(kept)

        box, kept = lax.cond(sec == turn, work, lambda state: state, state)
        part = ((sec == turn) | (sec == turn - 1)) & (turn >= 1) & (turn <= 15)
        kind = jnp.where(part, jnp.where(turn % 2 == 1, 1, 2), 0)
        box = lax.switch(
            kind,
            [
                lambda box: box,
                lambda box: lax.ppermute(box, "s", ODD),
                lambda box: lax.ppermute(box, "s", EVEN),
            ],
            box,
        )
        return box, kept

    start = (
        jnp.zeros((rows, width + TAIL), bf16),
        (
            jnp.zeros((CHUNKS, rows, width), bf16),
            jnp.zeros((CHUNKS, rows, group * rank), bf16),
            jnp.zeros((CHUNKS, rows, width), bf16),
            jnp.zeros((CHUNKS, rows, TAIL), f32),
        ),
    )
    _, kept = lax.fori_loop(0, 15 * CHUNKS + 2 * CHUNKS, step, start)
    sent_all, low_all, grad_all, coef_all = kept

    coef_sum = jnp.sum(spread(coef_all), axis=(0, -1))[..., None]
    new_grads = sent_all.astype(f32) - coef_sum * x_chunk.astype(f32)
    new_grads = new_grads.astype(bf16).reshape(micro, toks, width)
    keep = jnp.where(core == 0, new_grads[:, :, :half], new_grads[:, :, half:])
    give = jnp.where(core == 0, new_grads[:, :, half:], new_grads[:, :, :half])
    got = lax.ppermute(give, "c", SWAP)
    kept = jnp.concatenate(
        [jnp.where(core == 0, keep, got), jnp.where(core == 0, got, keep)], 1
    )

    both = jnp.concatenate(
        [
            grad_all.reshape(rows_all, width),
            jnp.pad(low_all.reshape(rows_all, group * rank), ((0, 0), (0, TAIL - group * rank))),
        ],
        1,
    )
    both = lax.all_gather(both, "z").reshape(4, micro, toks, width + TAIL)
    grads_z = both[..., :width]
    low_z = both[..., width : width + group * rank].reshape(4, micro, toks, group, rank)
    low_z = jnp.sum(low_z.astype(f32), axis=3).astype(bf16)
    hidden_z = h_all.reshape(4, micro, toks, width)
    down_part = multiplier * jnp.einsum(
        "zmtd,zmtr->mdr", hidden_z, low_z, preferred_element_type=f32
    )
    up_part = multiplier * jnp.einsum(
        "zmtr,zmtd->mrd", low_in_all, grads_z, preferred_element_type=f32
    )
    down_acc = half_sum(down_part, 1)
    up_acc = half_sum(up_part, 2)
    slot_hot = slot_ids[None, :] == iota[:, None]
    down_out = jnp.sum(jnp.where(slot_hot[:, :, None, None], down_acc[None], 0.0), axis=1)
    up_out = jnp.sum(jnp.where(slot_hot[:, :, None, None], up_acc[None], 0.0), axis=1)
    return (kept[None], down_out[None], up_out[None])


def solution(mesh):
    fine = Mesh(mesh.devices.reshape(16, 4, 2, 4), ("s", "y", "c", "z"))
    mp = ("y", "c")
    placed = (
        P("s", None, "z", None),
        P(None, "z", None),
        P("s", mp, "z"),
        P("s", mp),
        P("s", None, mp, None),
        P("s", None, None, None),
        P(),
        P("s", None),
    )
    return jax.shard_map(
        local,
        mesh=fine,
        in_specs=placed,
        out_specs=(
            P("s", None, "z", mp),
            P("s", None, mp, None),
            P("s", None, None, mp),
        ),
        check_vma=False,
    )
```

```python
import functools

import jax
import jax.numpy as jnp
from jax import lax
from jax.experimental import pallas as pl
from jax.experimental.pallas import tpu as pltpu
from jax.sharding import Mesh, PartitionSpec as P

norm_eps = 1e-05
low_rank_scale = 2.0
CHUNKS = 2
TAIL = 128
SWAP = [(0, 1), (1, 0)]
ODD = [(s, s - 1) for s in range(15, 0, -2)]
EVEN = [(s, s - 1) for s in range(14, 0, -2)]
EVERY = [(s, s - 1) for s in range(15, 0, -1)]
f32 = jnp.float32
bf16 = jnp.bfloat16
contract_last = (((1,), (1,)), ((), ()))
contract_inner = (((1,), (0,)), ((), ()))
LATE = 13
RIGHT = [(4 * s + z, 4 * s + (z + 1) % 4) for s in range(LATE) for z in range(4)]
LEFT = [(4 * s + z, 4 * s + (z + 3) % 4) for s in range(LATE) for z in range(4)]
LATE_SWAP = [(2 * s + c, 2 * s + 1 - c) for s in range(LATE) for c in range(2)]


def both_cores(value, axis):
    core = lax.axis_index("c")
    other = lax.ppermute(value, "c", SWAP)
    low = jnp.where(core == 0, value, other)
    high = jnp.where(core == 0, other, value)
    return jnp.concatenate([low, high], axis)


def half_sum(value, axis):
    core = lax.axis_index("c")
    width = value.shape[axis] // 2
    low = lax.slice_in_dim(value, 0, width, axis=axis)
    high = lax.slice_in_dim(value, width, 2 * width, axis=axis)
    mine = jnp.where(core == 0, low, high)
    theirs = jnp.where(core == 0, high, low)
    return mine + lax.ppermute(theirs, "c", SWAP)


def spread(value):
    sent = jnp.broadcast_to(value[None], (4,) + value.shape)
    return lax.all_to_all(sent, "y", 0, 0)


def corrected(parts_ref, before_ref, part, coef):
    width = before_ref.shape[3]
    fixed = parts_ref[part, :, :width].astype(f32)
    return (fixed - coef * before_ref[part, 0].astype(f32)).astype(bf16)


def stat_total(parts_ref, width):
    tail = parts_ref[:, :, width:].astype(f32)
    return jnp.sum(jnp.sum(tail, axis=0), axis=1, keepdims=True)


def own_group(low, group):
    rows, cols = low.shape
    row_group = lax.broadcasted_iota(jnp.int32, low.shape, 0) // (rows // group)
    col_group = lax.broadcasted_iota(jnp.int32, low.shape, 1) // (cols // group)
    return jnp.where(row_group == col_group, low, 0.0).astype(bf16)


def adapted(low, down_ref):
    return low_rank_scale * lax.dot_general(
        low, down_ref[0], contract_inner, preferred_element_type=f32
    )


def finish(total, grad_y, gain_ref, inv_ref, x_ref, box_ref, sent_ref, coef_ref, width_all):
    rows, width = total.shape
    normed_grad = (total * gain_ref[...]).astype(bf16).astype(f32)
    inv = inv_ref[0]
    sent = (grad_y.astype(f32) + inv * normed_grad).astype(bf16)
    coef = jnp.sum(normed_grad * x_ref[0].astype(f32), axis=1, keepdims=True)
    coef = coef * (inv * inv * inv / width_all)
    lane = lax.broadcasted_iota(jnp.int32, (rows, TAIL), 1)
    high = coef.astype(bf16).astype(f32)
    tail = jnp.where(lane == 0, high, jnp.where(lane == 1, coef - high, 0.0)).astype(bf16)
    box_ref[:, :width] = sent
    box_ref[:, width:] = tail
    sent_ref[0] = sent
    coef_ref[0] = jnp.where(lane == 0, coef, 0.0)


def stage_kernel(place_ref, parts_ref, before_ref, up_ref, down_ref, gain_ref, inv_ref, x_ref, *refs, group):
    weights, refs = refs[:14], refs[14 + 4 :]
    box_ref, sent_ref, low_ref, grad_ref, coef_ref, full, weight, sems = refs
    ypos, core, zpos = place_ref[1], place_ref[2], place_ref[3]
    width = x_ref.shape[2]
    width_all = full.shape[1]
    half = width // 2
    copies = []
    for piece in range(7):
        pair = []
        for side, base in enumerate((core * half, (1 - core) * half)):
            ref = weights[side * 7 + piece]
            start = 0 if piece == 0 else width + (piece - 1) * half
            lanes = pl.ds(pl.multiple_of(base, 128), half)
            target = weight.at[pl.ds(start, ref.shape[0]), lanes]
            copy = pltpu.make_async_copy(ref, target, sems.at[piece, side])
            copy.start()
            pair.append(copy)
        copies.append(pair)

    coef = stat_total(parts_ref, width)
    low = None
    for part in range(4):
        fixed = corrected(parts_ref, before_ref, part, coef)
        first = 2 * lax.rem(zpos - part + 4, 4) * half
        second = (2 * lax.rem(part - zpos + 4, 4) + 1) * half
        full[:, pl.ds(pl.multiple_of(first, 128), half)] = fixed[:, :half]
        full[:, pl.ds(pl.multiple_of(second, 128), half)] = fixed[:, half:]

        @pl.when(part == ypos)
        def _(fixed=fixed):
            grad_ref[0] = fixed

        term = lax.dot_general(
            fixed,
            up_ref[0, :, part * width : (part + 1) * width],
            contract_last,
            preferred_element_type=f32,
        )
        low = term if low is None else low + term
    low = own_group(low, group)
    low_ref[0] = low
    total = adapted(low, down_ref)
    for part in range(4):
        for copy in copies[0] if part == 0 else copies[2 * part - 1] + copies[2 * part]:
            copy.wait()
        span = slice(part * width, (part + 1) * width)
        total = total + lax.dot_general(
            full[:, span], weight[span], contract_inner, preferred_element_type=f32
        )
    finish(
        total, grad_ref[0], gain_ref, inv_ref, x_ref, box_ref, sent_ref, coef_ref, width_all
    )


def correct_kernel(place_ref, parts_ref, before_ref, up_ref, low_in, grad_in, blocks_ref, low_ref, grad_ref, *, group):
    del low_in, grad_in
    width = before_ref.shape[3]
    coef = stat_total(parts_ref, width)
    low = None
    for part in range(4):
        fixed = corrected(parts_ref, before_ref, part, coef)
        blocks_ref[part] = fixed

        @pl.when(part == place_ref[1])
        def _(fixed=fixed):
            grad_ref[0] = fixed

        term = lax.dot_general(
            fixed,
            up_ref[0, :, part * width : (part + 1) * width],
            contract_last,
            preferred_element_type=f32,
        )
        low = term if low is None else low + term
    low_ref[0] = own_group(low, group)


def product_kernel(place_ref, rows_ref, own_ref, other_ref, out_ref):
    core = place_ref[2]
    half = own_ref.shape[1]
    for ref, base in ((own_ref, core * half), (other_ref, (1 - core) * half)):
        out = lax.dot_general(rows_ref[...], ref[...], contract_inner, preferred_element_type=f32)
        out_ref[:, pl.ds(pl.multiple_of(base, 128), half)] = out.astype(bf16)


def finish_kernel(
    place_ref,
    terms_ref,
    low_ref,
    grad_ref,
    down_ref,
    gain_ref,
    inv_ref,
    x_ref,
    sent_in,
    coef_in,
    box_ref,
    sent_ref,
    coef_ref,
):
    del place_ref, sent_in, coef_in
    total = adapted(low_ref[0], down_ref)
    for part in range(4):
        total = total + terms_ref[part].astype(f32)
    width_all = 4 * total.shape[1]
    finish(
        total, grad_ref[0], gain_ref, inv_ref, x_ref, box_ref, sent_ref, coef_ref, width_all
    )


def whole(array):
    shape = array.shape
    return pl.BlockSpec(shape, lambda i, place: (0,) * len(shape))


def chunk(array):
    shape = array.shape[1:]
    return pl.BlockSpec((1,) + shape, lambda i, place: (place[0],) + (0,) * len(shape))


def second_chunk(array):
    shape = array.shape
    block = (shape[0], 1) + shape[2:]
    return pl.BlockSpec(block, lambda i, place: (0, place[0]) + (0,) * (len(shape) - 2))


any_space = pl.BlockSpec(memory_space=pl.ANY)


def call(kernel, place, inputs, keeps, outs, scratch, limit, flops, name):
    arrays = [a for a, _ in inputs]
    return pl.pallas_call(
        kernel,
        grid_spec=pltpu.PrefetchScalarGridSpec(
            num_scalar_prefetch=1,
            grid=(1,),
            in_specs=[spec for _, spec in inputs] + [any_space] * len(keeps),
            out_specs=[whole(o) for o in outs] + [chunk(k) for k in keeps],
            scratch_shapes=scratch,
        ),
        out_shape=list(outs) + [jax.ShapeDtypeStruct(k.shape, k.dtype) for k in keeps],
        input_output_aliases={1 + len(arrays) + i: len(outs) + i for i in range(len(keeps))},
        compiler_params=pltpu.CompilerParams(
            dimension_semantics=("arbitrary",), vmem_limit_bytes=limit * 1024 * 1024
        ),
        cost_estimate=pl.CostEstimate(
            flops=flops, bytes_accessed=sum(a.size * a.dtype.itemsize for a in arrays), transcendentals=0
        ),
        name=name,
    )(place, *arrays, *keeps)


def local(
    section_inputs,
    out_grads,
    proj_weight,
    norm_gain,
    adapter_down,
    adapter_up,
    tenant_ids,
    slot_table,
):
    sec = lax.axis_index("s")
    ypos = lax.axis_index("y")
    core = lax.axis_index("c")
    micro = section_inputs.shape[1]
    width_all = section_inputs.shape[3]
    half = proj_weight.shape[1]
    width = 2 * half
    toks = section_inputs.shape[2] // 2
    rank = adapter_down.shape[3]
    rows_all = micro * toks
    group = micro // CHUNKS
    rows = group * toks
    multiplier = low_rank_scale / (toks * 2 * lax.axis_size("z"))

    zpos = lax.axis_index("z")
    shard = proj_weight[0].T
    first, second = shard[:half], shard[half:]
    right_1 = lax.ppermute(first, ("s", "z"), RIGHT)
    left_1 = lax.ppermute(second, ("s", "z"), LEFT)
    shard_x = lax.ppermute(shard, "c", SWAP)

    x_full = section_inputs[0]
    x_mine = lax.dynamic_slice_in_dim(x_full, core * toks, toks, 1).reshape(rows_all, width_all)
    x_f = x_mine.astype(f32)
    inv_rms = lax.rsqrt(jnp.mean(x_f * x_f, axis=-1, keepdims=True) + norm_eps)
    x_y = lax.dynamic_slice_in_dim(x_mine, ypos * width, width, 1)
    normed_y = x_y.astype(f32) * inv_rms
    x_before = lax.cond(
        sec == 15,
        lambda x: jnp.zeros((4,) + x.shape, x.dtype),
        spread,
        lax.ppermute(x_y, "s", EVERY),
    )
    gain_y = both_cores(norm_gain, 1)
    down_y = both_cores(adapter_down[0], 1)
    h_y = (normed_y * gain_y).astype(bf16)

    iota = jnp.arange(micro, dtype=jnp.int32)
    tenant_hot = tenant_ids[:, None] == iota[None, :]
    slot_ids = jnp.sum(jnp.where(tenant_hot, slot_table[0][None, :], 0), axis=1)
    down_sel = down_y[slot_ids]
    up_sel = adapter_up[0][slot_ids]
    low_part = jnp.einsum(
        "mtd,mdr->mtr", h_y.reshape(micro, toks, width), down_sel, preferred_element_type=f32
    )

    def low_in_of(part):
        return lax.all_gather(lax.psum(part, "y").astype(bf16), "z")

    x_before = x_before.reshape(4, CHUNKS, rows, width)
    x_chunk = x_y.reshape(CHUNKS, rows, width)
    inv_chunk = inv_rms.reshape(CHUNKS, rows, 1)
    down_chunk = down_sel.transpose(0, 2, 1).reshape(CHUNKS, group * rank, width)
    up_chunk = up_sel.reshape(CHUNKS, group * rank, width_all)
    grads_top = lax.dynamic_slice_in_dim(out_grads, core * toks, toks, 1)
    grads_top = grads_top.reshape(CHUNKS, rows, width_all)

    ready = (shard_x, x_before, x_chunk, inv_chunk, down_chunk, up_chunk, gain_y, grads_top)
    right_1, left_1, ready = lax.optimization_barrier((right_1, left_1, ready))
    shard_x, x_before, x_chunk, inv_chunk, down_chunk, up_chunk, gain_y, grads_top = ready

    def around(args):
        right_1, left_1, h_y, low_part = args

        def swapped(value):
            return lax.ppermute(value, ("s", "c"), LATE_SWAP)

        right_2 = lax.ppermute(right_1, ("s", "z"), RIGHT)
        left_2 = lax.ppermute(left_1, ("s", "z"), LEFT)
        other_1 = (swapped(right_1), swapped(left_1))
        h_all = lax.all_gather(h_y, "z")
        right_2, left_2, other_1, h_all = lax.optimization_barrier(
            (right_2, left_2, other_1, h_all)
        )
        right_3 = lax.ppermute(right_2, ("s", "z"), RIGHT)
        left_3 = lax.ppermute(left_2, ("s", "z"), LEFT)
        other_2 = (swapped(right_2), swapped(left_2))
        low_in_all = low_in_of(low_part)
        right_3, left_3, other_2, low_in_all = lax.optimization_barrier(
            (right_3, left_3, other_2, low_in_all)
        )
        other_3 = (swapped(right_3), swapped(left_3))
        return (right_2, left_2, right_3, left_3) + other_1 + other_2 + other_3, (h_all, low_in_all)

    def alone(args):
        shapes = jax.eval_shape(around, args)
        return jax.tree.map(lambda a: jnp.zeros(a.shape, a.dtype), shapes)

    moved, extras = lax.cond(sec < LATE, around, alone, (right_1, left_1, h_y, low_part))
    mine = [shard, right_1, left_1, *moved[:4]]
    theirs = [shard_x, *moved[4:]]

    def pick(array, m):
        return lax.dynamic_index_in_dim(array, m, 0, keepdims=False)

    def step(u, state):
        t, m = u // CHUNKS, u % CHUNKS
        turn = 15 - t + m

        place = jnp.stack([m, ypos, core, zpos]).astype(jnp.int32)
        box_shape = jax.ShapeDtypeStruct((rows, width + TAIL), bf16)

        def top(box):
            grad = pick(grads_top, m).reshape(rows, 4, width).transpose(1, 0, 2)
            return jnp.pad(grad, ((0, 0), (0, 0), (0, TAIL)))

        def with_all(args):
            parts, kept = args
            inputs = [
                (parts, whole(parts)),
                (x_before, second_chunk(x_before)),
                (up_chunk, chunk(up_chunk)),
                (down_chunk, chunk(down_chunk)),
                (gain_y, whole(gain_y)),
                (inv_chunk, chunk(inv_chunk)),
                (x_chunk, chunk(x_chunk)),
            ] + [(w, any_space) for w in mine + theirs]
            scratch = [
                pltpu.VMEM((rows, width_all), bf16),
                pltpu.VMEM((width_all, width), bf16),
                pltpu.SemaphoreType.DMA((7, 2)),
            ]
            box, *kept = call(
                functools.partial(stage_kernel, group=group),
                place,
                inputs,
                list(kept),
                [box_shape],
                scratch,
                40,
                2 * rows * width * width_all,
                "stage",
            )
            return box, tuple(kept)

        def with_shard(args):
            parts, (sent_all, low_all, grad_all, coef_all) = args
            inputs = [
                (parts, whole(parts)),
                (x_before, second_chunk(x_before)),
                (up_chunk, chunk(up_chunk)),
            ]
            blocks, low_all, grad_all = call(
                functools.partial(correct_kernel, group=group),
                place,
                inputs,
                [low_all, grad_all],
                [jax.ShapeDtypeStruct((4, rows, width), bf16)],
                [],
                16,
                2 * rows * width_all * rank * group,
                "correct",
            )
            blocks = lax.all_to_all(blocks, "z", 0, 0).reshape(4 * rows, width)
            inputs = [(blocks, whole(blocks)), (shard, whole(shard)), (shard_x, whole(shard_x))]
            (terms,) = call(
                product_kernel,
                place,
                inputs,
                [],
                [jax.ShapeDtypeStruct((4 * rows, width), bf16)],
                [],
                24,
                8 * rows * width * width,
                "product",
            )
            terms = lax.all_to_all(terms.reshape(4, rows, width), "z", 0, 0)
            inputs = [
                (terms, whole(terms)),
                (low_all, chunk(low_all)),
                (grad_all, chunk(grad_all)),
                (down_chunk, chunk(down_chunk)),
                (gain_y, whole(gain_y)),
                (inv_chunk, chunk(inv_chunk)),
                (x_chunk, chunk(x_chunk)),
            ]
            box, sent_all, coef_all = call(
                finish_kernel,
                place,
                inputs,
                [sent_all, coef_all],
                [box_shape],
                [],
                16,
                2 * rows * width * rank * group,
                "finish",
            )
            return box, (sent_all, low_all, grad_all, coef_all)

        def work(state):
            box, kept = state
            parts = lax.cond(sec == 15, top, spread, box)
            return lax.cond(sec < LATE, with_all, with_shard, (parts, kept))

        box, kept = lax.cond(sec == turn, work, lambda state: state, state)
        part = ((sec == turn) | (sec == turn - 1)) & (turn >= 1) & (turn <= 15)
        kind = jnp.where(part, jnp.where(turn % 2 == 1, 1, 2), 0)
        box = lax.switch(
            kind,
            [
                lambda box: box,
                lambda box: lax.ppermute(box, "s", ODD),
                lambda box: lax.ppermute(box, "s", EVEN),
            ],
            box,
        )
        return box, kept

    start = (
        jnp.zeros((rows, width + TAIL), bf16),
        (
            jnp.zeros((CHUNKS, rows, width), bf16),
            jnp.zeros((CHUNKS, rows, group * rank), bf16),
            jnp.zeros((CHUNKS, rows, width), bf16),
            jnp.zeros((CHUNKS, rows, TAIL), f32),
        ),
    )
    _, kept = lax.fori_loop(0, 15 * CHUNKS + 2 * CHUNKS, step, start)
    sent_all, low_all, grad_all, coef_all = kept

    h_all, low_in_all = lax.cond(
        sec < LATE,
        lambda args: args[0],
        lambda args: (lax.all_gather(args[1], "z"), low_in_of(args[2])),
        (extras, h_y, low_part),
    )
    coef_sum = jnp.sum(spread(coef_all), axis=(0, -1))[..., None]
    new_grads = sent_all.astype(f32) - coef_sum * x_chunk.astype(f32)
    new_grads = new_grads.astype(bf16).reshape(micro, toks, width)
    keep = jnp.where(core == 0, new_grads[:, :, :half], new_grads[:, :, half:])
    give = jnp.where(core == 0, new_grads[:, :, half:], new_grads[:, :, :half])
    got = lax.ppermute(give, "c", SWAP)
    kept = jnp.concatenate(
        [jnp.where(core == 0, keep, got), jnp.where(core == 0, got, keep)], 1
    )

    both = jnp.concatenate(
        [
            grad_all.reshape(rows_all, width),
            jnp.pad(low_all.reshape(rows_all, group * rank), ((0, 0), (0, TAIL - group * rank))),
        ],
        1,
    )
    both = lax.all_gather(both, "z").reshape(4, micro, toks, width + TAIL)
    grads_z = both[..., :width]
    low_z = both[..., width : width + group * rank].reshape(4, micro, toks, group, rank)
    low_z = jnp.sum(low_z.astype(f32), axis=3).astype(bf16)
    hidden_z = h_all.reshape(4, micro, toks, width)
    down_part = multiplier * jnp.einsum(
        "zmtd,zmtr->mdr", hidden_z, low_z, preferred_element_type=f32
    )
    up_part = multiplier * jnp.einsum(
        "zmtr,zmtd->mrd", low_in_all, grads_z, preferred_element_type=f32
    )
    down_acc = half_sum(down_part, 1)
    up_acc = half_sum(up_part, 2)
    slot_hot = slot_ids[None, :] == iota[:, None]
    down_out = jnp.sum(jnp.where(slot_hot[:, :, None, None], down_acc[None], 0.0), axis=1)
    up_out = jnp.sum(jnp.where(slot_hot[:, :, None, None], up_acc[None], 0.0), axis=1)
    return (kept[None], down_out[None], up_out[None])


def solution(mesh):
    fine = Mesh(mesh.devices.reshape(16, 4, 2, 4), ("s", "y", "c", "z"))
    mp = ("y", "c")
    placed = (
        P("s", None, "z", None),
        P(None, "z", None),
        P("s", mp, "z"),
        P("s", mp),
        P("s", None, mp, None),
        P("s", None, None, None),
        P(),
        P("s", None),
    )
    return jax.shard_map(
        local,
        mesh=fine,
        in_specs=placed,
        out_specs=(
            P("s", None, "z", mp),
            P("s", None, mp, None),
            P("s", None, None, mp),
        ),
        check_vma=False,
    )
```

```python
import functools

import jax
import jax.numpy as jnp
from jax import lax
from jax.experimental import pallas as pl
from jax.experimental.pallas import tpu as pltpu
from jax.sharding import Mesh, PartitionSpec as P

norm_eps = 1e-05
low_rank_scale = 2.0
CHUNKS = 2
TAIL = 128
SWAP = [(0, 1), (1, 0)]
ODD = [(s, s - 1) for s in range(15, 0, -2)]
EVEN = [(s, s - 1) for s in range(14, 0, -2)]
EVERY = [(s, s - 1) for s in range(15, 0, -1)]
f32 = jnp.float32
bf16 = jnp.bfloat16
contract_last = (((1,), (1,)), ((), ()))
contract_inner = (((1,), (0,)), ((), ()))
TOP_SWAP = [(30, 31), (31, 30)]
AHEAD = 3


def both_cores(value, axis):
    core = lax.axis_index("c")
    other = lax.ppermute(value, "c", SWAP)
    low = jnp.where(core == 0, value, other)
    high = jnp.where(core == 0, other, value)
    return jnp.concatenate([low, high], axis)


def half_sum(value, axis):
    core = lax.axis_index("c")
    width = value.shape[axis] // 2
    low = lax.slice_in_dim(value, 0, width, axis=axis)
    high = lax.slice_in_dim(value, width, 2 * width, axis=axis)
    mine = jnp.where(core == 0, low, high)
    theirs = jnp.where(core == 0, high, low)
    return mine + lax.ppermute(theirs, "c", SWAP)


def spread(value):
    sent = jnp.broadcast_to(value[None], (4,) + value.shape)
    return lax.all_to_all(sent, "y", 0, 0)


def own_group(low, group):
    rows, cols = low.shape
    row_group = lax.broadcasted_iota(jnp.int32, low.shape, 0) // (rows // group)
    col_group = lax.broadcasted_iota(jnp.int32, low.shape, 1) // (cols // group)
    return jnp.where(row_group == col_group, low, 0.0).astype(bf16)


def message(total, grad_y, gain, inv, x, width_all):
    rows, width = total.shape
    normed_grad = (total * gain).astype(bf16).astype(f32)
    sent = (grad_y.astype(f32) + inv * normed_grad).astype(bf16)
    coef = jnp.sum(normed_grad * x.astype(f32), axis=1, keepdims=True)
    coef = coef * (inv * inv * inv / width_all)
    lane = lax.broadcasted_iota(jnp.int32, (rows, TAIL), 1)
    high = lax.reduce_precision(coef, 8, 7)
    tail = jnp.where(lane == 0, high, jnp.where(lane == 1, coef - high, 0.0)).astype(bf16)
    return sent, tail


def stage_kernel(
    place_ref,
    parts_ref,
    gain_ref,
    before_any,
    up_any,
    down_any,
    inv_any,
    x_any,
    own_any,
    other_any,
    boxes_in,
    low_in,
    grad_in,
    box_ref,
    boxes_any,
    low_any,
    grad_any,
    before_ref,
    up_ref,
    down_ref,
    inv_ref,
    x_ref,
    full,
    weight,
    low_ref,
    grad_ref,
    in_sems,
    w_sems,
    out_sems,
    *,
    group,
):
    del boxes_in, low_in, grad_in
    m, ypos, core = place_ref[0], place_ref[1], place_ref[2]
    width = x_ref.shape[1]
    width_all = full.shape[1]
    half = width // 2
    pieces = w_sems.shape[0]
    depth = width_all // pieces

    def started(source, target, sem):
        copy = pltpu.make_async_copy(source, target, sem)
        copy.start()
        return copy

    before_copy = started(before_any.at[:, m], before_ref, in_sems.at[0])
    up_copy = started(up_any.at[m], up_ref, in_sems.at[1])
    copies = []
    for piece in range(pieces):
        span = pl.ds(piece * depth, depth)
        for side, (ref, base) in enumerate(((own_any, core * half), (other_any, (1 - core) * half))):
            lanes = pl.ds(pl.multiple_of(base, 128), half)
            copies.append(started(ref.at[span], weight.at[span, lanes], w_sems.at[piece, side]))
        if piece == 0:
            down_copy = started(down_any.at[m], down_ref, in_sems.at[2])
            inv_copy = started(inv_any.at[m], inv_ref, in_sems.at[3])
            x_copy = started(x_any.at[m], x_ref, in_sems.at[4])

    tail = parts_ref[:, :, width:].astype(f32)
    coef = jnp.sum(jnp.sum(tail, axis=0), axis=1, keepdims=True)
    before_copy.wait()
    for part in range(4):
        fixed = parts_ref[part, :, :width].astype(f32) - coef * before_ref[part].astype(f32)
        full[:, part * width : (part + 1) * width] = fixed.astype(bf16)
    grad_ref[...] = full[:, pl.ds(pl.multiple_of(ypos * width, 128), width)]
    grad_copy = started(grad_ref, grad_any.at[m], out_sems.at[0])
    up_copy.wait()
    low = lax.dot_general(full[...], up_ref[...], contract_last, preferred_element_type=f32)
    low = own_group(low, group)
    low_ref[...] = low
    low_copy = started(low_ref, low_any.at[m], out_sems.at[1])
    down_copy.wait()
    total = low_rank_scale * lax.dot_general(
        low, down_ref[...], contract_inner, preferred_element_type=f32
    )
    for piece in range(pieces):
        copies[2 * piece].wait()
        copies[2 * piece + 1].wait()
        span = slice(piece * depth, (piece + 1) * depth)
        total = total + lax.dot_general(
            full[:, span], weight[span], contract_inner, preferred_element_type=f32
        )
    inv_copy.wait()
    x_copy.wait()
    sent, tail = message(
        total, grad_ref[...], gain_ref[...], inv_ref[:, 0:1], x_ref[...], width_all
    )
    box_ref[:, :width] = sent
    box_ref[:, width:] = tail
    box_copy = started(box_ref, boxes_any.at[m], out_sems.at[2])
    grad_copy.wait()
    low_copy.wait()
    box_copy.wait()


def run_stage(place, parts, before, up, down, gain, inv, x, own, other, kept):
    _, rows, width = x.shape
    width_all = own.shape[0]
    cols = up.shape[1]
    pieces = 5
    vmem = pl.BlockSpec(memory_space=pltpu.VMEM)
    any_space = pl.BlockSpec(memory_space=pl.ANY)
    return pl.pallas_call(
        functools.partial(stage_kernel, group=cols // 16),
        in_specs=[pl.BlockSpec(memory_space=pltpu.SMEM), vmem, vmem] + [any_space] * 10,
        out_specs=[vmem] + [any_space] * 3,
        scratch_shapes=[
            pltpu.VMEM((4, rows, width), bf16),
            pltpu.VMEM((cols, width_all), bf16),
            pltpu.VMEM((cols, width), bf16),
            pltpu.VMEM((rows, TAIL), f32),
            pltpu.VMEM((rows, width), bf16),
            pltpu.VMEM((rows, width_all), bf16),
            pltpu.VMEM((width_all, width), bf16),
            pltpu.VMEM((rows, cols), bf16),
            pltpu.VMEM((rows, width), bf16),
            pltpu.SemaphoreType.DMA((5,)),
            pltpu.SemaphoreType.DMA((pieces, 2)),
            pltpu.SemaphoreType.DMA((3,)),
        ],
        out_shape=[jax.ShapeDtypeStruct((rows, width + TAIL), bf16)]
        + [jax.ShapeDtypeStruct(k.shape, k.dtype) for k in kept],
        input_output_aliases={10: 1, 11: 2, 12: 3},
        compiler_params=pltpu.CompilerParams(vmem_limit_bytes=32 * 1024 * 1024),
        cost_estimate=pl.CostEstimate(
            flops=2 * rows * width * width_all, bytes_accessed=2 * width * width_all, transcendentals=0
        ),
        name="stage",
    )(place, parts, gain, before, up, down, inv, x, own, other, *kept)


def local(
    section_inputs,
    out_grads,
    proj_weight,
    norm_gain,
    adapter_down,
    adapter_up,
    tenant_ids,
    slot_table,
):
    sec = lax.axis_index("s")
    ypos = lax.axis_index("y")
    core = lax.axis_index("c")
    micro = section_inputs.shape[1]
    width_all = section_inputs.shape[3]
    half = proj_weight.shape[1]
    width = 2 * half
    toks = section_inputs.shape[2] // 2
    rank = adapter_down.shape[3]
    rows_all = micro * toks
    group = micro // CHUNKS
    rows = group * toks
    multiplier = low_rank_scale / (toks * 2 * lax.axis_size("z"))

    shard = proj_weight[0].T
    w_own = lax.all_gather(shard, "z", axis=0, tiled=True)

    x_full = section_inputs[0]
    x_mine = lax.dynamic_slice_in_dim(x_full, core * toks, toks, 1).reshape(rows_all, width_all)
    x_f = x_mine.astype(f32)
    inv_rms = lax.rsqrt(jnp.mean(x_f * x_f, axis=-1, keepdims=True) + norm_eps)
    x_y = lax.dynamic_slice_in_dim(x_mine, ypos * width, width, 1)
    normed_y = x_y.astype(f32) * inv_rms
    x_before = lax.cond(
        sec == 15,
        lambda x: jnp.zeros((4,) + x.shape, x.dtype),
        spread,
        lax.ppermute(x_y, "s", EVERY),
    )
    gain_y = both_cores(norm_gain, 1)
    down_y = both_cores(adapter_down[0], 1)
    h_y = (normed_y * gain_y).astype(bf16)

    iota = jnp.arange(micro, dtype=jnp.int32)
    tenant_hot = tenant_ids[:, None] == iota[None, :]
    slot_ids = jnp.sum(jnp.where(tenant_hot, slot_table[0][None, :], 0), axis=1)
    down_sel = down_y[slot_ids]
    up_sel = adapter_up[0][slot_ids]
    low_part = jnp.einsum(
        "mtd,mdr->mtr", h_y.reshape(micro, toks, width), down_sel, preferred_element_type=f32
    )

    def extra(args):
        h_y, low_part = args
        low_in = lax.psum(low_part, "y").astype(bf16)
        return lax.all_gather(h_y, "z"), lax.all_gather(low_in, "z")

    x_before = x_before.reshape(4, CHUNKS, rows, width)
    x_chunk = x_y.reshape(CHUNKS, rows, width)
    inv_chunk = jnp.broadcast_to(inv_rms.reshape(CHUNKS, rows, 1), (CHUNKS, rows, TAIL))
    down_chunk = down_sel.transpose(0, 2, 1).reshape(CHUNKS, group * rank, width)
    up_chunk = up_sel.reshape(CHUNKS, group * rank, width_all)

    def top(args):
        out_grads, shard = args
        shard_x = lax.ppermute(shard, ("s", "c"), TOP_SWAP)
        grad = lax.dynamic_slice_in_dim(out_grads, core * toks, toks, 1)
        low = jnp.einsum("mtd,mrd->mtr", grad, up_sel, preferred_element_type=f32).astype(bf16)
        adapt = jnp.einsum("mtr,mdr->mtd", low, down_sel, preferred_element_type=f32)
        grad = grad.reshape(rows_all, width_all)
        blocks = jnp.stack([grad[:, i * width : (i + 1) * width] for i in range(4)])
        blocks = lax.all_to_all(blocks, "z", 0, 0).reshape(4 * rows_all, width)
        mine, theirs = (
            lax.dot_general(blocks, w, contract_inner, preferred_element_type=f32).astype(bf16)
            for w in (shard, shard_x)
        )
        terms = jnp.concatenate(
            [jnp.where(core == 0, mine, theirs), jnp.where(core == 0, theirs, mine)], 1
        )
        terms = lax.all_to_all(terms.reshape(4, rows_all, width), "z", 0, 0)
        total = jnp.sum(terms.astype(f32), axis=0)
        total = total + low_rank_scale * adapt.reshape(rows_all, width)
        grad_y = lax.dynamic_slice_in_dim(grad, ypos * width, width, 1)
        sent, tail = message(total, grad_y, gain_y, inv_rms, x_y, width_all)
        boxes = jnp.concatenate([sent, tail], 1).reshape(CHUNKS, rows, width + TAIL)
        member = jnp.arange(rows_all)[:, None] // toks % group == jnp.arange(group)[None, :]
        low = jnp.where(member[:, :, None], low.reshape(rows_all, 1, rank), 0)
        low = low.astype(bf16).reshape(CHUNKS, rows, group * rank)
        return boxes, low, grad_y.reshape(CHUNKS, rows, width)

    def empty(args):
        return (
            jnp.zeros((CHUNKS, rows, width + TAIL), bf16),
            jnp.zeros((CHUNKS, rows, group * rank), bf16),
            jnp.zeros((CHUNKS, rows, width), bf16),
        )

    kept = lax.cond(sec == 15, top, empty, (out_grads, shard))

    ready = (x_before, x_chunk, inv_chunk, down_chunk, up_chunk, gain_y, kept)
    w_own, ready = lax.optimization_barrier((w_own, ready))
    x_before, x_chunk, inv_chunk, down_chunk, up_chunk, gain_y, kept = ready
    w_other = lax.ppermute(w_own, "c", SWAP)

    def pick(array, m):
        return lax.dynamic_index_in_dim(array, m, 0, keepdims=False)

    def step(u, state):
        box, kept, extras = state
        t, m = u // CHUNKS, u % CHUNKS
        turn = 15 - t + m

        def stored(args):
            _, kept = args
            return pick(kept[0], m), kept

        def computed(args):
            box, kept = args
            place = jnp.stack([m, ypos, core]).astype(jnp.int32)
            box, *kept = run_stage(
                place,
                spread(box),
                x_before,
                up_chunk,
                down_chunk,
                gain_y,
                inv_chunk,
                x_chunk,
                w_own,
                w_other,
                kept,
            )
            return box, tuple(kept)

        kind = jnp.where(sec == turn, jnp.where(sec == 15, 1, 2), 0)
        box, kept = lax.switch(kind, [lambda args: args, stored, computed], (box, kept))
        part = ((sec == turn) | (sec == turn - 1)) & (turn >= 1) & (turn <= 15)
        kind = jnp.where(part, jnp.where(turn % 2 == 1, 1, 2), 0)
        box = lax.switch(
            kind,
            [
                lambda box: box,
                lambda box: lax.ppermute(box, "s", ODD),
                lambda box: lax.ppermute(box, "s", EVEN),
            ],
            box,
        )
        extras = lax.cond(
            (sec == turn - AHEAD) & (m == 0),
            lambda args: extra((h_y, low_part)),
            lambda args: args,
            extras,
        )
        return box, kept, extras

    start = (
        jnp.zeros((rows, width + TAIL), bf16),
        kept,
        (
            jnp.zeros((4, rows_all, width), bf16),
            jnp.zeros((4, micro, toks, rank), bf16),
        ),
    )
    _, kept, extras = lax.fori_loop(0, (15 + CHUNKS) * CHUNKS, step, start)
    boxes, low_all, grad_all = kept
    h_all, low_in_all = lax.cond(
        sec > 15 - AHEAD, lambda args: extra((h_y, low_part)), lambda args: args, extras
    )

    coef_sum = jnp.sum(spread(boxes[:, :, width:]).astype(f32), axis=(0, -1))[..., None]
    new_grads = boxes[:, :, :width].astype(f32) - coef_sum * x_chunk.astype(f32)
    new_grads = new_grads.astype(bf16).reshape(micro, toks, width)
    keep = jnp.where(core == 0, new_grads[:, :, :half], new_grads[:, :, half:])
    give = jnp.where(core == 0, new_grads[:, :, half:], new_grads[:, :, :half])
    got = lax.ppermute(give, "c", SWAP)
    kept = jnp.concatenate(
        [jnp.where(core == 0, keep, got), jnp.where(core == 0, got, keep)], 1
    )

    both = jnp.concatenate(
        [
            grad_all.reshape(rows_all, width),
            jnp.pad(low_all.reshape(rows_all, group * rank), ((0, 0), (0, TAIL - group * rank))),
        ],
        1,
    )
    both = lax.all_gather(both, "z").reshape(4, micro, toks, width + TAIL)
    grads_z = both[..., :width]
    low_z = both[..., width : width + group * rank].reshape(4, micro, toks, group, rank)
    low_z = jnp.sum(low_z.astype(f32), axis=3).astype(bf16)
    hidden_z = h_all.reshape(4, micro, toks, width)
    down_part = multiplier * jnp.einsum(
        "zmtd,zmtr->mdr", hidden_z, low_z, preferred_element_type=f32
    )
    up_part = multiplier * jnp.einsum(
        "zmtr,zmtd->mrd", low_in_all, grads_z, preferred_element_type=f32
    )
    down_acc = half_sum(down_part, 1)
    up_acc = half_sum(up_part, 2)
    slot_hot = slot_ids[None, :] == iota[:, None]
    down_out = jnp.sum(jnp.where(slot_hot[:, :, None, None], down_acc[None], 0.0), axis=1)
    up_out = jnp.sum(jnp.where(slot_hot[:, :, None, None], up_acc[None], 0.0), axis=1)
    return (kept[None], down_out[None], up_out[None])


def solution(mesh):
    fine = Mesh(mesh.devices.reshape(16, 4, 2, 4), ("s", "y", "c", "z"))
    mp = ("y", "c")
    placed = (
        P("s", None, "z", None),
        P(None, "z", None),
        P("s", mp, "z"),
        P("s", mp),
        P("s", None, mp, None),
        P("s", None, None, None),
        P(),
        P("s", None),
    )
    return jax.shard_map(
        local,
        mesh=fine,
        in_specs=placed,
        out_specs=(
            P("s", None, "z", mp),
            P("s", None, mp, None),
            P("s", None, None, mp),
        ),
        check_vma=False,
    )
```

```python
import functools

import jax
import jax.numpy as jnp
from jax import lax
from jax.experimental import pallas as pl
from jax.experimental.pallas import tpu as pltpu
from jax.sharding import Mesh, PartitionSpec as P

norm_eps = 1e-05
low_rank_scale = 2.0
CHUNKS = 2
TAIL = 128
SWAP = [(0, 1), (1, 0)]
ODD = [(s, s - 1) for s in range(15, 0, -2)]
EVEN = [(s, s - 1) for s in range(14, 0, -2)]
EVERY = [(s, s - 1) for s in range(15, 0, -1)]
f32 = jnp.float32
bf16 = jnp.bfloat16
contract_last = (((1,), (1,)), ((), ()))
contract_inner = (((1,), (0,)), ((), ()))
TOP_SWAP = [(30, 31), (31, 30)]
AHEAD = 3


def both_cores(value, axis):
    core = lax.axis_index("c")
    other = lax.ppermute(value, "c", SWAP)
    low = jnp.where(core == 0, value, other)
    high = jnp.where(core == 0, other, value)
    return jnp.concatenate([low, high], axis)


def half_sum(value, axis):
    core = lax.axis_index("c")
    width = value.shape[axis] // 2
    low = lax.slice_in_dim(value, 0, width, axis=axis)
    high = lax.slice_in_dim(value, width, 2 * width, axis=axis)
    mine = jnp.where(core == 0, low, high)
    theirs = jnp.where(core == 0, high, low)
    return mine + lax.ppermute(theirs, "c", SWAP)


def spread(value):
    sent = jnp.broadcast_to(value[None], (4,) + value.shape)
    return lax.all_to_all(sent, "y", 0, 0)


def own_group(low, group):
    rows, cols = low.shape
    row_group = lax.broadcasted_iota(jnp.int32, low.shape, 0) // (rows // group)
    col_group = lax.broadcasted_iota(jnp.int32, low.shape, 1) // (cols // group)
    return jnp.where(row_group == col_group, low, 0.0).astype(bf16)


def message(total, grad_y, gain, inv, x, width_all):
    rows, width = total.shape
    normed_grad = (total * gain).astype(bf16).astype(f32)
    sent = (grad_y.astype(f32) + inv * normed_grad).astype(bf16)
    coef = jnp.sum(normed_grad * x.astype(f32), axis=1, keepdims=True)
    coef = coef * (inv * inv * inv / width_all)
    lane = lax.broadcasted_iota(jnp.int32, (rows, TAIL), 1)
    high = lax.reduce_precision(coef, 8, 7)
    tail = jnp.where(lane == 0, high, jnp.where(lane == 1, coef - high, 0.0)).astype(bf16)
    return sent, tail


def stage_kernel(
    place_ref,
    parts_ref,
    gain_ref,
    before_any,
    up_any,
    down_any,
    inv_any,
    x_any,
    own_any,
    other_any,
    boxes_in,
    low_in,
    grad_in,
    box_ref,
    boxes_any,
    low_any,
    grad_any,
    before_ref,
    up_ref,
    down_ref,
    inv_ref,
    x_ref,
    full,
    weight,
    low_ref,
    grad_ref,
    in_sems,
    w_sems,
    out_sems,
    *,
    group,
):
    del boxes_in, low_in, grad_in
    m, ypos, core = place_ref[0], place_ref[1], place_ref[2]
    width = x_ref.shape[1]
    width_all = full.shape[1]
    half = width // 2
    pieces = w_sems.shape[0]
    depth = width_all // pieces

    def started(source, target, sem):
        copy = pltpu.make_async_copy(source, target, sem)
        copy.start()
        return copy

    before_copy = started(before_any.at[:, m], before_ref, in_sems.at[0])
    up_copy = started(up_any.at[m], up_ref, in_sems.at[1])
    copies = []
    for piece in range(pieces):
        span = pl.ds(piece * depth, depth)
        for side, (ref, base) in enumerate(((own_any, core * half), (other_any, (1 - core) * half))):
            lanes = pl.ds(pl.multiple_of(base, 128), half)
            copies.append(started(ref.at[span], weight.at[span, lanes], w_sems.at[piece, side]))
        if piece == 0:
            down_copy = started(down_any.at[m], down_ref, in_sems.at[2])
            inv_copy = started(inv_any.at[m], inv_ref, in_sems.at[3])
            x_copy = started(x_any.at[m], x_ref, in_sems.at[4])

    tail = parts_ref[:, :, width:].astype(f32)
    coef = jnp.sum(jnp.sum(tail, axis=0), axis=1, keepdims=True)
    before_copy.wait()
    for part in range(4):
        fixed = parts_ref[part, :, :width].astype(f32) - coef * before_ref[part].astype(f32)
        full[:, part * width : (part + 1) * width] = fixed.astype(bf16)
    grad_ref[...] = full[:, pl.ds(pl.multiple_of(ypos * width, 128), width)]
    grad_copy = started(grad_ref, grad_any.at[m], out_sems.at[0])
    up_copy.wait()
    low = lax.dot_general(full[...], up_ref[...], contract_last, preferred_element_type=f32)
    low = own_group(low, group)
    low_ref[...] = low
    low_copy = started(low_ref, low_any.at[m], out_sems.at[1])
    down_copy.wait()
    total = low_rank_scale * lax.dot_general(
        low, down_ref[...], contract_inner, preferred_element_type=f32
    )
    for piece in range(pieces):
        copies[2 * piece].wait()
        copies[2 * piece + 1].wait()
        span = slice(piece * depth, (piece + 1) * depth)
        total = total + lax.dot_general(
            full[:, span], weight[span], contract_inner, preferred_element_type=f32
        )
    inv_copy.wait()
    x_copy.wait()
    sent, tail = message(
        total, grad_ref[...], gain_ref[...], inv_ref[:, 0:1], x_ref[...], width_all
    )
    box_ref[:, :width] = sent
    box_ref[:, width:] = tail
    box_copy = started(box_ref, boxes_any.at[m], out_sems.at[2])
    grad_copy.wait()
    low_copy.wait()
    box_copy.wait()


def run_stage(place, parts, before, up, down, gain, inv, x, own, other, kept):
    _, rows, width = x.shape
    width_all = own.shape[0]
    cols = up.shape[1]
    pieces = 5
    vmem = pl.BlockSpec(memory_space=pltpu.VMEM)
    any_space = pl.BlockSpec(memory_space=pl.ANY)
    return pl.pallas_call(
        functools.partial(stage_kernel, group=cols // 16),
        in_specs=[pl.BlockSpec(memory_space=pltpu.SMEM), vmem, vmem] + [any_space] * 10,
        out_specs=[vmem] + [any_space] * 3,
        scratch_shapes=[
            pltpu.VMEM((4, rows, width), bf16),
            pltpu.VMEM((cols, width_all), bf16),
            pltpu.VMEM((cols, width), bf16),
            pltpu.VMEM((rows, TAIL), f32),
            pltpu.VMEM((rows, width), bf16),
            pltpu.VMEM((rows, width_all), bf16),
            pltpu.VMEM((width_all, width), bf16),
            pltpu.VMEM((rows, cols), bf16),
            pltpu.VMEM((rows, width), bf16),
            pltpu.SemaphoreType.DMA((5,)),
            pltpu.SemaphoreType.DMA((pieces, 2)),
            pltpu.SemaphoreType.DMA((3,)),
        ],
        out_shape=[jax.ShapeDtypeStruct((rows, width + TAIL), bf16)]
        + [jax.ShapeDtypeStruct(k.shape, k.dtype) for k in kept],
        input_output_aliases={10: 1, 11: 2, 12: 3},
        compiler_params=pltpu.CompilerParams(vmem_limit_bytes=32 * 1024 * 1024),
        cost_estimate=pl.CostEstimate(
            flops=2 * rows * width * width_all, bytes_accessed=2 * width * width_all, transcendentals=0
        ),
        name="stage",
    )(place, parts, gain, before, up, down, inv, x, own, other, *kept)


def local(
    section_inputs,
    out_grads,
    proj_weight,
    norm_gain,
    adapter_down,
    adapter_up,
    tenant_ids,
    slot_table,
):
    sec = lax.axis_index("s")
    ypos = lax.axis_index("y")
    core = lax.axis_index("c")
    micro = section_inputs.shape[1]
    width_all = section_inputs.shape[3]
    half = proj_weight.shape[1]
    width = 2 * half
    toks = section_inputs.shape[2] // 2
    rank = adapter_down.shape[3]
    rows_all = micro * toks
    group = micro // CHUNKS
    rows = group * toks
    multiplier = low_rank_scale / (toks * 2 * lax.axis_size("z"))

    shard = proj_weight[0].T
    w_own = lax.all_gather(shard, "z", axis=0, tiled=True)

    x_full = section_inputs[0]
    x_mine = lax.dynamic_slice_in_dim(x_full, core * toks, toks, 1).reshape(rows_all, width_all)
    x_f = x_mine.astype(f32)
    inv_rms = lax.rsqrt(jnp.mean(x_f * x_f, axis=-1, keepdims=True) + norm_eps)
    x_y = lax.dynamic_slice_in_dim(x_mine, ypos * width, width, 1)
    normed_y = x_y.astype(f32) * inv_rms
    x_before = lax.cond(
        sec == 15,
        lambda x: jnp.zeros((4,) + x.shape, x.dtype),
        spread,
        lax.ppermute(x_y, "s", EVERY),
    )
    gain_y = both_cores(norm_gain, 1)
    down_y = both_cores(adapter_down[0], 1)
    h_y = (normed_y * gain_y).astype(bf16)

    iota = jnp.arange(micro, dtype=jnp.int32)
    tenant_hot = tenant_ids[:, None] == iota[None, :]
    slot_ids = jnp.sum(jnp.where(tenant_hot, slot_table[0][None, :], 0), axis=1)
    down_sel = down_y[slot_ids]
    up_sel = adapter_up[0][slot_ids]
    low_part = jnp.einsum(
        "mtd,mdr->mtr", h_y.reshape(micro, toks, width), down_sel, preferred_element_type=f32
    )

    def extra(args):
        h_y, low_part = args
        low_in = lax.psum(low_part, "y").astype(bf16)
        return lax.all_gather(h_y, "z"), lax.all_gather(low_in, "z")

    x_before = x_before.reshape(4, CHUNKS, rows, width)
    x_chunk = x_y.reshape(CHUNKS, rows, width)
    inv_chunk = jnp.broadcast_to(inv_rms.reshape(CHUNKS, rows, 1), (CHUNKS, rows, TAIL))
    down_chunk = down_sel.transpose(0, 2, 1).reshape(CHUNKS, group * rank, width)
    up_chunk = up_sel.reshape(CHUNKS, group * rank, width_all)

    def top(args):
        out_grads, shard = args
        shard_x = lax.ppermute(shard, ("s", "c"), TOP_SWAP)
        grad = lax.dynamic_slice_in_dim(out_grads, core * toks, toks, 1)
        low = jnp.einsum("mtd,mrd->mtr", grad, up_sel, preferred_element_type=f32).astype(bf16)
        adapt = jnp.einsum("mtr,mdr->mtd", low, down_sel, preferred_element_type=f32)
        grad = grad.reshape(rows_all, width_all)
        blocks = jnp.stack([grad[:, i * width : (i + 1) * width] for i in range(4)])
        blocks = lax.all_to_all(blocks, "z", 0, 0).reshape(4 * rows_all, width)
        mine, theirs = (
            lax.dot_general(blocks, w, contract_inner, preferred_element_type=f32).astype(bf16)
            for w in (shard, shard_x)
        )
        terms = jnp.concatenate(
            [jnp.where(core == 0, mine, theirs), jnp.where(core == 0, theirs, mine)], 1
        )
        terms = lax.all_to_all(terms.reshape(4, rows_all, width), "z", 0, 0)
        total = jnp.sum(terms.astype(f32), axis=0)
        total = total + low_rank_scale * adapt.reshape(rows_all, width)
        grad_y = lax.dynamic_slice_in_dim(grad, ypos * width, width, 1)
        sent, tail = message(total, grad_y, gain_y, inv_rms, x_y, width_all)
        boxes = jnp.concatenate([sent, tail], 1).reshape(CHUNKS, rows, width + TAIL)
        member = jnp.arange(rows_all)[:, None] // toks % group == jnp.arange(group)[None, :]
        low = jnp.where(member[:, :, None], low.reshape(rows_all, 1, rank), 0)
        low = low.astype(bf16).reshape(CHUNKS, rows, group * rank)
        return boxes, low, grad_y.reshape(CHUNKS, rows, width)

    def empty(args):
        return (
            jnp.zeros((CHUNKS, rows, width + TAIL), bf16),
            jnp.zeros((CHUNKS, rows, group * rank), bf16),
            jnp.zeros((CHUNKS, rows, width), bf16),
        )

    kept = lax.cond(sec == 15, top, empty, (out_grads, shard))

    boxes_top = lax.ppermute(kept[0], "s", [(15, 14)])

    ready = (x_before, x_chunk, inv_chunk, down_chunk, up_chunk, gain_y, kept, boxes_top)
    w_own, ready = lax.optimization_barrier((w_own, ready))
    x_before, x_chunk, inv_chunk, down_chunk, up_chunk, gain_y, kept, boxes_top = ready
    w_other = lax.ppermute(w_own, "c", SWAP)

    def pick(array, m):
        return lax.dynamic_index_in_dim(array, m, 0, keepdims=False)

    def step(u, state):
        box, kept, extras = state
        t, m = u // CHUNKS, u % CHUNKS
        turn = 15 - t + m

        def computed(args):
            box, kept = args
            place = jnp.stack([m, ypos, core]).astype(jnp.int32)
            parts = lax.cond(
                sec == 15, lambda box: jnp.zeros((4,) + box.shape, box.dtype), spread, box
            )
            box, *kept = run_stage(
                place,
                parts,
                x_before,
                up_chunk,
                down_chunk,
                gain_y,
                inv_chunk,
                x_chunk,
                w_own,
                w_other,
                kept,
            )
            return box, tuple(kept)

        box, kept = lax.cond(
            (sec == turn) & (sec < 15), computed, lambda args: args, (box, kept)
        )
        part = ((sec == turn) | (sec == turn - 1)) & (turn >= 1) & (turn <= 14)
        kind = jnp.where(part, jnp.where(turn % 2 == 1, 1, 2), 0)
        kind = jnp.where((turn == 15) & (sec == 14), 3, kind)
        box = lax.switch(
            kind,
            [
                lambda box: box,
                lambda box: lax.ppermute(box, "s", ODD),
                lambda box: lax.ppermute(box, "s", EVEN),
                lambda box: pick(boxes_top, m),
            ],
            box,
        )
        extras = lax.cond(
            (sec == turn - AHEAD) & (m == 0),
            lambda args: extra((h_y, low_part)),
            lambda args: args,
            extras,
        )
        return box, kept, extras

    start = (
        jnp.zeros((rows, width + TAIL), bf16),
        kept,
        (
            jnp.zeros((4, rows_all, width), bf16),
            jnp.zeros((4, micro, toks, rank), bf16),
        ),
    )
    _, kept, extras = lax.fori_loop(0, (15 + CHUNKS) * CHUNKS, step, start)
    boxes, low_all, grad_all = kept
    h_all, low_in_all = lax.cond(
        sec > 15 - AHEAD, lambda args: extra((h_y, low_part)), lambda args: args, extras
    )

    coefs = spread(boxes[:, :, width:])
    coefs, low_all, grad_all = lax.optimization_barrier((coefs, low_all, grad_all))
    coef_sum = jnp.sum(coefs.astype(f32), axis=(0, -1))[..., None]
    new_grads = boxes[:, :, :width].astype(f32) - coef_sum * x_chunk.astype(f32)
    new_grads = new_grads.astype(bf16).reshape(micro, toks, width)
    keep = jnp.where(core == 0, new_grads[:, :, :half], new_grads[:, :, half:])
    give = jnp.where(core == 0, new_grads[:, :, half:], new_grads[:, :, :half])
    got = lax.ppermute(give, "c", SWAP)
    kept = jnp.concatenate(
        [jnp.where(core == 0, keep, got), jnp.where(core == 0, got, keep)], 1
    )

    both = jnp.concatenate(
        [
            grad_all.reshape(rows_all, width),
            jnp.pad(low_all.reshape(rows_all, group * rank), ((0, 0), (0, TAIL - group * rank))),
        ],
        1,
    )
    both = lax.all_gather(both, "z").reshape(4, micro, toks, width + TAIL)
    grads_z = both[..., :width]
    low_z = both[..., width : width + group * rank].reshape(4, micro, toks, group, rank)
    low_z = jnp.sum(low_z.astype(f32), axis=3).astype(bf16)
    hidden_z = h_all.reshape(4, micro, toks, width)
    down_part = multiplier * jnp.einsum(
        "zmtd,zmtr->mdr", hidden_z, low_z, preferred_element_type=f32
    )
    up_part = multiplier * jnp.einsum(
        "zmtr,zmtd->mrd", low_in_all, grads_z, preferred_element_type=f32
    )
    down_acc = half_sum(down_part, 1)
    up_acc = half_sum(up_part, 2)
    slot_hot = slot_ids[None, :] == iota[:, None]
    down_out = jnp.sum(jnp.where(slot_hot[:, :, None, None], down_acc[None], 0.0), axis=1)
    up_out = jnp.sum(jnp.where(slot_hot[:, :, None, None], up_acc[None], 0.0), axis=1)
    return (kept[None], down_out[None], up_out[None])


def solution(mesh):
    fine = Mesh(mesh.devices.reshape(16, 4, 2, 4), ("s", "y", "c", "z"))
    mp = ("y", "c")
    placed = (
        P("s", None, "z", None),
        P(None, "z", None),
        P("s", mp, "z"),
        P("s", mp),
        P("s", None, mp, None),
        P("s", None, None, None),
        P(),
        P("s", None),
    )
    return jax.shard_map(
        local,
        mesh=fine,
        in_specs=placed,
        out_specs=(
            P("s", None, "z", mp),
            P("s", None, mp, None),
            P("s", None, None, mp),
        ),
        check_vma=False,
    )
```

```python
import functools

import jax
import jax.numpy as jnp
from jax import lax
from jax.experimental import pallas as pl
from jax.experimental.pallas import tpu as pltpu
from jax.sharding import Mesh, PartitionSpec as P

norm_eps = 1e-05
low_rank_scale = 2.0
CHUNKS = 2
TAIL = 128
SWAP = [(0, 1), (1, 0)]
ODD = [(s, s - 1) for s in range(15, 0, -2)]
EVEN = [(s, s - 1) for s in range(14, 0, -2)]
EVERY = [(s, s - 1) for s in range(15, 0, -1)]
f32 = jnp.float32
bf16 = jnp.bfloat16
contract_last = (((1,), (1,)), ((), ()))
contract_inner = (((1,), (0,)), ((), ()))
AHEAD = 3


def both_cores(value, axis):
    core = lax.axis_index("c")
    other = lax.ppermute(value, "c", SWAP)
    low = jnp.where(core == 0, value, other)
    high = jnp.where(core == 0, other, value)
    return jnp.concatenate([low, high], axis)


def half_sum(value, axis):
    core = lax.axis_index("c")
    width = value.shape[axis] // 2
    low = lax.slice_in_dim(value, 0, width, axis=axis)
    high = lax.slice_in_dim(value, width, 2 * width, axis=axis)
    mine = jnp.where(core == 0, low, high)
    theirs = jnp.where(core == 0, high, low)
    return mine + lax.ppermute(theirs, "c", SWAP)


def spread(value):
    sent = jnp.broadcast_to(value[None], (4,) + value.shape)
    return lax.all_to_all(sent, "y", 0, 0)


def own_group(low, group):
    rows, cols = low.shape
    row_group = lax.broadcasted_iota(jnp.int32, low.shape, 0) // (rows // group)
    col_group = lax.broadcasted_iota(jnp.int32, low.shape, 1) // (cols // group)
    return jnp.where(row_group == col_group, low, 0.0).astype(bf16)


def message(total, grad_y, gain, inv, x, width_all):
    rows, width = total.shape
    normed_grad = (total * gain).astype(bf16).astype(f32)
    sent = (grad_y.astype(f32) + inv * normed_grad).astype(bf16)
    coef = jnp.sum(normed_grad * x.astype(f32), axis=1, keepdims=True)
    coef = coef * (inv * inv * inv / width_all)
    lane = lax.broadcasted_iota(jnp.int32, (rows, TAIL), 1)
    high = lax.reduce_precision(coef, 8, 7)
    tail = jnp.where(lane == 0, high, jnp.where(lane == 1, coef - high, 0.0)).astype(bf16)
    return sent, tail


def stage_kernel(
    place_ref,
    parts_ref,
    gain_ref,
    before_any,
    up_any,
    down_any,
    inv_any,
    x_any,
    own_any,
    other_any,
    boxes_in,
    low_in,
    grad_in,
    box_ref,
    boxes_any,
    low_any,
    grad_any,
    before_ref,
    up_ref,
    down_ref,
    inv_ref,
    x_ref,
    full,
    weight,
    low_ref,
    grad_ref,
    in_sems,
    w_sems,
    out_sems,
    *,
    group,
):
    del boxes_in, low_in, grad_in
    m, ypos, core = place_ref[0], place_ref[1], place_ref[2]
    width = x_ref.shape[1]
    width_all = full.shape[1]
    half = width // 2
    pieces = w_sems.shape[0]
    depth = width_all // pieces

    def started(source, target, sem):
        copy = pltpu.make_async_copy(source, target, sem)
        copy.start()
        return copy

    before_copy = started(before_any.at[:, m], before_ref, in_sems.at[0])
    up_copy = started(up_any.at[m], up_ref, in_sems.at[1])
    copies = []
    for piece in range(pieces):
        span = pl.ds(piece * depth, depth)
        for side, (ref, base) in enumerate(((own_any, core * half), (other_any, (1 - core) * half))):
            lanes = pl.ds(pl.multiple_of(base, 128), half)
            copies.append(started(ref.at[span], weight.at[span, lanes], w_sems.at[piece, side]))
        if piece == 0:
            down_copy = started(down_any.at[m], down_ref, in_sems.at[2])
            inv_copy = started(inv_any.at[m], inv_ref, in_sems.at[3])
            x_copy = started(x_any.at[m], x_ref, in_sems.at[4])

    tail = parts_ref[:, :, width:].astype(f32)
    coef = jnp.sum(jnp.sum(tail, axis=0), axis=1, keepdims=True)
    before_copy.wait()
    for part in range(4):
        fixed = parts_ref[part, :, :width].astype(f32) - coef * before_ref[part].astype(f32)
        full[:, part * width : (part + 1) * width] = fixed.astype(bf16)
    grad_ref[...] = full[:, pl.ds(pl.multiple_of(ypos * width, 128), width)]
    grad_copy = started(grad_ref, grad_any.at[m], out_sems.at[0])
    up_copy.wait()
    low = lax.dot_general(full[...], up_ref[...], contract_last, preferred_element_type=f32)
    low = own_group(low, group)
    low_ref[...] = low
    low_copy = started(low_ref, low_any.at[m], out_sems.at[1])
    down_copy.wait()
    total = low_rank_scale * lax.dot_general(
        low, down_ref[...], contract_inner, preferred_element_type=f32
    )
    for piece in range(pieces):
        copies[2 * piece].wait()
        copies[2 * piece + 1].wait()
        span = slice(piece * depth, (piece + 1) * depth)
        total = total + lax.dot_general(
            full[:, span], weight[span], contract_inner, preferred_element_type=f32
        )
    inv_copy.wait()
    x_copy.wait()
    sent, tail = message(
        total, grad_ref[...], gain_ref[...], inv_ref[:, 0:1], x_ref[...], width_all
    )
    box_ref[:, :width] = sent
    box_ref[:, width:] = tail
    box_copy = started(box_ref, boxes_any.at[m], out_sems.at[2])
    grad_copy.wait()
    low_copy.wait()
    box_copy.wait()


def run_stage(place, parts, before, up, down, gain, inv, x, own, other, kept):
    _, rows, width = x.shape
    width_all = own.shape[0]
    cols = up.shape[1]
    pieces = 5
    vmem = pl.BlockSpec(memory_space=pltpu.VMEM)
    any_space = pl.BlockSpec(memory_space=pl.ANY)
    return pl.pallas_call(
        functools.partial(stage_kernel, group=cols // 16),
        in_specs=[pl.BlockSpec(memory_space=pltpu.SMEM), vmem, vmem] + [any_space] * 10,
        out_specs=[vmem] + [any_space] * 3,
        scratch_shapes=[
            pltpu.VMEM((4, rows, width), bf16),
            pltpu.VMEM((cols, width_all), bf16),
            pltpu.VMEM((cols, width), bf16),
            pltpu.VMEM((rows, TAIL), f32),
            pltpu.VMEM((rows, width), bf16),
            pltpu.VMEM((rows, width_all), bf16),
            pltpu.VMEM((width_all, width), bf16),
            pltpu.VMEM((rows, cols), bf16),
            pltpu.VMEM((rows, width), bf16),
            pltpu.SemaphoreType.DMA((5,)),
            pltpu.SemaphoreType.DMA((pieces, 2)),
            pltpu.SemaphoreType.DMA((3,)),
        ],
        out_shape=[jax.ShapeDtypeStruct((rows, width + TAIL), bf16)]
        + [jax.ShapeDtypeStruct(k.shape, k.dtype) for k in kept],
        input_output_aliases={10: 1, 11: 2, 12: 3},
        compiler_params=pltpu.CompilerParams(vmem_limit_bytes=32 * 1024 * 1024),
        cost_estimate=pl.CostEstimate(
            flops=2 * rows * width * width_all, bytes_accessed=2 * width * width_all, transcendentals=0
        ),
        name="stage",
    )(place, parts, gain, before, up, down, inv, x, own, other, *kept)


def local(
    section_inputs,
    out_grads,
    proj_weight,
    norm_gain,
    adapter_down,
    adapter_up,
    tenant_ids,
    slot_table,
):
    sec = lax.axis_index("s")
    ypos = lax.axis_index("y")
    core = lax.axis_index("c")
    micro = section_inputs.shape[1]
    width_all = section_inputs.shape[3]
    half = proj_weight.shape[1]
    width = 2 * half
    toks = section_inputs.shape[2] // 2
    rank = adapter_down.shape[3]
    rows_all = micro * toks
    group = micro // CHUNKS
    rows = group * toks
    multiplier = low_rank_scale / (toks * 2 * lax.axis_size("z"))

    shard = proj_weight[0].T
    w_own = lax.all_gather(shard, "z", axis=0, tiled=True)

    x_full = section_inputs[0]
    x_mine = lax.dynamic_slice_in_dim(x_full, core * toks, toks, 1).reshape(rows_all, width_all)
    x_f = x_mine.astype(f32)
    inv_rms = lax.rsqrt(jnp.mean(x_f * x_f, axis=-1, keepdims=True) + norm_eps)
    x_y = lax.dynamic_slice_in_dim(x_mine, ypos * width, width, 1)
    normed_y = x_y.astype(f32) * inv_rms
    x_before = lax.cond(
        sec == 15,
        lambda x: jnp.zeros((4,) + x.shape, x.dtype),
        spread,
        lax.ppermute(x_y, "s", EVERY),
    )
    gain_y = both_cores(norm_gain, 1)
    down_y = both_cores(adapter_down[0], 1)
    h_y = (normed_y * gain_y).astype(bf16)

    iota = jnp.arange(micro, dtype=jnp.int32)
    tenant_hot = tenant_ids[:, None] == iota[None, :]
    slot_ids = jnp.sum(jnp.where(tenant_hot, slot_table[0][None, :], 0), axis=1)
    down_sel = down_y[slot_ids]
    up_sel = adapter_up[0][slot_ids]
    low_part = jnp.einsum(
        "mtd,mdr->mtr", h_y.reshape(micro, toks, width), down_sel, preferred_element_type=f32
    )

    def extra(args):
        h_y, low_part = args
        low_in = lax.psum(low_part, "y").astype(bf16)
        return lax.all_gather(h_y, "z"), lax.all_gather(low_in, "z")

    x_before = x_before.reshape(4, CHUNKS, rows, width)
    x_chunk = x_y.reshape(CHUNKS, rows, width)
    inv_chunk = jnp.broadcast_to(inv_rms.reshape(CHUNKS, rows, 1), (CHUNKS, rows, TAIL))
    down_chunk = down_sel.transpose(0, 2, 1).reshape(CHUNKS, group * rank, width)
    up_chunk = up_sel.reshape(CHUNKS, group * rank, width_all)

    grads_top = lax.dynamic_slice_in_dim(out_grads, core * toks, toks, 1)
    grads_top = grads_top.reshape(CHUNKS, rows, width_all)
    grads_top = jnp.stack([grads_top[:, :, i * width : (i + 1) * width] for i in range(4)], 1)
    grads_top = jnp.pad(grads_top, ((0, 0), (0, 0), (0, 0), (0, TAIL)))
    kept = (
        jnp.zeros((CHUNKS, rows, width + TAIL), bf16),
        jnp.zeros((CHUNKS, rows, group * rank), bf16),
        jnp.zeros((CHUNKS, rows, width), bf16),
    )

    ready = (x_before, x_chunk, inv_chunk, down_chunk, up_chunk, gain_y, kept, grads_top)
    w_own, ready = lax.optimization_barrier((w_own, ready))
    x_before, x_chunk, inv_chunk, down_chunk, up_chunk, gain_y, kept, grads_top = ready
    w_other = lax.ppermute(w_own, "c", SWAP)

    def pick(array, m):
        return lax.dynamic_index_in_dim(array, m, 0, keepdims=False)

    def step(u, state):
        box, kept, extras = state
        t, m = u // CHUNKS, u % CHUNKS
        turn = 15 - t + m

        def computed(args):
            box, kept = args
            place = jnp.stack([m, ypos, core]).astype(jnp.int32)
            parts = lax.cond(sec == 15, lambda box: pick(grads_top, m), spread, box)
            box, *kept = run_stage(
                place,
                parts,
                x_before,
                up_chunk,
                down_chunk,
                gain_y,
                inv_chunk,
                x_chunk,
                w_own,
                w_other,
                kept,
            )
            return box, tuple(kept)

        box, kept = lax.cond(sec == turn, computed, lambda args: args, (box, kept))
        part = ((sec == turn) | (sec == turn - 1)) & (turn >= 1) & (turn <= 15)
        kind = jnp.where(part, jnp.where(turn % 2 == 1, 1, 2), 0)
        box = lax.switch(
            kind,
            [
                lambda box: box,
                lambda box: lax.ppermute(box, "s", ODD),
                lambda box: lax.ppermute(box, "s", EVEN),
            ],
            box,
        )
        extras = lax.cond(
            (sec == turn - AHEAD) & (m == 0),
            lambda args: extra((h_y, low_part)),
            lambda args: args,
            extras,
        )
        return box, kept, extras

    start = (
        jnp.zeros((rows, width + TAIL), bf16),
        kept,
        (
            jnp.zeros((4, rows_all, width), bf16),
            jnp.zeros((4, micro, toks, rank), bf16),
        ),
    )
    _, kept, extras = lax.fori_loop(0, (15 + CHUNKS) * CHUNKS, step, start)
    boxes, low_all, grad_all = kept
    h_all, low_in_all = lax.cond(
        sec > 15 - AHEAD, lambda args: extra((h_y, low_part)), lambda args: args, extras
    )

    coefs = spread(boxes[:, :, width:])
    coefs, low_all, grad_all = lax.optimization_barrier((coefs, low_all, grad_all))
    coef_sum = jnp.sum(coefs.astype(f32), axis=(0, -1))[..., None]
    new_grads = boxes[:, :, :width].astype(f32) - coef_sum * x_chunk.astype(f32)
    new_grads = new_grads.astype(bf16).reshape(micro, toks, width)
    keep = jnp.where(core == 0, new_grads[:, :, :half], new_grads[:, :, half:])
    give = jnp.where(core == 0, new_grads[:, :, half:], new_grads[:, :, :half])
    got = lax.ppermute(give, "c", SWAP)
    kept = jnp.concatenate(
        [jnp.where(core == 0, keep, got), jnp.where(core == 0, got, keep)], 1
    )

    both = jnp.concatenate(
        [
            grad_all.reshape(rows_all, width),
            jnp.pad(low_all.reshape(rows_all, group * rank), ((0, 0), (0, TAIL - group * rank))),
        ],
        1,
    )
    both = lax.all_gather(both, "z").reshape(4, micro, toks, width + TAIL)
    grads_z = both[..., :width]
    low_z = both[..., width : width + group * rank].reshape(4, micro, toks, group, rank)
    low_z = jnp.sum(low_z.astype(f32), axis=3).astype(bf16)
    hidden_z = h_all.reshape(4, micro, toks, width)
    down_part = multiplier * jnp.einsum(
        "zmtd,zmtr->mdr", hidden_z, low_z, preferred_element_type=f32
    )
    up_part = multiplier * jnp.einsum(
        "zmtr,zmtd->mrd", low_in_all, grads_z, preferred_element_type=f32
    )
    down_acc = half_sum(down_part, 1)
    up_acc = half_sum(up_part, 2)
    slot_hot = slot_ids[None, :] == iota[:, None]
    down_out = jnp.sum(jnp.where(slot_hot[:, :, None, None], down_acc[None], 0.0), axis=1)
    up_out = jnp.sum(jnp.where(slot_hot[:, :, None, None], up_acc[None], 0.0), axis=1)
    return (kept[None], down_out[None], up_out[None])


def solution(mesh):
    fine = Mesh(mesh.devices.reshape(16, 4, 2, 4), ("s", "y", "c", "z"))
    mp = ("y", "c")
    placed = (
        P("s", None, "z", None),
        P(None, "z", None),
        P("s", mp, "z"),
        P("s", mp),
        P("s", None, mp, None),
        P("s", None, None, None),
        P(),
        P("s", None),
    )
    return jax.shard_map(
        local,
        mesh=fine,
        in_specs=placed,
        out_specs=(
            P("s", None, "z", mp),
            P("s", None, mp, None),
            P("s", None, None, mp),
        ),
        check_vma=False,
    )
```

```python
import functools

import jax
import jax.numpy as jnp
from jax import lax
from jax.experimental import pallas as pl
from jax.experimental.pallas import tpu as pltpu
from jax.sharding import Mesh, PartitionSpec as P

norm_eps = 1e-05
low_rank_scale = 2.0
CHUNKS = 2
TAIL = 128
SWAP = [(0, 1), (1, 0)]
ODD = [(s, s - 1) for s in range(15, 0, -2)]
EVEN = [(s, s - 1) for s in range(14, 0, -2)]
EVERY = [(s, s - 1) for s in range(15, 0, -1)]
f32 = jnp.float32
bf16 = jnp.bfloat16
contract_last = (((1,), (1,)), ((), ()))
contract_inner = (((1,), (0,)), ((), ()))
AHEAD = 3
TOP_SWAP = [(30, 31), (31, 30)]
RIGHT = [(4 * s + z, 4 * s + (z + 1) % 4) for s in range(15) for z in range(4)]
LEFT = [(4 * s + z, 4 * s + (z + 3) % 4) for s in range(15) for z in range(4)]
PAIRS = [(2 * s + c, 2 * s + 1 - c) for s in range(15) for c in range(2)]


def both_cores(value, axis):
    core = lax.axis_index("c")
    other = lax.ppermute(value, "c", SWAP)
    low = jnp.where(core == 0, value, other)
    high = jnp.where(core == 0, other, value)
    return jnp.concatenate([low, high], axis)


def half_sum(value, axis):
    core = lax.axis_index("c")
    width = value.shape[axis] // 2
    low = lax.slice_in_dim(value, 0, width, axis=axis)
    high = lax.slice_in_dim(value, width, 2 * width, axis=axis)
    mine = jnp.where(core == 0, low, high)
    theirs = jnp.where(core == 0, high, low)
    return mine + lax.ppermute(theirs, "c", SWAP)


def spread(value):
    sent = jnp.broadcast_to(value[None], (4,) + value.shape)
    return lax.all_to_all(sent, "y", 0, 0)


def own_group(low, group):
    rows, cols = low.shape
    row_group = lax.broadcasted_iota(jnp.int32, low.shape, 0) // (rows // group)
    col_group = lax.broadcasted_iota(jnp.int32, low.shape, 1) // (cols // group)
    return jnp.where(row_group == col_group, low, 0.0).astype(bf16)


def message(total, grad_y, gain, inv, x, width_all):
    rows, width = total.shape
    normed_grad = (total * gain).astype(bf16).astype(f32)
    sent = (grad_y.astype(f32) + inv * normed_grad).astype(bf16)
    coef = jnp.sum(normed_grad * x.astype(f32), axis=1, keepdims=True)
    coef = coef * (inv * inv * inv / width_all)
    lane = lax.broadcasted_iota(jnp.int32, (rows, TAIL), 1)
    high = lax.reduce_precision(coef, 8, 7)
    tail = jnp.where(lane == 0, high, jnp.where(lane == 1, coef - high, 0.0)).astype(bf16)
    return sent, tail


def stage_kernel(place_ref, parts_ref, gain_ref, before_any, up_any, down_any, inv_any, x_any, *refs, group):
    weights, refs = refs[:16], refs[16 + 4 :]
    box_ref, boxes_any, low_any, grad_any, tail_any = refs[:5]
    before_ref, up_ref, down_ref, inv_ref, x_ref, full, weight, low_ref, grad_ref, tail_ref = refs[5:15]
    in_sems, w_sems, out_sems = refs[15:]
    m, ypos, core, zpos = place_ref[0], place_ref[1], place_ref[2], place_ref[3]
    width = x_ref.shape[1]
    width_all = full.shape[1]
    half = width // 2

    def started(source, target, sem):
        copy = pltpu.make_async_copy(source, target, sem)
        copy.start()
        return copy

    before_copy = started(before_any.at[:, m], before_ref, in_sems.at[0])
    up_copy = started(up_any.at[m], up_ref, in_sems.at[1])
    copies = []
    for piece in range(8):
        for side, base in enumerate((core * half, (1 - core) * half)):
            lanes = pl.ds(pl.multiple_of(base, 128), half)
            target = weight.at[pl.ds(piece * half, half), lanes]
            copies.append(started(weights[8 * side + piece], target, w_sems.at[piece, side]))
        if piece == 0:
            down_copy = started(down_any.at[m], down_ref, in_sems.at[2])
            inv_copy = started(inv_any.at[m], inv_ref, in_sems.at[3])
            x_copy = started(x_any.at[m], x_ref, in_sems.at[4])

    tail = parts_ref[:, :, width:].astype(f32)
    coef = jnp.sum(jnp.sum(tail, axis=0), axis=1, keepdims=True)
    before_copy.wait()
    up_copy.wait()
    low = None
    for part in range(4):
        fixed = parts_ref[part, :, :width].astype(f32) - coef * before_ref[part].astype(f32)
        fixed = fixed.astype(bf16)
        first = 2 * lax.rem(zpos - part + 4, 4) * half
        second = (2 * lax.rem(part - zpos + 4, 4) + 1) * half
        full[:, pl.ds(pl.multiple_of(first, 128), half)] = fixed[:, :half]
        full[:, pl.ds(pl.multiple_of(second, 128), half)] = fixed[:, half:]

        @pl.when(part == ypos)
        def _(fixed=fixed):
            grad_ref[...] = fixed

        term = lax.dot_general(
            fixed,
            up_ref[:, part * width : (part + 1) * width],
            contract_last,
            preferred_element_type=f32,
        )
        low = term if low is None else low + term
    grad_copy = started(grad_ref, grad_any.at[m], out_sems.at[0])
    low = own_group(low, group)
    low_ref[...] = low
    low_copy = started(low_ref, low_any.at[m], out_sems.at[1])
    down_copy.wait()
    total = low_rank_scale * lax.dot_general(
        low, down_ref[...], contract_inner, preferred_element_type=f32
    )
    for part in range(4):
        for copy in copies[4 * part : 4 * part + 4]:
            copy.wait()
        span = slice(part * width, (part + 1) * width)
        total = total + lax.dot_general(
            full[:, span], weight[span], contract_inner, preferred_element_type=f32
        )
    inv_copy.wait()
    x_copy.wait()
    sent, tail = message(
        total, grad_ref[...], gain_ref[...], inv_ref[:, 0:1], x_ref[...], width_all
    )
    box_ref[:, :width] = sent
    box_ref[:, width:] = tail
    tail_ref[...] = tail
    box_copy = started(box_ref, boxes_any.at[m], out_sems.at[2])
    tail_copy = started(tail_ref, tail_any.at[m], out_sems.at[3])
    grad_copy.wait()
    low_copy.wait()
    box_copy.wait()
    tail_copy.wait()


def run_stage(place, parts, before, up, down, gain, inv, x, weights, kept):
    _, rows, width = x.shape
    width_all = 4 * width
    cols = up.shape[1]
    vmem = pl.BlockSpec(memory_space=pltpu.VMEM)
    any_space = pl.BlockSpec(memory_space=pl.ANY)
    inputs = [place, parts, gain, before, up, down, inv, x, *weights]
    return pl.pallas_call(
        functools.partial(stage_kernel, group=cols // 16),
        in_specs=[pl.BlockSpec(memory_space=pltpu.SMEM), vmem, vmem]
        + [any_space] * (len(inputs) + len(kept) - 3),
        out_specs=[vmem] + [any_space] * len(kept),
        scratch_shapes=[
            pltpu.VMEM((4, rows, width), bf16),
            pltpu.VMEM((cols, width_all), bf16),
            pltpu.VMEM((cols, width), bf16),
            pltpu.VMEM((rows, TAIL), f32),
            pltpu.VMEM((rows, width), bf16),
            pltpu.VMEM((rows, width_all), bf16),
            pltpu.VMEM((width_all, width), bf16),
            pltpu.VMEM((rows, cols), bf16),
            pltpu.VMEM((rows, width), bf16),
            pltpu.VMEM((rows, TAIL), bf16),
            pltpu.SemaphoreType.DMA((5,)),
            pltpu.SemaphoreType.DMA((8, 2)),
            pltpu.SemaphoreType.DMA((4,)),
        ],
        out_shape=[jax.ShapeDtypeStruct((rows, width + TAIL), bf16)]
        + [jax.ShapeDtypeStruct(k.shape, k.dtype) for k in kept],
        input_output_aliases={len(inputs) + i: 1 + i for i in range(len(kept))},
        compiler_params=pltpu.CompilerParams(vmem_limit_bytes=32 * 1024 * 1024),
        cost_estimate=pl.CostEstimate(
            flops=2 * rows * width * width_all, bytes_accessed=2 * width * width_all, transcendentals=0
        ),
        name="stage",
    )(*inputs, *kept)


def local(
    section_inputs,
    out_grads,
    proj_weight,
    norm_gain,
    adapter_down,
    adapter_up,
    tenant_ids,
    slot_table,
):
    sec = lax.axis_index("s")
    ypos = lax.axis_index("y")
    core = lax.axis_index("c")
    micro = section_inputs.shape[1]
    width_all = section_inputs.shape[3]
    half = proj_weight.shape[1]
    width = 2 * half
    toks = section_inputs.shape[2] // 2
    rank = adapter_down.shape[3]
    rows_all = micro * toks
    group = micro // CHUNKS
    rows = group * toks
    multiplier = low_rank_scale / (toks * 2 * lax.axis_size("z"))

    zpos = lax.axis_index("z")
    first = proj_weight[0][:, :half].T
    second = proj_weight[0][:, half:].T
    right_1 = lax.ppermute(first, ("s", "z"), RIGHT)
    left_1 = lax.ppermute(second, ("s", "z"), LEFT)

    x_full = section_inputs[0]
    x_mine = lax.dynamic_slice_in_dim(x_full, core * toks, toks, 1).reshape(rows_all, width_all)
    x_f = x_mine.astype(f32)
    inv_rms = lax.rsqrt(jnp.mean(x_f * x_f, axis=-1, keepdims=True) + norm_eps)
    x_y = lax.dynamic_slice_in_dim(x_mine, ypos * width, width, 1)
    normed_y = x_y.astype(f32) * inv_rms
    x_before = lax.cond(
        sec == 15,
        lambda x: jnp.zeros((4,) + x.shape, x.dtype),
        spread,
        lax.ppermute(x_y, "s", EVERY),
    )
    gain_y = both_cores(norm_gain, 1)
    down_y = both_cores(adapter_down[0], 1)
    h_y = (normed_y * gain_y).astype(bf16)

    iota = jnp.arange(micro, dtype=jnp.int32)
    tenant_hot = tenant_ids[:, None] == iota[None, :]
    slot_ids = jnp.sum(jnp.where(tenant_hot, slot_table[0][None, :], 0), axis=1)
    down_sel = down_y[slot_ids]
    up_sel = adapter_up[0][slot_ids]
    low_part = jnp.einsum(
        "mtd,mdr->mtr", h_y.reshape(micro, toks, width), down_sel, preferred_element_type=f32
    )

    def extra(args):
        h_y, low_part = args
        low_in = lax.psum(low_part, "y").astype(bf16)
        return lax.all_gather(h_y, "z"), lax.all_gather(low_in, "z")

    x_before = x_before.reshape(4, CHUNKS, rows, width)
    x_chunk = x_y.reshape(CHUNKS, rows, width)
    inv_chunk = jnp.broadcast_to(inv_rms.reshape(CHUNKS, rows, 1), (CHUNKS, rows, TAIL))
    down_chunk = down_sel.transpose(0, 2, 1).reshape(CHUNKS, group * rank, width)
    up_chunk = up_sel.reshape(CHUNKS, group * rank, width_all)

    ready = (x_before, x_chunk, inv_chunk, down_chunk, up_chunk, gain_y)
    right_1, left_1, ready = lax.optimization_barrier((right_1, left_1, ready))
    x_before, x_chunk, inv_chunk, down_chunk, up_chunk, gain_y = ready

    def top(args):
        out_grads, first, second = args[:3]
        shard = jnp.concatenate([first, second], 0)
        shard_x = lax.ppermute(shard, ("s", "c"), TOP_SWAP)
        grad = lax.dynamic_slice_in_dim(out_grads, core * toks, toks, 1)
        low = jnp.einsum("mtd,mrd->mtr", grad, up_sel, preferred_element_type=f32).astype(bf16)
        adapt = jnp.einsum("mtr,mdr->mtd", low, down_sel, preferred_element_type=f32)
        grad = grad.reshape(rows_all, width_all)
        blocks = jnp.stack([grad[:, i * width : (i + 1) * width] for i in range(4)])
        blocks = lax.all_to_all(blocks, "z", 0, 0).reshape(4 * rows_all, width)
        mine, theirs = (
            lax.dot_general(blocks, w, contract_inner, preferred_element_type=f32).astype(bf16)
            for w in (shard, shard_x)
        )
        terms = jnp.concatenate(
            [jnp.where(core == 0, mine, theirs), jnp.where(core == 0, theirs, mine)], 1
        )
        terms = lax.all_to_all(terms.reshape(4, rows_all, width), "z", 0, 0)
        total = jnp.sum(terms.astype(f32), axis=0)
        total = total + low_rank_scale * adapt.reshape(rows_all, width)
        grad_y = lax.dynamic_slice_in_dim(grad, ypos * width, width, 1)
        sent, tail = message(total, grad_y, gain_y, inv_rms, x_y, width_all)
        boxes = jnp.concatenate([sent, tail], 1).reshape(CHUNKS, rows, width + TAIL)
        member = jnp.arange(rows_all)[:, None] // toks % group == jnp.arange(group)[None, :]
        low = jnp.where(member[:, :, None], low.reshape(rows_all, 1, rank), 0)
        low = low.astype(bf16).reshape(CHUNKS, rows, group * rank)
        tail = tail.reshape(CHUNKS, rows, TAIL)
        moved = tuple(jnp.zeros(first.shape, first.dtype) for _ in range(12))
        return moved, (boxes, low, grad_y.reshape(CHUNKS, rows, width), tail)

    def around(args):
        _, first, second, right_1, left_1 = args

        def swapped(value):
            return lax.ppermute(value, ("s", "c"), PAIRS)

        right_2 = lax.ppermute(right_1, ("s", "z"), RIGHT)
        left_2 = lax.ppermute(left_1, ("s", "z"), LEFT)
        others = [swapped(w) for w in (first, second, right_1, left_1)]
        right_2, left_2, others = lax.optimization_barrier((right_2, left_2, others))
        right_3 = lax.ppermute(right_2, ("s", "z"), RIGHT)
        left_3 = lax.ppermute(left_2, ("s", "z"), LEFT)
        more = [swapped(w) for w in (right_2, left_2)]
        right_3, left_3, more = lax.optimization_barrier((right_3, left_3, more))
        more = more + [swapped(w) for w in (right_3, left_3)]
        kept = (
            jnp.zeros((CHUNKS, rows, width + TAIL), bf16),
            jnp.zeros((CHUNKS, rows, group * rank), bf16),
            jnp.zeros((CHUNKS, rows, width), bf16),
            jnp.zeros((CHUNKS, rows, TAIL), bf16),
        )
        return (right_2, left_2, right_3, left_3, *others, *more), kept

    args = (out_grads, first, second, right_1, left_1)
    moved, kept = lax.cond(sec == 15, top, around, args)
    weights = [first, second, right_1, left_1, *moved]

    def pick(array, m):
        return lax.dynamic_index_in_dim(array, m, 0, keepdims=False)

    def step(u, state):
        box, kept, extras = state
        t, m = u // CHUNKS, u % CHUNKS
        turn = 15 - t + m

        def stored(args):
            _, kept = args
            return pick(kept[0], m), kept

        def computed(args):
            box, kept = args
            place = jnp.stack([m, ypos, core, zpos]).astype(jnp.int32)
            parts = lax.cond(
                sec == 15, lambda box: jnp.zeros((4,) + box.shape, box.dtype), spread, box
            )
            box, *kept = run_stage(
                place,
                parts,
                x_before,
                up_chunk,
                down_chunk,
                gain_y,
                inv_chunk,
                x_chunk,
                weights,
                kept,
            )
            return box, tuple(kept)

        kind = jnp.where(sec == turn, jnp.where(sec == 15, 1, 2), 0)
        box, kept = lax.switch(kind, [lambda args: args, stored, computed], (box, kept))
        part = ((sec == turn) | (sec == turn - 1)) & (turn >= 1) & (turn <= 15)
        kind = jnp.where(part, jnp.where(turn % 2 == 1, 1, 2), 0)
        box = lax.switch(
            kind,
            [
                lambda box: box,
                lambda box: lax.ppermute(box, "s", ODD),
                lambda box: lax.ppermute(box, "s", EVEN),
            ],
            box,
        )
        extras = lax.cond(
            (sec == turn - AHEAD) & (m == 0),
            lambda args: extra((h_y, low_part)),
            lambda args: args,
            extras,
        )
        return box, kept, extras

    start = (
        jnp.zeros((rows, width + TAIL), bf16),
        kept,
        (
            jnp.zeros((4, rows_all, width), bf16),
            jnp.zeros((4, micro, toks, rank), bf16),
        ),
    )
    _, kept, extras = lax.fori_loop(0, (15 + CHUNKS) * CHUNKS, step, start)
    boxes, low_all, grad_all, tail_all = kept
    h_all, low_in_all = lax.cond(
        sec > 15 - AHEAD, lambda args: extra((h_y, low_part)), lambda args: args, extras
    )

    coefs = spread(tail_all)
    coef_sum = jnp.sum(coefs.astype(f32), axis=(0, -1))[..., None]
    new_grads = boxes[:, :, :width].astype(f32) - coef_sum * x_chunk.astype(f32)
    new_grads = new_grads.astype(bf16).reshape(micro, toks, width)
    keep = jnp.where(core == 0, new_grads[:, :, :half], new_grads[:, :, half:])
    give = jnp.where(core == 0, new_grads[:, :, half:], new_grads[:, :, :half])
    got = lax.ppermute(give, "c", SWAP)
    kept = jnp.concatenate(
        [jnp.where(core == 0, keep, got), jnp.where(core == 0, got, keep)], 1
    )

    both = jnp.concatenate(
        [
            grad_all.reshape(rows_all, width),
            jnp.pad(low_all.reshape(rows_all, group * rank), ((0, 0), (0, TAIL - group * rank))),
        ],
        1,
    )
    both = lax.all_gather(both, "z").reshape(4, micro, toks, width + TAIL)
    grads_z = both[..., :width]
    low_z = both[..., width : width + group * rank].reshape(4, micro, toks, group, rank)
    low_z = jnp.sum(low_z.astype(f32), axis=3).astype(bf16)
    hidden_z = h_all.reshape(4, micro, toks, width)
    down_part = multiplier * jnp.einsum(
        "zmtd,zmtr->mdr", hidden_z, low_z, preferred_element_type=f32
    )
    up_part = multiplier * jnp.einsum(
        "zmtr,zmtd->mrd", low_in_all, grads_z, preferred_element_type=f32
    )
    down_acc = half_sum(down_part, 1)
    up_acc = half_sum(up_part, 2)
    slot_hot = slot_ids[None, :] == iota[:, None]
    down_out = jnp.sum(jnp.where(slot_hot[:, :, None, None], down_acc[None], 0.0), axis=1)
    up_out = jnp.sum(jnp.where(slot_hot[:, :, None, None], up_acc[None], 0.0), axis=1)
    return (kept[None], down_out[None], up_out[None])


def solution(mesh):
    fine = Mesh(mesh.devices.reshape(16, 4, 2, 4), ("s", "y", "c", "z"))
    mp = ("y", "c")
    placed = (
        P("s", None, "z", None),
        P(None, "z", None),
        P("s", mp, "z"),
        P("s", mp),
        P("s", None, mp, None),
        P("s", None, None, None),
        P(),
        P("s", None),
    )
    return jax.shard_map(
        local,
        mesh=fine,
        in_specs=placed,
        out_specs=(
            P("s", None, "z", mp),
            P("s", None, mp, None),
            P("s", None, None, mp),
        ),
        check_vma=False,
    )
```

```python
import functools

import jax
import jax.numpy as jnp
from jax import lax
from jax.experimental import pallas as pl
from jax.experimental.pallas import tpu as pltpu
from jax.sharding import Mesh, PartitionSpec as P

norm_eps = 1e-05
low_rank_scale = 2.0
CHUNKS = 2
TAIL = 128
SWAP = [(0, 1), (1, 0)]
ODD = [(s, s - 1) for s in range(15, 0, -2)]
EVEN = [(s, s - 1) for s in range(14, 0, -2)]
EVERY = [(s, s - 1) for s in range(15, 0, -1)]
f32 = jnp.float32
bf16 = jnp.bfloat16
contract_last = (((1,), (1,)), ((), ()))
contract_inner = (((1,), (0,)), ((), ()))
AHEAD = 3
TOP_SWAP = [(30, 31), (31, 30)]
RIGHT = [(4 * s + z, 4 * s + (z + 1) % 4) for s in range(15) for z in range(4)]
LEFT = [(4 * s + z, 4 * s + (z + 3) % 4) for s in range(15) for z in range(4)]
PAIRS = [(2 * s + c, 2 * s + 1 - c) for s in range(15) for c in range(2)]


def both_cores(value, axis):
    core = lax.axis_index("c")
    other = lax.ppermute(value, "c", SWAP)
    low = jnp.where(core == 0, value, other)
    high = jnp.where(core == 0, other, value)
    return jnp.concatenate([low, high], axis)


def half_sum(value, axis):
    core = lax.axis_index("c")
    width = value.shape[axis] // 2
    low = lax.slice_in_dim(value, 0, width, axis=axis)
    high = lax.slice_in_dim(value, width, 2 * width, axis=axis)
    mine = jnp.where(core == 0, low, high)
    theirs = jnp.where(core == 0, high, low)
    return mine + lax.ppermute(theirs, "c", SWAP)


def spread(value):
    sent = jnp.broadcast_to(value[None], (4,) + value.shape)
    return lax.all_to_all(sent, "y", 0, 0)


def own_group(low, group):
    rows, cols = low.shape
    row_group = lax.broadcasted_iota(jnp.int32, low.shape, 0) // (rows // group)
    col_group = lax.broadcasted_iota(jnp.int32, low.shape, 1) // (cols // group)
    return jnp.where(row_group == col_group, low, 0.0).astype(bf16)


def message(total, grad_y, gain, inv, x, width_all):
    rows, width = total.shape
    normed_grad = (total * gain).astype(bf16).astype(f32)
    sent = (grad_y.astype(f32) + inv * normed_grad).astype(bf16)
    coef = jnp.sum(normed_grad * x.astype(f32), axis=1, keepdims=True)
    coef = coef * (inv * inv * inv / width_all)
    lane = lax.broadcasted_iota(jnp.int32, (rows, TAIL), 1)
    high = lax.reduce_precision(coef, 8, 7)
    tail = jnp.where(lane == 0, high, jnp.where(lane == 1, coef - high, 0.0)).astype(bf16)
    return sent, tail


def stage_kernel(place_ref, parts_ref, gain_ref, before_any, up_any, down_any, inv_any, x_any, *refs, group):
    weights, refs = refs[:16], refs[16 + 4 :]
    box_ref, boxes_any, low_any, grad_any, tail_any = refs[:5]
    before_ref, up_ref, down_ref, inv_ref, x_ref, full, weight, low_ref, grad_ref, tail_ref = refs[5:15]
    in_sems, w_sems, out_sems = refs[15:]
    m, ypos, core, zpos = place_ref[0], place_ref[1], place_ref[2], place_ref[3]
    width = x_ref.shape[1]
    width_all = full.shape[1]
    half = width // 2

    def started(source, target, sem):
        copy = pltpu.make_async_copy(source, target, sem)
        copy.start()
        return copy

    before_copy = started(before_any.at[:, m], before_ref, in_sems.at[0])
    up_copy = started(up_any.at[m], up_ref, in_sems.at[1])
    copies = []
    for piece in range(8):
        for side, base in enumerate((core * half, (1 - core) * half)):
            lanes = pl.ds(pl.multiple_of(base, 128), half)
            target = weight.at[pl.ds(piece * half, half), lanes]
            copies.append(started(weights[8 * side + piece], target, w_sems.at[piece, side]))
        if piece == 0:
            down_copy = started(down_any.at[m], down_ref, in_sems.at[2])
            inv_copy = started(inv_any.at[m], inv_ref, in_sems.at[3])
            x_copy = started(x_any.at[m], x_ref, in_sems.at[4])

    tail = parts_ref[:, :, width:].astype(f32)
    coef = jnp.sum(jnp.sum(tail, axis=0), axis=1, keepdims=True)
    before_copy.wait()
    up_copy.wait()
    low = None
    for part in range(4):
        fixed = parts_ref[part, :, :width].astype(f32) - coef * before_ref[part].astype(f32)
        fixed = fixed.astype(bf16)
        first = 2 * lax.rem(zpos - part + 4, 4) * half
        second = (2 * lax.rem(part - zpos + 4, 4) + 1) * half
        full[:, pl.ds(pl.multiple_of(first, 128), half)] = fixed[:, :half]
        full[:, pl.ds(pl.multiple_of(second, 128), half)] = fixed[:, half:]

        @pl.when(part == ypos)
        def _(fixed=fixed):
            grad_ref[...] = fixed

        term = lax.dot_general(
            fixed,
            up_ref[:, part * width : (part + 1) * width],
            contract_last,
            preferred_element_type=f32,
        )
        low = term if low is None else low + term
    grad_copy = started(grad_ref, grad_any.at[m], out_sems.at[0])
    low = own_group(low, group)
    low_ref[...] = low
    low_copy = started(low_ref, low_any.at[m], out_sems.at[1])
    down_copy.wait()
    total = low_rank_scale * lax.dot_general(
        low, down_ref[...], contract_inner, preferred_element_type=f32
    )
    for part in range(4):
        for copy in copies[4 * part : 4 * part + 4]:
            copy.wait()
        span = slice(part * width, (part + 1) * width)
        total = total + lax.dot_general(
            full[:, span], weight[span], contract_inner, preferred_element_type=f32
        )
    inv_copy.wait()
    x_copy.wait()
    sent, tail = message(
        total, grad_ref[...], gain_ref[...], inv_ref[:, 0:1], x_ref[...], width_all
    )
    box_ref[:, :width] = sent
    box_ref[:, width:] = tail
    tail_ref[...] = tail
    box_copy = started(box_ref, boxes_any.at[m], out_sems.at[2])
    tail_copy = started(tail_ref, tail_any.at[m], out_sems.at[3])
    grad_copy.wait()
    low_copy.wait()
    box_copy.wait()
    tail_copy.wait()


def run_stage(place, parts, before, up, down, gain, inv, x, weights, kept):
    _, rows, width = x.shape
    width_all = 4 * width
    cols = up.shape[1]
    vmem = pl.BlockSpec(memory_space=pltpu.VMEM)
    any_space = pl.BlockSpec(memory_space=pl.ANY)
    inputs = [place, parts, gain, before, up, down, inv, x, *weights]
    return pl.pallas_call(
        functools.partial(stage_kernel, group=cols // 16),
        in_specs=[pl.BlockSpec(memory_space=pltpu.SMEM), vmem, vmem]
        + [any_space] * (len(inputs) + len(kept) - 3),
        out_specs=[vmem] + [any_space] * len(kept),
        scratch_shapes=[
            pltpu.VMEM((4, rows, width), bf16),
            pltpu.VMEM((cols, width_all), bf16),
            pltpu.VMEM((cols, width), bf16),
            pltpu.VMEM((rows, TAIL), f32),
            pltpu.VMEM((rows, width), bf16),
            pltpu.VMEM((rows, width_all), bf16),
            pltpu.VMEM((width_all, width), bf16),
            pltpu.VMEM((rows, cols), bf16),
            pltpu.VMEM((rows, width), bf16),
            pltpu.VMEM((rows, TAIL), bf16),
            pltpu.SemaphoreType.DMA((5,)),
            pltpu.SemaphoreType.DMA((8, 2)),
            pltpu.SemaphoreType.DMA((4,)),
        ],
        out_shape=[jax.ShapeDtypeStruct((rows, width + TAIL), bf16)]
        + [jax.ShapeDtypeStruct(k.shape, k.dtype) for k in kept],
        input_output_aliases={len(inputs) + i: 1 + i for i in range(len(kept))},
        compiler_params=pltpu.CompilerParams(vmem_limit_bytes=32 * 1024 * 1024),
        cost_estimate=pl.CostEstimate(
            flops=2 * rows * width * width_all, bytes_accessed=2 * width * width_all, transcendentals=0
        ),
        name="stage",
    )(*inputs, *kept)


def local(
    section_inputs,
    out_grads,
    proj_weight,
    norm_gain,
    adapter_down,
    adapter_up,
    tenant_ids,
    slot_table,
):
    sec = lax.axis_index("s")
    ypos = lax.axis_index("y")
    core = lax.axis_index("c")
    micro = section_inputs.shape[1]
    width_all = section_inputs.shape[3]
    half = proj_weight.shape[1]
    width = 2 * half
    toks = section_inputs.shape[2] // 2
    rank = adapter_down.shape[3]
    rows_all = micro * toks
    group = micro // CHUNKS
    rows = group * toks
    multiplier = low_rank_scale / (toks * 2 * lax.axis_size("z"))

    zpos = lax.axis_index("z")
    first = proj_weight[0][:, :half].T
    second = proj_weight[0][:, half:].T

    x_tokens = lax.dynamic_slice_in_dim(section_inputs[0], core * toks, toks, 1)
    x_y = lax.dynamic_slice_in_dim(x_tokens, ypos * width, width, 2).reshape(rows_all, width)
    x_moved = lax.ppermute(x_y, "s", EVERY)
    x_moved, first, second, norm_gain, adapter_down, x_tokens = lax.optimization_barrier(
        (x_moved, first, second, norm_gain, adapter_down, x_tokens)
    )
    right_1 = lax.ppermute(first, ("s", "z"), RIGHT)
    left_1 = lax.ppermute(second, ("s", "z"), LEFT)

    x_f = x_tokens.reshape(rows_all, width_all).astype(f32)
    inv_rms = lax.rsqrt(jnp.mean(x_f * x_f, axis=-1, keepdims=True) + norm_eps)
    normed_y = x_y.astype(f32) * inv_rms
    x_before = lax.cond(
        sec == 15, lambda x: jnp.zeros((4,) + x.shape, x.dtype), spread, x_moved
    )
    gain_y = both_cores(norm_gain, 1)
    down_y = both_cores(adapter_down[0], 1)
    h_y = (normed_y * gain_y).astype(bf16)

    iota = jnp.arange(micro, dtype=jnp.int32)
    tenant_hot = tenant_ids[:, None] == iota[None, :]
    slot_ids = jnp.sum(jnp.where(tenant_hot, slot_table[0][None, :], 0), axis=1)
    down_sel = down_y[slot_ids]
    up_sel = adapter_up[0][slot_ids]
    low_part = jnp.einsum(
        "mtd,mdr->mtr", h_y.reshape(micro, toks, width), down_sel, preferred_element_type=f32
    )

    def extra(args):
        h_y, low_part = args
        low_in = lax.psum(low_part, "y").astype(bf16)
        return lax.all_gather(h_y, "z"), lax.all_gather(low_in, "z")

    x_before = x_before.reshape(4, CHUNKS, rows, width)
    x_chunk = x_y.reshape(CHUNKS, rows, width)
    inv_chunk = jnp.broadcast_to(inv_rms.reshape(CHUNKS, rows, 1), (CHUNKS, rows, TAIL))
    down_chunk = down_sel.transpose(0, 2, 1).reshape(CHUNKS, group * rank, width)
    up_chunk = up_sel.reshape(CHUNKS, group * rank, width_all)

    ready = (x_before, x_chunk, inv_chunk, down_chunk, up_chunk, gain_y)
    right_1, left_1, ready = lax.optimization_barrier((right_1, left_1, ready))
    x_before, x_chunk, inv_chunk, down_chunk, up_chunk, gain_y = ready

    def top(args):
        out_grads, first, second = args[:3]
        shard = jnp.concatenate([first, second], 0)
        shard_x = lax.ppermute(shard, ("s", "c"), TOP_SWAP)
        grad = lax.dynamic_slice_in_dim(out_grads, core * toks, toks, 1)
        low = jnp.einsum("mtd,mrd->mtr", grad, up_sel, preferred_element_type=f32).astype(bf16)
        adapt = jnp.einsum("mtr,mdr->mtd", low, down_sel, preferred_element_type=f32)
        grad = grad.reshape(rows_all, width_all)
        blocks = jnp.stack([grad[:, i * width : (i + 1) * width] for i in range(4)])
        blocks = lax.all_to_all(blocks, "z", 0, 0).reshape(4 * rows_all, width)
        mine, theirs = (
            lax.dot_general(blocks, w, contract_inner, preferred_element_type=f32).astype(bf16)
            for w in (shard, shard_x)
        )
        terms = jnp.concatenate(
            [jnp.where(core == 0, mine, theirs), jnp.where(core == 0, theirs, mine)], 1
        )
        terms = lax.all_to_all(terms.reshape(4, rows_all, width), "z", 0, 0)
        total = jnp.sum(terms.astype(f32), axis=0)
        total = total + low_rank_scale * adapt.reshape(rows_all, width)
        grad_y = lax.dynamic_slice_in_dim(grad, ypos * width, width, 1)
        sent, tail = message(total, grad_y, gain_y, inv_rms, x_y, width_all)
        boxes = jnp.concatenate([sent, tail], 1).reshape(CHUNKS, rows, width + TAIL)
        member = jnp.arange(rows_all)[:, None] // toks % group == jnp.arange(group)[None, :]
        low = jnp.where(member[:, :, None], low.reshape(rows_all, 1, rank), 0)
        low = low.astype(bf16).reshape(CHUNKS, rows, group * rank)
        tail = tail.reshape(CHUNKS, rows, TAIL)
        moved = tuple(jnp.zeros(first.shape, first.dtype) for _ in range(12))
        return moved, (boxes, low, grad_y.reshape(CHUNKS, rows, width), tail)

    def around(args):
        _, first, second, right_1, left_1 = args

        def swapped(value):
            return lax.ppermute(value, ("s", "c"), PAIRS)

        right_2 = lax.ppermute(right_1, ("s", "z"), RIGHT)
        left_2 = lax.ppermute(left_1, ("s", "z"), LEFT)
        others = [swapped(w) for w in (first, second, right_1, left_1)]
        right_2, left_2, others = lax.optimization_barrier((right_2, left_2, others))
        right_3 = lax.ppermute(right_2, ("s", "z"), RIGHT)
        left_3 = lax.ppermute(left_2, ("s", "z"), LEFT)
        more = [swapped(w) for w in (right_2, left_2)]
        right_3, left_3, more = lax.optimization_barrier((right_3, left_3, more))
        more = more + [swapped(w) for w in (right_3, left_3)]
        kept = (
            jnp.zeros((CHUNKS, rows, width + TAIL), bf16),
            jnp.zeros((CHUNKS, rows, group * rank), bf16),
            jnp.zeros((CHUNKS, rows, width), bf16),
            jnp.zeros((CHUNKS, rows, TAIL), bf16),
        )
        return (right_2, left_2, right_3, left_3, *others, *more), kept

    args = (out_grads, first, second, right_1, left_1)
    moved, kept = lax.cond(sec == 15, top, around, args)
    weights = [first, second, right_1, left_1, *moved]

    def pick(array, m):
        return lax.dynamic_index_in_dim(array, m, 0, keepdims=False)

    def step(u, state):
        box, kept, extras = state
        t, m = u // CHUNKS, u % CHUNKS
        turn = 15 - t + m

        def stored(args):
            _, kept = args
            return pick(kept[0], m), kept

        def computed(args):
            box, kept = args
            place = jnp.stack([m, ypos, core, zpos]).astype(jnp.int32)
            parts = lax.cond(
                sec == 15, lambda box: jnp.zeros((4,) + box.shape, box.dtype), spread, box
            )
            box, *kept = run_stage(
                place,
                parts,
                x_before,
                up_chunk,
                down_chunk,
                gain_y,
                inv_chunk,
                x_chunk,
                weights,
                kept,
            )
            return box, tuple(kept)

        kind = jnp.where(sec == turn, jnp.where(sec == 15, 1, 2), 0)
        box, kept = lax.switch(kind, [lambda args: args, stored, computed], (box, kept))
        part = ((sec == turn) | (sec == turn - 1)) & (turn >= 1) & (turn <= 15)
        kind = jnp.where(part, jnp.where(turn % 2 == 1, 1, 2), 0)
        box = lax.switch(
            kind,
            [
                lambda box: box,
                lambda box: lax.ppermute(box, "s", ODD),
                lambda box: lax.ppermute(box, "s", EVEN),
            ],
            box,
        )
        extras = lax.cond(
            (sec == turn - AHEAD) & (m == 0),
            lambda args: extra((h_y, low_part)),
            lambda args: args,
            extras,
        )
        return box, kept, extras

    start = (
        jnp.zeros((rows, width + TAIL), bf16),
        kept,
        (
            jnp.zeros((4, rows_all, width), bf16),
            jnp.zeros((4, micro, toks, rank), bf16),
        ),
    )
    _, kept, extras = lax.fori_loop(0, (15 + CHUNKS) * CHUNKS, step, start)
    boxes, low_all, grad_all, tail_all = kept
    h_all, low_in_all = lax.cond(
        sec > 15 - AHEAD, lambda args: extra((h_y, low_part)), lambda args: args, extras
    )

    coefs = spread(tail_all)
    coef_sum = jnp.sum(coefs.astype(f32), axis=(0, -1))[..., None]
    new_grads = boxes[:, :, :width].astype(f32) - coef_sum * x_chunk.astype(f32)
    new_grads = new_grads.astype(bf16).reshape(micro, toks, width)
    keep = jnp.where(core == 0, new_grads[:, :, :half], new_grads[:, :, half:])
    give = jnp.where(core == 0, new_grads[:, :, half:], new_grads[:, :, :half])
    got = lax.ppermute(give, "c", SWAP)
    kept = jnp.concatenate(
        [jnp.where(core == 0, keep, got), jnp.where(core == 0, got, keep)], 1
    )

    both = jnp.concatenate(
        [
            grad_all.reshape(rows_all, width),
            jnp.pad(low_all.reshape(rows_all, group * rank), ((0, 0), (0, TAIL - group * rank))),
        ],
        1,
    )
    both = lax.all_gather(both, "z").reshape(4, micro, toks, width + TAIL)
    grads_z = both[..., :width]
    low_z = both[..., width : width + group * rank].reshape(4, micro, toks, group, rank)
    low_z = jnp.sum(low_z.astype(f32), axis=3).astype(bf16)
    hidden_z = h_all.reshape(4, micro, toks, width)
    down_part = multiplier * jnp.einsum(
        "zmtd,zmtr->mdr", hidden_z, low_z, preferred_element_type=f32
    )
    up_part = multiplier * jnp.einsum(
        "zmtr,zmtd->mrd", low_in_all, grads_z, preferred_element_type=f32
    )
    down_acc = half_sum(down_part, 1)
    up_acc = half_sum(up_part, 2)
    slot_hot = slot_ids[None, :] == iota[:, None]
    down_out = jnp.sum(jnp.where(slot_hot[:, :, None, None], down_acc[None], 0.0), axis=1)
    up_out = jnp.sum(jnp.where(slot_hot[:, :, None, None], up_acc[None], 0.0), axis=1)
    return (kept[None], down_out[None], up_out[None])


def solution(mesh):
    fine = Mesh(mesh.devices.reshape(16, 4, 2, 4), ("s", "y", "c", "z"))
    mp = ("y", "c")
    placed = (
        P("s", None, "z", None),
        P(None, "z", None),
        P("s", mp, "z"),
        P("s", mp),
        P("s", None, mp, None),
        P("s", None, None, None),
        P(),
        P("s", None),
    )
    return jax.shard_map(
        local,
        mesh=fine,
        in_specs=placed,
        out_specs=(
            P("s", None, "z", mp),
            P("s", None, mp, None),
            P("s", None, None, mp),
        ),
        check_vma=False,
    )
```

```python
import functools

import jax
import jax.numpy as jnp
from jax import lax
from jax.experimental import pallas as pl
from jax.experimental.pallas import tpu as pltpu
from jax.sharding import Mesh, PartitionSpec as P

norm_eps = 1e-05
low_rank_scale = 2.0
CHUNKS = 2
TAIL = 128
SWAP = [(0, 1), (1, 0)]
ODD = [(s, s - 1) for s in range(15, 0, -2)]
EVEN = [(s, s - 1) for s in range(14, 0, -2)]
EVERY = [(s, s - 1) for s in range(15, 0, -1)]
f32 = jnp.float32
bf16 = jnp.bfloat16
contract_last = (((1,), (1,)), ((), ()))
contract_inner = (((1,), (0,)), ((), ()))
AHEAD = 3
TOP_SWAP = [(30, 31), (31, 30)]
RIGHT = [(4 * s + z, 4 * s + (z + 1) % 4) for s in range(15) for z in range(4)]
LEFT = [(4 * s + z, 4 * s + (z + 3) % 4) for s in range(15) for z in range(4)]
PAIRS = [(2 * s + c, 2 * s + 1 - c) for s in range(15) for c in range(2)]


def both_cores(value, axis):
    core = lax.axis_index("c")
    other = lax.ppermute(value, "c", SWAP)
    low = jnp.where(core == 0, value, other)
    high = jnp.where(core == 0, other, value)
    return jnp.concatenate([low, high], axis)


def half_sum(value, axis):
    core = lax.axis_index("c")
    width = value.shape[axis] // 2
    low = lax.slice_in_dim(value, 0, width, axis=axis)
    high = lax.slice_in_dim(value, width, 2 * width, axis=axis)
    mine = jnp.where(core == 0, low, high)
    theirs = jnp.where(core == 0, high, low)
    return mine + lax.ppermute(theirs, "c", SWAP)


def spread(value):
    sent = jnp.broadcast_to(value[None], (4,) + value.shape)
    return lax.all_to_all(sent, "y", 0, 0)


def own_group(low, group):
    rows, cols = low.shape
    row_group = lax.broadcasted_iota(jnp.int32, low.shape, 0) // (rows // group)
    col_group = lax.broadcasted_iota(jnp.int32, low.shape, 1) // (cols // group)
    return jnp.where(row_group == col_group, low, 0.0).astype(bf16)


def message(total, grad_y, gain, inv, x, width_all):
    rows, width = total.shape
    normed_grad = (total * gain).astype(bf16).astype(f32)
    sent = (grad_y.astype(f32) + inv * normed_grad).astype(bf16)
    coef = jnp.sum(normed_grad * x.astype(f32), axis=1, keepdims=True)
    coef = coef * (inv * inv * inv / width_all)
    lane = lax.broadcasted_iota(jnp.int32, (rows, TAIL), 1)
    high = lax.reduce_precision(coef, 8, 7)
    tail = jnp.where(lane == 0, high, jnp.where(lane == 1, coef - high, 0.0)).astype(bf16)
    return sent, tail


def stage_kernel(place_ref, parts_ref, gain_ref, before_any, up_any, down_any, inv_any, x_any, *refs, group):
    weights, refs = refs[:16], refs[16 + 4 :]
    box_ref, boxes_any, low_any, grad_any, tail_any = refs[:5]
    before_ref, up_ref, down_ref, inv_ref, x_ref, full, weight, low_ref, grad_ref, tail_ref = refs[5:15]
    in_sems, w_sems, out_sems = refs[15:]
    m, ypos, core, zpos = place_ref[0], place_ref[1], place_ref[2], place_ref[3]
    width = x_ref.shape[1]
    width_all = full.shape[1]
    half = width // 2

    def started(source, target, sem):
        copy = pltpu.make_async_copy(source, target, sem)
        copy.start()
        return copy

    before_copy = started(before_any.at[:, m], before_ref, in_sems.at[0])
    up_copy = started(up_any.at[m], up_ref, in_sems.at[1])
    copies = []
    for piece in range(8):
        for side, base in enumerate((core * half, (1 - core) * half)):
            lanes = pl.ds(pl.multiple_of(base, 128), half)
            target = weight.at[pl.ds(piece * half, half), lanes]
            copies.append(started(weights[8 * side + piece], target, w_sems.at[piece, side]))
        if piece == 0:
            down_copy = started(down_any.at[m], down_ref, in_sems.at[2])
            inv_copy = started(inv_any.at[m], inv_ref, in_sems.at[3])
            x_copy = started(x_any.at[m], x_ref, in_sems.at[4])

    tail = parts_ref[:, :, width:].astype(f32)
    coef = jnp.sum(jnp.sum(tail, axis=0), axis=1, keepdims=True)
    before_copy.wait()
    up_copy.wait()
    low = None
    for part in range(4):
        fixed = parts_ref[part, :, :width].astype(f32) - coef * before_ref[part].astype(f32)
        fixed = fixed.astype(bf16)
        first = 2 * lax.rem(zpos - part + 4, 4) * half
        second = (2 * lax.rem(part - zpos + 4, 4) + 1) * half
        full[:, pl.ds(pl.multiple_of(first, 128), half)] = fixed[:, :half]
        full[:, pl.ds(pl.multiple_of(second, 128), half)] = fixed[:, half:]

        @pl.when(part == ypos)
        def _(fixed=fixed):
            grad_ref[...] = fixed

        term = lax.dot_general(
            fixed,
            up_ref[:, part * width : (part + 1) * width],
            contract_last,
            preferred_element_type=f32,
        )
        low = term if low is None else low + term
    grad_copy = started(grad_ref, grad_any.at[m], out_sems.at[0])
    low = own_group(low, group)
    low_ref[...] = low
    low_copy = started(low_ref, low_any.at[m], out_sems.at[1])
    down_copy.wait()
    total = low_rank_scale * lax.dot_general(
        low, down_ref[...], contract_inner, preferred_element_type=f32
    )
    for part in range(4):
        for copy in copies[4 * part : 4 * part + 4]:
            copy.wait()
        span = slice(part * width, (part + 1) * width)
        total = total + lax.dot_general(
            full[:, span], weight[span], contract_inner, preferred_element_type=f32
        )
    inv_copy.wait()
    x_copy.wait()
    sent, tail = message(
        total, grad_ref[...], gain_ref[...], inv_ref[:, 0:1], x_ref[...], width_all
    )
    box_ref[:, :width] = sent
    box_ref[:, width:] = tail
    tail_ref[...] = tail
    box_copy = started(box_ref, boxes_any.at[m], out_sems.at[2])
    tail_copy = started(tail_ref, tail_any.at[m], out_sems.at[3])
    grad_copy.wait()
    low_copy.wait()
    box_copy.wait()
    tail_copy.wait()


def run_stage(place, parts, before, up, down, gain, inv, x, weights, kept):
    _, rows, width = x.shape
    width_all = 4 * width
    cols = up.shape[1]
    vmem = pl.BlockSpec(memory_space=pltpu.VMEM)
    any_space = pl.BlockSpec(memory_space=pl.ANY)
    inputs = [place, parts, gain, before, up, down, inv, x, *weights]
    return pl.pallas_call(
        functools.partial(stage_kernel, group=cols // 16),
        in_specs=[pl.BlockSpec(memory_space=pltpu.SMEM), vmem, vmem]
        + [any_space] * (len(inputs) + len(kept) - 3),
        out_specs=[vmem] + [any_space] * len(kept),
        scratch_shapes=[
            pltpu.VMEM((4, rows, width), bf16),
            pltpu.VMEM((cols, width_all), bf16),
            pltpu.VMEM((cols, width), bf16),
            pltpu.VMEM((rows, TAIL), f32),
            pltpu.VMEM((rows, width), bf16),
            pltpu.VMEM((rows, width_all), bf16),
            pltpu.VMEM((width_all, width), bf16),
            pltpu.VMEM((rows, cols), bf16),
            pltpu.VMEM((rows, width), bf16),
            pltpu.VMEM((rows, TAIL), bf16),
            pltpu.SemaphoreType.DMA((5,)),
            pltpu.SemaphoreType.DMA((8, 2)),
            pltpu.SemaphoreType.DMA((4,)),
        ],
        out_shape=[jax.ShapeDtypeStruct((rows, width + TAIL), bf16)]
        + [jax.ShapeDtypeStruct(k.shape, k.dtype) for k in kept],
        input_output_aliases={len(inputs) + i: 1 + i for i in range(len(kept))},
        compiler_params=pltpu.CompilerParams(vmem_limit_bytes=32 * 1024 * 1024),
        cost_estimate=pl.CostEstimate(
            flops=2 * rows * width * width_all, bytes_accessed=2 * width * width_all, transcendentals=0
        ),
        name="stage",
    )(*inputs, *kept)


def local(
    section_inputs,
    out_grads,
    proj_weight,
    norm_gain,
    adapter_down,
    adapter_up,
    tenant_ids,
    slot_table,
):
    sec = lax.axis_index("s")
    ypos = lax.axis_index("y")
    core = lax.axis_index("c")
    micro = section_inputs.shape[1]
    width_all = section_inputs.shape[3]
    half = proj_weight.shape[1]
    width = 2 * half
    toks = section_inputs.shape[2] // 2
    rank = adapter_down.shape[3]
    rows_all = micro * toks
    group = micro // CHUNKS
    rows = group * toks
    multiplier = low_rank_scale / (toks * 2 * lax.axis_size("z"))

    zpos = lax.axis_index("z")
    first = proj_weight[0][:, :half].T
    second = proj_weight[0][:, half:].T

    x_tokens = lax.dynamic_slice_in_dim(section_inputs[0], core * toks, toks, 1)
    x_y = lax.dynamic_slice_in_dim(x_tokens, ypos * width, width, 2).reshape(rows_all, width)
    x_moved = lax.ppermute(x_y, "s", EVERY)
    first, second, norm_gain, adapter_down = lax.optimization_barrier(
        (first, second, norm_gain, adapter_down)
    )
    gain_y = both_cores(norm_gain, 1)
    down_y = both_cores(adapter_down[0], 1)
    empty = (
        jnp.zeros((CHUNKS, rows, width + TAIL), bf16),
        jnp.zeros((CHUNKS, rows, group * rank), bf16),
        jnp.zeros((CHUNKS, rows, width), bf16),
        jnp.zeros((CHUNKS, rows, TAIL), bf16),
    )
    idle = (
        jnp.zeros((rows, width + TAIL), bf16),
        jnp.zeros((4, rows_all, width), bf16),
        jnp.zeros((4, micro, toks, rank), bf16),
    )
    x_moved, first, second, gain_y, down_y, x_tokens, empty, idle = lax.optimization_barrier(
        (x_moved, first, second, gain_y, down_y, x_tokens, empty, idle)
    )
    right_1 = lax.ppermute(first, ("s", "z"), RIGHT)
    left_1 = lax.ppermute(second, ("s", "z"), LEFT)

    x_f = x_tokens.reshape(rows_all, width_all).astype(f32)
    inv_rms = lax.rsqrt(jnp.mean(x_f * x_f, axis=-1, keepdims=True) + norm_eps)
    normed_y = x_y.astype(f32) * inv_rms
    x_before = lax.cond(
        sec == 15, lambda x: jnp.zeros((4,) + x.shape, x.dtype), spread, x_moved
    )
    h_y = (normed_y * gain_y).astype(bf16)

    iota = jnp.arange(micro, dtype=jnp.int32)
    tenant_hot = tenant_ids[:, None] == iota[None, :]
    slot_ids = jnp.sum(jnp.where(tenant_hot, slot_table[0][None, :], 0), axis=1)
    down_sel = down_y[slot_ids]
    up_sel = adapter_up[0][slot_ids]
    low_part = jnp.einsum(
        "mtd,mdr->mtr", h_y.reshape(micro, toks, width), down_sel, preferred_element_type=f32
    )

    def extra(args):
        h_y, low_part = args
        low_in = lax.psum(low_part, "y").astype(bf16)
        return lax.all_gather(h_y, "z"), lax.all_gather(low_in, "z")

    x_before = x_before.reshape(4, CHUNKS, rows, width)
    x_chunk = x_y.reshape(CHUNKS, rows, width)
    inv_chunk = jnp.broadcast_to(inv_rms.reshape(CHUNKS, rows, 1), (CHUNKS, rows, TAIL))
    down_chunk = down_sel.transpose(0, 2, 1).reshape(CHUNKS, group * rank, width)
    up_chunk = up_sel.reshape(CHUNKS, group * rank, width_all)

    def top(args):
        out_grads, first, second, _ = args
        shard = jnp.concatenate([first, second], 0)
        shard_x = lax.ppermute(shard, ("s", "c"), TOP_SWAP)
        grad = lax.dynamic_slice_in_dim(out_grads, core * toks, toks, 1)
        low = jnp.einsum("mtd,mrd->mtr", grad, up_sel, preferred_element_type=f32).astype(bf16)
        adapt = jnp.einsum("mtr,mdr->mtd", low, down_sel, preferred_element_type=f32)
        grad = grad.reshape(rows_all, width_all)
        blocks = jnp.stack([grad[:, i * width : (i + 1) * width] for i in range(4)])
        blocks = lax.all_to_all(blocks, "z", 0, 0).reshape(4 * rows_all, width)
        mine, theirs = (
            lax.dot_general(blocks, w, contract_inner, preferred_element_type=f32).astype(bf16)
            for w in (shard, shard_x)
        )
        terms = jnp.concatenate(
            [jnp.where(core == 0, mine, theirs), jnp.where(core == 0, theirs, mine)], 1
        )
        terms = lax.all_to_all(terms.reshape(4, rows_all, width), "z", 0, 0)
        total = jnp.sum(terms.astype(f32), axis=0)
        total = total + low_rank_scale * adapt.reshape(rows_all, width)
        grad_y = lax.dynamic_slice_in_dim(grad, ypos * width, width, 1)
        sent, tail = message(total, grad_y, gain_y, inv_rms, x_y, width_all)
        boxes = jnp.concatenate([sent, tail], 1).reshape(CHUNKS, rows, width + TAIL)
        member = jnp.arange(rows_all)[:, None] // toks % group == jnp.arange(group)[None, :]
        low = jnp.where(member[:, :, None], low.reshape(rows_all, 1, rank), 0)
        low = low.astype(bf16).reshape(CHUNKS, rows, group * rank)
        tail = tail.reshape(CHUNKS, rows, TAIL)
        return boxes, low, grad_y.reshape(CHUNKS, rows, width), tail

    def swapped(value):
        return lax.ppermute(value, ("s", "c"), PAIRS)

    ready = (x_before, x_chunk, inv_chunk, down_chunk, up_chunk, gain_y)
    right_1, left_1, ready = lax.optimization_barrier((right_1, left_1, ready))
    kept = lax.cond(sec == 15, top, lambda args: args[3], (out_grads, first, second, empty))
    boxes_top = lax.ppermute(kept[0], "s", [(15, 14)])
    right_2 = lax.ppermute(right_1, ("s", "z"), RIGHT)
    left_2 = lax.ppermute(left_1, ("s", "z"), LEFT)
    others = [swapped(w) for w in (first, second, right_1, left_1)]
    right_2, left_2, others = lax.optimization_barrier((right_2, left_2, others))
    right_3 = lax.ppermute(right_2, ("s", "z"), RIGHT)
    left_3 = lax.ppermute(left_2, ("s", "z"), LEFT)
    more = [swapped(w) for w in (right_2, left_2)]
    right_3, left_3, more, kept, boxes_top, ready = lax.optimization_barrier(
        (right_3, left_3, more, kept, boxes_top, ready)
    )
    x_before, x_chunk, inv_chunk, down_chunk, up_chunk, gain_y = ready
    more = more + [swapped(w) for w in (right_3, left_3)]
    weights = [first, second, right_1, left_1, right_2, left_2, right_3, left_3, *others, *more]

    def pick(array, m):
        return lax.dynamic_index_in_dim(array, m, 0, keepdims=False)

    def step(u, state):
        box, kept, extras = state
        t, m = u // CHUNKS, u % CHUNKS
        turn = 15 - t + m

        def computed(args):
            box, kept = args
            place = jnp.stack([m, ypos, core, zpos]).astype(jnp.int32)
            parts = lax.cond(
                sec == 15, lambda box: jnp.zeros((4,) + box.shape, box.dtype), spread, box
            )
            box, *kept = run_stage(
                place,
                parts,
                x_before,
                up_chunk,
                down_chunk,
                gain_y,
                inv_chunk,
                x_chunk,
                weights,
                kept,
            )
            return box, tuple(kept)

        box, kept = lax.cond(
            (sec == turn) & (sec < 15), computed, lambda args: args, (box, kept)
        )
        part = ((sec == turn) | (sec == turn - 1)) & (turn >= 1) & (turn <= 14)
        kind = jnp.where(part, jnp.where(turn % 2 == 1, 1, 2), 0)
        kind = jnp.where((turn == 15) & (sec == 14), 3, kind)
        box = lax.switch(
            kind,
            [
                lambda box: box,
                lambda box: lax.ppermute(box, "s", ODD),
                lambda box: lax.ppermute(box, "s", EVEN),
                lambda box: pick(boxes_top, m),
            ],
            box,
        )
        extras = lax.cond(
            (sec == turn - AHEAD) & (m == 0),
            lambda args: extra((h_y, low_part)),
            lambda args: args,
            extras,
        )
        return box, kept, extras

    start = (idle[0], kept, idle[1:])
    _, kept, extras = lax.fori_loop(0, (15 + CHUNKS) * CHUNKS, step, start)
    boxes, low_all, grad_all, tail_all = kept
    h_all, low_in_all = lax.cond(
        sec > 15 - AHEAD, lambda args: extra((h_y, low_part)), lambda args: args, extras
    )

    coefs = spread(tail_all)
    coef_sum = jnp.sum(coefs.astype(f32), axis=(0, -1))[..., None]
    new_grads = boxes[:, :, :width].astype(f32) - coef_sum * x_chunk.astype(f32)
    new_grads = new_grads.astype(bf16).reshape(micro, toks, width)
    keep = jnp.where(core == 0, new_grads[:, :, :half], new_grads[:, :, half:])
    give = jnp.where(core == 0, new_grads[:, :, half:], new_grads[:, :, :half])
    got = lax.ppermute(give, "c", SWAP)
    kept = jnp.concatenate(
        [jnp.where(core == 0, keep, got), jnp.where(core == 0, got, keep)], 1
    )

    both = jnp.concatenate(
        [
            grad_all.reshape(rows_all, width),
            jnp.pad(low_all.reshape(rows_all, group * rank), ((0, 0), (0, TAIL - group * rank))),
        ],
        1,
    )
    both = lax.all_gather(both, "z").reshape(4, micro, toks, width + TAIL)
    grads_z = both[..., :width]
    low_z = both[..., width : width + group * rank].reshape(4, micro, toks, group, rank)
    low_z = jnp.sum(low_z.astype(f32), axis=3).astype(bf16)
    hidden_z = h_all.reshape(4, micro, toks, width)
    down_part = multiplier * jnp.einsum(
        "zmtd,zmtr->mdr", hidden_z, low_z, preferred_element_type=f32
    )
    up_part = multiplier * jnp.einsum(
        "zmtr,zmtd->mrd", low_in_all, grads_z, preferred_element_type=f32
    )
    down_acc = half_sum(down_part, 1)
    up_acc = half_sum(up_part, 2)
    slot_hot = slot_ids[None, :] == iota[:, None]
    down_out = jnp.sum(jnp.where(slot_hot[:, :, None, None], down_acc[None], 0.0), axis=1)
    up_out = jnp.sum(jnp.where(slot_hot[:, :, None, None], up_acc[None], 0.0), axis=1)
    return (kept[None], down_out[None], up_out[None])


def solution(mesh):
    fine = Mesh(mesh.devices.reshape(16, 4, 2, 4), ("s", "y", "c", "z"))
    mp = ("y", "c")
    placed = (
        P("s", None, "z", None),
        P(None, "z", None),
        P("s", mp, "z"),
        P("s", mp),
        P("s", None, mp, None),
        P("s", None, None, None),
        P(),
        P("s", None),
    )
    return jax.shard_map(
        local,
        mesh=fine,
        in_specs=placed,
        out_specs=(
            P("s", None, "z", mp),
            P("s", None, mp, None),
            P("s", None, None, mp),
        ),
        check_vma=False,
    )
```

```python
import functools

import jax
import jax.numpy as jnp
from jax import lax
from jax.experimental import pallas as pl
from jax.experimental.pallas import tpu as pltpu
from jax.sharding import Mesh, PartitionSpec as P

norm_eps = 1e-05
low_rank_scale = 2.0
CHUNKS = 2
TAIL = 128
SWAP = [(0, 1), (1, 0)]
ODD = [(s, s - 1) for s in range(15, 0, -2)]
EVEN = [(s, s - 1) for s in range(14, 0, -2)]
EVERY = [(s, s - 1) for s in range(15, 0, -1)]
f32 = jnp.float32
bf16 = jnp.bfloat16
contract_last = (((1,), (1,)), ((), ()))
contract_inner = (((1,), (0,)), ((), ()))
AHEAD = 3
TOP_SWAP = [(30, 31), (31, 30)]
RIGHT = [(4 * s + z, 4 * s + (z + 1) % 4) for s in range(15) for z in range(4)]
LEFT = [(4 * s + z, 4 * s + (z + 3) % 4) for s in range(15) for z in range(4)]
PAIRS = [(2 * s + c, 2 * s + 1 - c) for s in range(15) for c in range(2)]


def both_cores(value, axis):
    core = lax.axis_index("c")
    other = lax.ppermute(value, "c", SWAP)
    low = jnp.where(core == 0, value, other)
    high = jnp.where(core == 0, other, value)
    return jnp.concatenate([low, high], axis)


def half_sum(value, axis):
    core = lax.axis_index("c")
    width = value.shape[axis] // 2
    low = lax.slice_in_dim(value, 0, width, axis=axis)
    high = lax.slice_in_dim(value, width, 2 * width, axis=axis)
    mine = jnp.where(core == 0, low, high)
    theirs = jnp.where(core == 0, high, low)
    return mine + lax.ppermute(theirs, "c", SWAP)


def spread(value):
    sent = jnp.broadcast_to(value[None], (4,) + value.shape)
    return lax.all_to_all(sent, "y", 0, 0)


def own_group(low, group):
    rows, cols = low.shape
    row_group = lax.broadcasted_iota(jnp.int32, low.shape, 0) // (rows // group)
    col_group = lax.broadcasted_iota(jnp.int32, low.shape, 1) // (cols // group)
    return jnp.where(row_group == col_group, low, 0.0).astype(bf16)


def message(total, grad_y, gain, inv, x, width_all):
    rows, width = total.shape
    normed_grad = (total * gain).astype(bf16).astype(f32)
    sent = (grad_y.astype(f32) + inv * normed_grad).astype(bf16)
    coef = jnp.sum(normed_grad * x.astype(f32), axis=1, keepdims=True)
    coef = coef * (inv * inv * inv / width_all)
    lane = lax.broadcasted_iota(jnp.int32, (rows, TAIL), 1)
    high = lax.reduce_precision(coef, 8, 7)
    tail = jnp.where(lane == 0, high, jnp.where(lane == 1, coef - high, 0.0)).astype(bf16)
    return sent, tail


def stage_kernel(place_ref, parts_ref, gain_ref, before_any, up_any, down_any, inv_any, x_any, *refs, group):
    weights, refs = refs[:16], refs[16 + 4 :]
    box_ref, boxes_any, low_any, grad_any, tail_any = refs[:5]
    before_ref, up_ref, down_ref, inv_ref, x_ref, full, weight, low_ref, grad_ref, tail_ref = refs[5:15]
    in_sems, w_sems, out_sems = refs[15:]
    m, ypos, core, zpos = place_ref[0], place_ref[1], place_ref[2], place_ref[3]
    width = x_ref.shape[1]
    width_all = full.shape[1]
    half = width // 2

    def started(source, target, sem):
        copy = pltpu.make_async_copy(source, target, sem)
        copy.start()
        return copy

    before_copy = started(before_any.at[:, m], before_ref, in_sems.at[0])
    up_copy = started(up_any.at[m], up_ref, in_sems.at[1])
    copies = []
    for piece in range(8):
        for side, base in enumerate((core * half, (1 - core) * half)):
            lanes = pl.ds(pl.multiple_of(base, 128), half)
            target = weight.at[pl.ds(piece * half, half), lanes]
            copies.append(started(weights[8 * side + piece], target, w_sems.at[piece, side]))
        if piece == 0:
            down_copy = started(down_any.at[m], down_ref, in_sems.at[2])
            inv_copy = started(inv_any.at[m], inv_ref, in_sems.at[3])
            x_copy = started(x_any.at[m], x_ref, in_sems.at[4])

    tail = parts_ref[:, :, width:].astype(f32)
    coef = jnp.sum(jnp.sum(tail, axis=0), axis=1, keepdims=True)
    before_copy.wait()
    up_copy.wait()
    low = None
    for part in range(4):
        fixed = parts_ref[part, :, :width].astype(f32) - coef * before_ref[part].astype(f32)
        fixed = fixed.astype(bf16)
        first = 2 * lax.rem(zpos - part + 4, 4) * half
        second = (2 * lax.rem(part - zpos + 4, 4) + 1) * half
        full[:, pl.ds(pl.multiple_of(first, 128), half)] = fixed[:, :half]
        full[:, pl.ds(pl.multiple_of(second, 128), half)] = fixed[:, half:]

        @pl.when(part == ypos)
        def _(fixed=fixed):
            grad_ref[...] = fixed

        term = lax.dot_general(
            fixed,
            up_ref[:, part * width : (part + 1) * width],
            contract_last,
            preferred_element_type=f32,
        )
        low = term if low is None else low + term
    grad_copy = started(grad_ref, grad_any.at[m], out_sems.at[0])
    low = own_group(low, group)
    low_ref[...] = low
    low_copy = started(low_ref, low_any.at[m], out_sems.at[1])
    down_copy.wait()
    total = low_rank_scale * lax.dot_general(
        low, down_ref[...], contract_inner, preferred_element_type=f32
    )
    for part in range(4):
        for copy in copies[4 * part : 4 * part + 4]:
            copy.wait()
        span = slice(part * width, (part + 1) * width)
        total = total + lax.dot_general(
            full[:, span], weight[span], contract_inner, preferred_element_type=f32
        )
    inv_copy.wait()
    x_copy.wait()
    sent, tail = message(
        total, grad_ref[...], gain_ref[...], inv_ref[:, 0:1], x_ref[...], width_all
    )
    box_ref[:, :width] = sent
    box_ref[:, width:] = tail
    tail_ref[...] = tail
    box_copy = started(box_ref, boxes_any.at[m], out_sems.at[2])
    tail_copy = started(tail_ref, tail_any.at[m], out_sems.at[3])
    grad_copy.wait()
    low_copy.wait()
    box_copy.wait()
    tail_copy.wait()


def run_stage(place, parts, before, up, down, gain, inv, x, weights, kept):
    _, rows, width = x.shape
    width_all = 4 * width
    cols = up.shape[1]
    vmem = pl.BlockSpec(memory_space=pltpu.VMEM)
    any_space = pl.BlockSpec(memory_space=pl.ANY)
    inputs = [place, parts, gain, before, up, down, inv, x, *weights]
    return pl.pallas_call(
        functools.partial(stage_kernel, group=cols // 16),
        in_specs=[pl.BlockSpec(memory_space=pltpu.SMEM), vmem, vmem]
        + [any_space] * (len(inputs) + len(kept) - 3),
        out_specs=[vmem] + [any_space] * len(kept),
        scratch_shapes=[
            pltpu.VMEM((4, rows, width), bf16),
            pltpu.VMEM((cols, width_all), bf16),
            pltpu.VMEM((cols, width), bf16),
            pltpu.VMEM((rows, TAIL), f32),
            pltpu.VMEM((rows, width), bf16),
            pltpu.VMEM((rows, width_all), bf16),
            pltpu.VMEM((width_all, width), bf16),
            pltpu.VMEM((rows, cols), bf16),
            pltpu.VMEM((rows, width), bf16),
            pltpu.VMEM((rows, TAIL), bf16),
            pltpu.SemaphoreType.DMA((5,)),
            pltpu.SemaphoreType.DMA((8, 2)),
            pltpu.SemaphoreType.DMA((4,)),
        ],
        out_shape=[jax.ShapeDtypeStruct((rows, width + TAIL), bf16)]
        + [jax.ShapeDtypeStruct(k.shape, k.dtype) for k in kept],
        input_output_aliases={len(inputs) + i: 1 + i for i in range(len(kept))},
        compiler_params=pltpu.CompilerParams(vmem_limit_bytes=32 * 1024 * 1024),
        cost_estimate=pl.CostEstimate(
            flops=2 * rows * width * width_all, bytes_accessed=2 * width * width_all, transcendentals=0
        ),
        name="stage",
    )(*inputs, *kept)


def local(
    section_inputs,
    out_grads,
    proj_weight,
    norm_gain,
    adapter_down,
    adapter_up,
    tenant_ids,
    slot_table,
):
    sec = lax.axis_index("s")
    ypos = lax.axis_index("y")
    core = lax.axis_index("c")
    micro = section_inputs.shape[1]
    width_all = section_inputs.shape[3]
    half = proj_weight.shape[1]
    width = 2 * half
    toks = section_inputs.shape[2] // 2
    rank = adapter_down.shape[3]
    rows_all = micro * toks
    group = micro // CHUNKS
    rows = group * toks
    multiplier = low_rank_scale / (toks * 2 * lax.axis_size("z"))

    zpos = lax.axis_index("z")
    x_tokens = lax.dynamic_slice_in_dim(section_inputs[0], core * toks, toks, 1)
    x_y = lax.dynamic_slice_in_dim(x_tokens, ypos * width, width, 2).reshape(rows_all, width)
    x_moved = lax.ppermute(x_y, "s", EVERY)
    first = proj_weight[0][:, :half].T
    second = proj_weight[0][:, half:].T
    empty = (
        jnp.zeros((CHUNKS, rows, width + TAIL), bf16),
        jnp.zeros((CHUNKS, rows, group * rank), bf16),
        jnp.zeros((CHUNKS, rows, width), bf16),
        jnp.zeros((CHUNKS, rows, TAIL), bf16),
    )
    x_moved, first, second, x_tokens, x_y, empty = lax.optimization_barrier(
        (x_moved, first, second, x_tokens, x_y, empty)
    )
    right_1 = lax.ppermute(first, ("s", "z"), RIGHT)
    left_1 = lax.ppermute(second, ("s", "z"), LEFT)

    x_f = x_tokens.reshape(rows_all, width_all).astype(f32)
    inv_rms = lax.rsqrt(jnp.mean(x_f * x_f, axis=-1, keepdims=True) + norm_eps)
    normed_y = x_y.astype(f32) * inv_rms
    x_before = lax.cond(
        sec == 15, lambda x: jnp.zeros((4,) + x.shape, x.dtype), spread, x_moved
    )
    x_before, norm_gain, adapter_down = lax.optimization_barrier(
        (x_before, norm_gain, adapter_down)
    )
    gain_y = both_cores(norm_gain, 1)
    down_y = both_cores(adapter_down[0], 1)
    h_y = (normed_y * gain_y).astype(bf16)

    iota = jnp.arange(micro, dtype=jnp.int32)
    tenant_hot = tenant_ids[:, None] == iota[None, :]
    slot_ids = jnp.sum(jnp.where(tenant_hot, slot_table[0][None, :], 0), axis=1)
    down_sel = down_y[slot_ids]
    up_sel = adapter_up[0][slot_ids]
    low_part = jnp.einsum(
        "mtd,mdr->mtr", h_y.reshape(micro, toks, width), down_sel, preferred_element_type=f32
    )

    def extra(args):
        h_y, low_part = args
        low_in = lax.psum(low_part, "y").astype(bf16)
        return lax.all_gather(h_y, "z"), lax.all_gather(low_in, "z")

    x_before = x_before.reshape(4, CHUNKS, rows, width)
    x_chunk = x_y.reshape(CHUNKS, rows, width)
    inv_chunk = jnp.broadcast_to(inv_rms.reshape(CHUNKS, rows, 1), (CHUNKS, rows, TAIL))
    down_chunk = down_sel.transpose(0, 2, 1).reshape(CHUNKS, group * rank, width)
    up_chunk = up_sel.reshape(CHUNKS, group * rank, width_all)

    def top(args):
        out_grads, first, second, _ = args
        shard = jnp.concatenate([first, second], 0)
        shard_x = lax.ppermute(shard, ("s", "c"), TOP_SWAP)
        grad = lax.dynamic_slice_in_dim(out_grads, core * toks, toks, 1)
        low = jnp.einsum("mtd,mrd->mtr", grad, up_sel, preferred_element_type=f32).astype(bf16)
        adapt = jnp.einsum("mtr,mdr->mtd", low, down_sel, preferred_element_type=f32)
        grad = grad.reshape(rows_all, width_all)
        blocks = jnp.stack([grad[:, i * width : (i + 1) * width] for i in range(4)])
        blocks = lax.all_to_all(blocks, "z", 0, 0).reshape(4 * rows_all, width)
        mine, theirs = (
            lax.dot_general(blocks, w, contract_inner, preferred_element_type=f32).astype(bf16)
            for w in (shard, shard_x)
        )
        terms = jnp.concatenate(
            [jnp.where(core == 0, mine, theirs), jnp.where(core == 0, theirs, mine)], 1
        )
        terms = lax.all_to_all(terms.reshape(4, rows_all, width), "z", 0, 0)
        total = jnp.sum(terms.astype(f32), axis=0)
        total = total + low_rank_scale * adapt.reshape(rows_all, width)
        grad_y = lax.dynamic_slice_in_dim(grad, ypos * width, width, 1)
        sent, tail = message(total, grad_y, gain_y, inv_rms, x_y, width_all)
        boxes = jnp.concatenate([sent, tail], 1).reshape(CHUNKS, rows, width + TAIL)
        member = jnp.arange(rows_all)[:, None] // toks % group == jnp.arange(group)[None, :]
        low = jnp.where(member[:, :, None], low.reshape(rows_all, 1, rank), 0)
        low = low.astype(bf16).reshape(CHUNKS, rows, group * rank)
        tail = tail.reshape(CHUNKS, rows, TAIL)
        return boxes, low, grad_y.reshape(CHUNKS, rows, width), tail

    def swapped(value):
        return lax.ppermute(value, ("s", "c"), PAIRS)

    ready = (x_before, x_chunk, inv_chunk, down_chunk, up_chunk, gain_y, h_y, low_part)
    right_1, left_1, ready = lax.optimization_barrier((right_1, left_1, ready))
    kept = lax.cond(sec == 15, top, lambda args: args[3], (out_grads, first, second, empty))
    boxes_top = lax.ppermute(kept[0], "s", [(15, 14)])
    right_2 = lax.ppermute(right_1, ("s", "z"), RIGHT)
    left_2 = lax.ppermute(left_1, ("s", "z"), LEFT)
    others = [swapped(w) for w in (right_1, left_1)]
    right_2, left_2, others, first, second = lax.optimization_barrier(
        (right_2, left_2, others, first, second)
    )
    right_3 = lax.ppermute(right_2, ("s", "z"), RIGHT)
    left_3 = lax.ppermute(left_2, ("s", "z"), LEFT)
    more = [swapped(w) for w in (first, second, right_2, left_2)]
    right_3, left_3, more, kept, boxes_top, ready = lax.optimization_barrier(
        (right_3, left_3, more, kept, boxes_top, ready)
    )
    x_before, x_chunk, inv_chunk, down_chunk, up_chunk, gain_y, h_y, low_part = ready
    last = [swapped(w) for w in (right_3, left_3)]
    weights = [first, second, right_1, left_1, right_2, left_2, right_3, left_3]
    weights = weights + more[:2] + others + more[2:] + last
    extras = lax.cond(
        sec <= 15 - AHEAD,
        extra,
        lambda args: (
            jnp.zeros((4, rows_all, width), bf16),
            jnp.zeros((4, micro, toks, rank), bf16),
        ),
        (h_y, low_part),
    )

    def pick(array, m):
        return lax.dynamic_index_in_dim(array, m, 0, keepdims=False)

    def step(u, state):
        box, kept = state
        t, m = u // CHUNKS, u % CHUNKS
        turn = 15 - t + m

        def computed(args):
            box, kept = args
            place = jnp.stack([m, ypos, core, zpos]).astype(jnp.int32)
            parts = lax.cond(
                sec == 15, lambda box: jnp.zeros((4,) + box.shape, box.dtype), spread, box
            )
            box, *kept = run_stage(
                place,
                parts,
                x_before,
                up_chunk,
                down_chunk,
                gain_y,
                inv_chunk,
                x_chunk,
                weights,
                kept,
            )
            return box, tuple(kept)

        box, kept = lax.cond(
            (sec == turn) & (sec < 15), computed, lambda args: args, (box, kept)
        )
        part = ((sec == turn) | (sec == turn - 1)) & (turn >= 1) & (turn <= 14)
        kind = jnp.where(part, jnp.where(turn % 2 == 1, 1, 2), 0)
        kind = jnp.where((turn == 15) & (sec == 14), 3, kind)
        box = lax.switch(
            kind,
            [
                lambda box: box,
                lambda box: lax.ppermute(box, "s", ODD),
                lambda box: lax.ppermute(box, "s", EVEN),
                lambda box: pick(boxes_top, m),
            ],
            box,
        )
        return box, kept

    start = (pick(boxes_top, 0), kept)
    _, kept = lax.fori_loop(0, (15 + CHUNKS) * CHUNKS, step, start)
    boxes, low_all, grad_all, tail_all = kept
    low_all, h_y, low_part = lax.optimization_barrier((low_all, h_y, low_part))
    h_all, low_in_all = lax.cond(
        sec > 15 - AHEAD, lambda args: extra((h_y, low_part)), lambda args: args, extras
    )

    coefs = spread(tail_all)
    coef_sum = jnp.sum(coefs.astype(f32), axis=(0, -1))[..., None]
    new_grads = boxes[:, :, :width].astype(f32) - coef_sum * x_chunk.astype(f32)
    new_grads = new_grads.astype(bf16).reshape(micro, toks, width)
    keep = jnp.where(core == 0, new_grads[:, :, :half], new_grads[:, :, half:])
    give = jnp.where(core == 0, new_grads[:, :, half:], new_grads[:, :, :half])
    got = lax.ppermute(give, "c", SWAP)
    kept = jnp.concatenate(
        [jnp.where(core == 0, keep, got), jnp.where(core == 0, got, keep)], 1
    )

    both = jnp.concatenate(
        [
            grad_all.reshape(rows_all, width),
            jnp.pad(low_all.reshape(rows_all, group * rank), ((0, 0), (0, TAIL - group * rank))),
        ],
        1,
    )
    both = lax.all_gather(both, "z").reshape(4, micro, toks, width + TAIL)
    grads_z = both[..., :width]
    low_z = both[..., width : width + group * rank].reshape(4, micro, toks, group, rank)
    low_z = jnp.sum(low_z.astype(f32), axis=3).astype(bf16)
    hidden_z = h_all.reshape(4, micro, toks, width)
    down_part = multiplier * jnp.einsum(
        "zmtd,zmtr->mdr", hidden_z, low_z, preferred_element_type=f32
    )
    up_part = multiplier * jnp.einsum(
        "zmtr,zmtd->mrd", low_in_all, grads_z, preferred_element_type=f32
    )
    down_acc = half_sum(down_part, 1)
    up_acc = half_sum(up_part, 2)
    slot_hot = slot_ids[None, :] == iota[:, None]
    down_out = jnp.sum(jnp.where(slot_hot[:, :, None, None], down_acc[None], 0.0), axis=1)
    up_out = jnp.sum(jnp.where(slot_hot[:, :, None, None], up_acc[None], 0.0), axis=1)
    return (kept[None], down_out[None], up_out[None])


def solution(mesh):
    fine = Mesh(mesh.devices.reshape(16, 4, 2, 4), ("s", "y", "c", "z"))
    mp = ("y", "c")
    placed = (
        P("s", None, "z", None),
        P(None, "z", None),
        P("s", mp, "z"),
        P("s", mp),
        P("s", None, mp, None),
        P("s", None, None, None),
        P(),
        P("s", None),
    )
    return jax.shard_map(
        local,
        mesh=fine,
        in_specs=placed,
        out_specs=(
            P("s", None, "z", mp),
            P("s", None, mp, None),
            P("s", None, None, mp),
        ),
        check_vma=False,
    )
```

```python
import functools

import jax
import jax.numpy as jnp
from jax import lax
from jax.experimental import pallas as pl
from jax.experimental.pallas import tpu as pltpu
from jax.sharding import Mesh, PartitionSpec as P

norm_eps = 1e-05
low_rank_scale = 2.0
CHUNKS = 2
TAIL = 128
SWAP = [(0, 1), (1, 0)]
ODD = [(s, s - 1) for s in range(15, 0, -2)]
EVEN = [(s, s - 1) for s in range(14, 0, -2)]
EVERY = [(s, s - 1) for s in range(15, 0, -1)]
f32 = jnp.float32
bf16 = jnp.bfloat16
contract_last = (((1,), (1,)), ((), ()))
contract_inner = (((1,), (0,)), ((), ()))
AHEAD = 3
TOP_SWAP = [(30, 31), (31, 30)]
RIGHT = [(4 * s + z, 4 * s + (z + 1) % 4) for s in range(15) for z in range(4)]
LEFT = [(4 * s + z, 4 * s + (z + 3) % 4) for s in range(15) for z in range(4)]
PAIRS = [(2 * s + c, 2 * s + 1 - c) for s in range(15) for c in range(2)]


def both_cores(value, axis):
    core = lax.axis_index("c")
    other = lax.ppermute(value, "c", SWAP)
    low = jnp.where(core == 0, value, other)
    high = jnp.where(core == 0, other, value)
    return jnp.concatenate([low, high], axis)


def half_sum(value, axis):
    core = lax.axis_index("c")
    width = value.shape[axis] // 2
    low = lax.slice_in_dim(value, 0, width, axis=axis)
    high = lax.slice_in_dim(value, width, 2 * width, axis=axis)
    mine = jnp.where(core == 0, low, high)
    theirs = jnp.where(core == 0, high, low)
    return mine + lax.ppermute(theirs, "c", SWAP)


def spread(value):
    sent = jnp.broadcast_to(value[None], (4,) + value.shape)
    return lax.all_to_all(sent, "y", 0, 0)


def own_group(low, group):
    rows, cols = low.shape
    row_group = lax.broadcasted_iota(jnp.int32, low.shape, 0) // (rows // group)
    col_group = lax.broadcasted_iota(jnp.int32, low.shape, 1) // (cols // group)
    return jnp.where(row_group == col_group, low, 0.0).astype(bf16)


def message(total, grad_y, gain, inv, x, width_all):
    rows, width = total.shape
    normed_grad = (total * gain).astype(bf16).astype(f32)
    sent = (grad_y.astype(f32) + inv * normed_grad).astype(bf16)
    coef = jnp.sum(normed_grad * x.astype(f32), axis=1, keepdims=True)
    coef = coef * (inv * inv * inv / width_all)
    lane = lax.broadcasted_iota(jnp.int32, (rows, TAIL), 1)
    high = lax.reduce_precision(coef, 8, 7)
    tail = jnp.where(lane == 0, high, jnp.where(lane == 1, coef - high, 0.0)).astype(bf16)
    return sent, tail


def stage_kernel(place_ref, parts_ref, gain_ref, before_any, up_any, down_any, inv_any, x_any, *refs, group):
    weights, refs = refs[:16], refs[16 + 4 :]
    box_ref, boxes_any, low_any, grad_any, tail_any = refs[:5]
    before_ref, up_ref, down_ref, inv_ref, x_ref, full, weight, low_ref, grad_ref, tail_ref = refs[5:15]
    in_sems, w_sems, out_sems = refs[15:]
    m, ypos, core, zpos = place_ref[0], place_ref[1], place_ref[2], place_ref[3]
    width = x_ref.shape[1]
    width_all = full.shape[1]
    half = width // 2

    def started(source, target, sem):
        copy = pltpu.make_async_copy(source, target, sem)
        copy.start()
        return copy

    before_copy = started(before_any.at[:, m], before_ref, in_sems.at[0])
    up_copy = started(up_any.at[m], up_ref, in_sems.at[1])
    copies = []
    for piece in range(8):
        for side, base in enumerate((core * half, (1 - core) * half)):
            lanes = pl.ds(pl.multiple_of(base, 128), half)
            target = weight.at[pl.ds(piece * half, half), lanes]
            copies.append(started(weights[8 * side + piece], target, w_sems.at[piece, side]))
        if piece == 0:
            down_copy = started(down_any.at[m], down_ref, in_sems.at[2])
            inv_copy = started(inv_any.at[m], inv_ref, in_sems.at[3])
            x_copy = started(x_any.at[m], x_ref, in_sems.at[4])

    tail = parts_ref[:, :, width:].astype(f32)
    coef = jnp.sum(jnp.sum(tail, axis=0), axis=1, keepdims=True)
    before_copy.wait()
    up_copy.wait()
    low = None
    for part in range(4):
        fixed = parts_ref[part, :, :width].astype(f32) - coef * before_ref[part].astype(f32)
        fixed = fixed.astype(bf16)
        first = 2 * lax.rem(zpos - part + 4, 4) * half
        second = (2 * lax.rem(part - zpos + 4, 4) + 1) * half
        full[:, pl.ds(pl.multiple_of(first, 128), half)] = fixed[:, :half]
        full[:, pl.ds(pl.multiple_of(second, 128), half)] = fixed[:, half:]

        @pl.when(part == ypos)
        def _(fixed=fixed):
            grad_ref[...] = fixed

        term = lax.dot_general(
            fixed,
            up_ref[:, part * width : (part + 1) * width],
            contract_last,
            preferred_element_type=f32,
        )
        low = term if low is None else low + term
    grad_copy = started(grad_ref, grad_any.at[m], out_sems.at[0])
    low = own_group(low, group)
    low_ref[...] = low
    low_copy = started(low_ref, low_any.at[m], out_sems.at[1])
    down_copy.wait()
    total = low_rank_scale * lax.dot_general(
        low, down_ref[...], contract_inner, preferred_element_type=f32
    )
    for part in range(4):
        for copy in copies[4 * part : 4 * part + 4]:
            copy.wait()
        span = slice(part * width, (part + 1) * width)
        total = total + lax.dot_general(
            full[:, span], weight[span], contract_inner, preferred_element_type=f32
        )
    inv_copy.wait()
    x_copy.wait()
    sent, tail = message(
        total, grad_ref[...], gain_ref[...], inv_ref[:, 0:1], x_ref[...], width_all
    )
    box_ref[:, :width] = sent
    box_ref[:, width:] = tail
    tail_ref[...] = tail
    box_copy = started(box_ref, boxes_any.at[m], out_sems.at[2])
    tail_copy = started(tail_ref, tail_any.at[m], out_sems.at[3])
    grad_copy.wait()
    low_copy.wait()
    box_copy.wait()
    tail_copy.wait()


def run_stage(place, parts, before, up, down, gain, inv, x, weights, kept):
    _, rows, width = x.shape
    width_all = 4 * width
    cols = up.shape[1]
    vmem = pl.BlockSpec(memory_space=pltpu.VMEM)
    any_space = pl.BlockSpec(memory_space=pl.ANY)
    inputs = [place, parts, gain, before, up, down, inv, x, *weights]
    return pl.pallas_call(
        functools.partial(stage_kernel, group=cols // 16),
        in_specs=[pl.BlockSpec(memory_space=pltpu.SMEM), vmem, vmem]
        + [any_space] * (len(inputs) + len(kept) - 3),
        out_specs=[vmem] + [any_space] * len(kept),
        scratch_shapes=[
            pltpu.VMEM((4, rows, width), bf16),
            pltpu.VMEM((cols, width_all), bf16),
            pltpu.VMEM((cols, width), bf16),
            pltpu.VMEM((rows, TAIL), f32),
            pltpu.VMEM((rows, width), bf16),
            pltpu.VMEM((rows, width_all), bf16),
            pltpu.VMEM((width_all, width), bf16),
            pltpu.VMEM((rows, cols), bf16),
            pltpu.VMEM((rows, width), bf16),
            pltpu.VMEM((rows, TAIL), bf16),
            pltpu.SemaphoreType.DMA((5,)),
            pltpu.SemaphoreType.DMA((8, 2)),
            pltpu.SemaphoreType.DMA((4,)),
        ],
        out_shape=[jax.ShapeDtypeStruct((rows, width + TAIL), bf16)]
        + [jax.ShapeDtypeStruct(k.shape, k.dtype) for k in kept],
        input_output_aliases={len(inputs) + i: 1 + i for i in range(len(kept))},
        compiler_params=pltpu.CompilerParams(vmem_limit_bytes=32 * 1024 * 1024),
        cost_estimate=pl.CostEstimate(
            flops=2 * rows * width * width_all, bytes_accessed=2 * width * width_all, transcendentals=0
        ),
        name="stage",
    )(*inputs, *kept)


def local(
    section_inputs,
    out_grads,
    proj_weight,
    norm_gain,
    adapter_down,
    adapter_up,
    tenant_ids,
    slot_table,
):
    sec = lax.axis_index("s")
    ypos = lax.axis_index("y")
    core = lax.axis_index("c")
    micro = section_inputs.shape[1]
    width_all = section_inputs.shape[3]
    half = proj_weight.shape[1]
    width = 2 * half
    toks = section_inputs.shape[2] // 2
    rank = adapter_down.shape[3]
    rows_all = micro * toks
    group = micro // CHUNKS
    rows = group * toks
    multiplier = low_rank_scale / (toks * 2 * lax.axis_size("z"))

    zpos = lax.axis_index("z")
    x_tokens = lax.dynamic_slice_in_dim(section_inputs[0], core * toks, toks, 1)
    x_y = lax.dynamic_slice_in_dim(x_tokens, ypos * width, width, 2).reshape(rows_all, width)
    x_moved = lax.ppermute(x_y, "s", EVERY)
    first = proj_weight[0][:, :half].T
    second = proj_weight[0][:, half:].T
    empty = (
        jnp.zeros((CHUNKS, rows, width + TAIL), bf16),
        jnp.zeros((CHUNKS, rows, group * rank), bf16),
        jnp.zeros((CHUNKS, rows, width), bf16),
        jnp.zeros((CHUNKS, rows, TAIL), bf16),
    )
    x_moved, first, second, norm_gain, adapter_down, x_tokens, x_y, empty = lax.optimization_barrier(
        (x_moved, first, second, norm_gain, adapter_down, x_tokens, x_y, empty)
    )
    right_1 = lax.ppermute(first, ("s", "z"), RIGHT)
    left_1 = lax.ppermute(second, ("s", "z"), LEFT)

    x_f = x_tokens.reshape(rows_all, width_all).astype(f32)
    inv_rms = lax.rsqrt(jnp.mean(x_f * x_f, axis=-1, keepdims=True) + norm_eps)
    normed_y = x_y.astype(f32) * inv_rms
    x_before = lax.cond(
        sec == 15, lambda x: jnp.zeros((4,) + x.shape, x.dtype), spread, x_moved
    )
    gain_y = both_cores(norm_gain, 1)
    down_y = both_cores(adapter_down[0], 1)
    h_y = (normed_y * gain_y).astype(bf16)

    iota = jnp.arange(micro, dtype=jnp.int32)
    tenant_hot = tenant_ids[:, None] == iota[None, :]
    slot_ids = jnp.sum(jnp.where(tenant_hot, slot_table[0][None, :], 0), axis=1)
    down_sel = down_y[slot_ids]
    up_sel = adapter_up[0][slot_ids]
    low_part = jnp.einsum(
        "mtd,mdr->mtr", h_y.reshape(micro, toks, width), down_sel, preferred_element_type=f32
    )

    def extra(args):
        h_y, low_part = args
        low_in = lax.psum(low_part, "y").astype(bf16)
        return lax.all_gather(h_y, "z"), lax.all_gather(low_in, "z")

    x_before = x_before.reshape(4, CHUNKS, rows, width)
    x_chunk = x_y.reshape(CHUNKS, rows, width)
    inv_chunk = jnp.broadcast_to(inv_rms.reshape(CHUNKS, rows, 1), (CHUNKS, rows, TAIL))
    down_chunk = down_sel.transpose(0, 2, 1).reshape(CHUNKS, group * rank, width)
    up_chunk = up_sel.reshape(CHUNKS, group * rank, width_all)

    def top(args):
        out_grads, first, second, _ = args
        shard = jnp.concatenate([first, second], 0)
        shard_x = lax.ppermute(shard, ("s", "c"), TOP_SWAP)
        grad = lax.dynamic_slice_in_dim(out_grads, core * toks, toks, 1)
        low = jnp.einsum("mtd,mrd->mtr", grad, up_sel, preferred_element_type=f32).astype(bf16)
        adapt = jnp.einsum("mtr,mdr->mtd", low, down_sel, preferred_element_type=f32)
        grad = grad.reshape(rows_all, width_all)
        blocks = jnp.stack([grad[:, i * width : (i + 1) * width] for i in range(4)])
        blocks = lax.all_to_all(blocks, "z", 0, 0).reshape(4 * rows_all, width)
        mine, theirs = (
            lax.dot_general(blocks, w, contract_inner, preferred_element_type=f32).astype(bf16)
            for w in (shard, shard_x)
        )
        terms = jnp.concatenate(
            [jnp.where(core == 0, mine, theirs), jnp.where(core == 0, theirs, mine)], 1
        )
        terms = lax.all_to_all(terms.reshape(4, rows_all, width), "z", 0, 0)
        total = jnp.sum(terms.astype(f32), axis=0)
        total = total + low_rank_scale * adapt.reshape(rows_all, width)
        grad_y = lax.dynamic_slice_in_dim(grad, ypos * width, width, 1)
        sent, tail = message(total, grad_y, gain_y, inv_rms, x_y, width_all)
        boxes = jnp.concatenate([sent, tail], 1).reshape(CHUNKS, rows, width + TAIL)
        member = jnp.arange(rows_all)[:, None] // toks % group == jnp.arange(group)[None, :]
        low = jnp.where(member[:, :, None], low.reshape(rows_all, 1, rank), 0)
        low = low.astype(bf16).reshape(CHUNKS, rows, group * rank)
        tail = tail.reshape(CHUNKS, rows, TAIL)
        return boxes, low, grad_y.reshape(CHUNKS, rows, width), tail

    def swapped(value):
        return lax.ppermute(value, ("s", "c"), PAIRS)

    ready = (x_before, x_chunk, inv_chunk, down_chunk, up_chunk, gain_y, h_y, low_part)
    right_1, left_1, ready = lax.optimization_barrier((right_1, left_1, ready))
    kept = lax.cond(sec == 15, top, lambda args: args[3], (out_grads, first, second, empty))
    boxes_top = lax.ppermute(kept[0], "s", [(15, 14)])
    right_2 = lax.ppermute(right_1, ("s", "z"), RIGHT)
    left_2 = lax.ppermute(left_1, ("s", "z"), LEFT)
    others = [swapped(w) for w in (right_1, left_1)]
    right_2, left_2, others, first, second = lax.optimization_barrier(
        (right_2, left_2, others, first, second)
    )
    right_3 = lax.ppermute(right_2, ("s", "z"), RIGHT)
    left_3 = lax.ppermute(left_2, ("s", "z"), LEFT)
    more = [swapped(w) for w in (first, second, right_2, left_2)]
    right_3, left_3, more, kept, boxes_top, ready = lax.optimization_barrier(
        (right_3, left_3, more, kept, boxes_top, ready)
    )
    x_before, x_chunk, inv_chunk, down_chunk, up_chunk, gain_y, h_y, low_part = ready
    last = [swapped(w) for w in (right_3, left_3)]
    weights = [first, second, right_1, left_1, right_2, left_2, right_3, left_3]
    weights = weights + more[:2] + others + more[2:] + last
    extras = lax.cond(
        sec <= 15 - AHEAD,
        extra,
        lambda args: (
            jnp.zeros((4, rows_all, width), bf16),
            jnp.zeros((4, micro, toks, rank), bf16),
        ),
        (h_y, low_part),
    )

    def pick(array, m):
        return lax.dynamic_index_in_dim(array, m, 0, keepdims=False)

    def step(u, state):
        box, kept = state
        t, m = u // CHUNKS, u % CHUNKS
        turn = 15 - t + m

        def computed(args):
            box, kept = args
            place = jnp.stack([m, ypos, core, zpos]).astype(jnp.int32)
            parts = lax.cond(
                sec == 15, lambda box: jnp.zeros((4,) + box.shape, box.dtype), spread, box
            )
            box, *kept = run_stage(
                place,
                parts,
                x_before,
                up_chunk,
                down_chunk,
                gain_y,
                inv_chunk,
                x_chunk,
                weights,
                kept,
            )
            return box, tuple(kept)

        box, kept = lax.cond(
            (sec == turn) & (sec < 15), computed, lambda args: args, (box, kept)
        )
        part = ((sec == turn) | (sec == turn - 1)) & (turn >= 1) & (turn <= 14)
        kind = jnp.where(part, jnp.where(turn % 2 == 1, 1, 2), 0)
        kind = jnp.where((turn == 15) & (sec == 14), 3, kind)
        box = lax.switch(
            kind,
            [
                lambda box: box,
                lambda box: lax.ppermute(box, "s", ODD),
                lambda box: lax.ppermute(box, "s", EVEN),
                lambda box: pick(boxes_top, m),
            ],
            box,
        )
        return box, kept

    start = (pick(boxes_top, 0), kept)
    _, kept = lax.fori_loop(0, (15 + CHUNKS) * CHUNKS, step, start)
    boxes, low_all, grad_all, tail_all = kept
    low_all, h_y, low_part = lax.optimization_barrier((low_all, h_y, low_part))
    h_all, low_in_all = lax.cond(
        sec > 15 - AHEAD, lambda args: extra((h_y, low_part)), lambda args: args, extras
    )

    coefs = spread(tail_all)
    coef_sum = jnp.sum(coefs.astype(f32), axis=(0, -1))[..., None]
    new_grads = boxes[:, :, :width].astype(f32) - coef_sum * x_chunk.astype(f32)
    new_grads = new_grads.astype(bf16).reshape(micro, toks, width)
    keep = jnp.where(core == 0, new_grads[:, :, :half], new_grads[:, :, half:])
    give = jnp.where(core == 0, new_grads[:, :, half:], new_grads[:, :, :half])
    got = lax.ppermute(give, "c", SWAP)
    kept = jnp.concatenate(
        [jnp.where(core == 0, keep, got), jnp.where(core == 0, got, keep)], 1
    )

    both = jnp.concatenate(
        [
            grad_all.reshape(rows_all, width),
            jnp.pad(low_all.reshape(rows_all, group * rank), ((0, 0), (0, TAIL - group * rank))),
        ],
        1,
    )
    both = lax.all_gather(both, "z").reshape(4, micro, toks, width + TAIL)
    grads_z = both[..., :width]
    low_z = both[..., width : width + group * rank].reshape(4, micro, toks, group, rank)
    low_z = jnp.sum(low_z.astype(f32), axis=3).astype(bf16)
    hidden_z = h_all.reshape(4, micro, toks, width)
    down_part = multiplier * jnp.einsum(
        "zmtd,zmtr->mdr", hidden_z, low_z, preferred_element_type=f32
    )
    up_part = multiplier * jnp.einsum(
        "zmtr,zmtd->mrd", low_in_all, grads_z, preferred_element_type=f32
    )
    down_acc = half_sum(down_part, 1)
    up_acc = half_sum(up_part, 2)
    slot_hot = slot_ids[None, :] == iota[:, None]
    down_out = jnp.sum(jnp.where(slot_hot[:, :, None, None], down_acc[None], 0.0), axis=1)
    up_out = jnp.sum(jnp.where(slot_hot[:, :, None, None], up_acc[None], 0.0), axis=1)
    return (kept[None], down_out[None], up_out[None])


def solution(mesh):
    fine = Mesh(mesh.devices.reshape(16, 4, 2, 4), ("s", "y", "c", "z"))
    mp = ("y", "c")
    placed = (
        P("s", None, "z", None),
        P(None, "z", None),
        P("s", mp, "z"),
        P("s", mp),
        P("s", None, mp, None),
        P("s", None, None, None),
        P(),
        P("s", None),
    )
    return jax.shard_map(
        local,
        mesh=fine,
        in_specs=placed,
        out_specs=(
            P("s", None, "z", mp),
            P("s", None, mp, None),
            P("s", None, None, mp),
        ),
        check_vma=False,
    )
```

```python
import functools

import jax
import jax.numpy as jnp
from jax import lax
from jax.experimental import pallas as pl
from jax.experimental.pallas import tpu as pltpu
from jax.sharding import Mesh, PartitionSpec as P

norm_eps = 1e-05
low_rank_scale = 2.0
CHUNKS = 2
TAIL = 128
SWAP = [(0, 1), (1, 0)]
ODD = [(s, s - 1) for s in range(15, 0, -2)]
EVEN = [(s, s - 1) for s in range(14, 0, -2)]
EVERY = [(s, s - 1) for s in range(15, 0, -1)]
f32 = jnp.float32
bf16 = jnp.bfloat16
contract_last = (((1,), (1,)), ((), ()))
contract_inner = (((1,), (0,)), ((), ()))
AHEAD = 3
TOP_SWAP = [(30, 31), (31, 30)]
RIGHT = [(4 * s + z, 4 * s + (z + 1) % 4) for s in range(15) for z in range(4)]
LEFT = [(4 * s + z, 4 * s + (z + 3) % 4) for s in range(15) for z in range(4)]
PAIRS = [(2 * s + c, 2 * s + 1 - c) for s in range(15) for c in range(2)]


def both_cores(value, axis):
    core = lax.axis_index("c")
    other = lax.ppermute(value, "c", SWAP)
    low = jnp.where(core == 0, value, other)
    high = jnp.where(core == 0, other, value)
    return jnp.concatenate([low, high], axis)


def half_sum(value, axis):
    core = lax.axis_index("c")
    width = value.shape[axis] // 2
    low = lax.slice_in_dim(value, 0, width, axis=axis)
    high = lax.slice_in_dim(value, width, 2 * width, axis=axis)
    mine = jnp.where(core == 0, low, high)
    theirs = jnp.where(core == 0, high, low)
    return mine + lax.ppermute(theirs, "c", SWAP)


def spread(value):
    sent = jnp.broadcast_to(value[None], (4,) + value.shape)
    return lax.all_to_all(sent, "y", 0, 0)


def own_group(low, group):
    rows, cols = low.shape
    row_group = lax.broadcasted_iota(jnp.int32, low.shape, 0) // (rows // group)
    col_group = lax.broadcasted_iota(jnp.int32, low.shape, 1) // (cols // group)
    return jnp.where(row_group == col_group, low, 0.0).astype(bf16)


def message(total, grad_y, gain, inv, x, width_all):
    rows, width = total.shape
    normed_grad = (total * gain).astype(bf16).astype(f32)
    sent = (grad_y.astype(f32) + inv * normed_grad).astype(bf16)
    coef = jnp.sum(normed_grad * x.astype(f32), axis=1, keepdims=True)
    coef = coef * (inv * inv * inv / width_all)
    lane = lax.broadcasted_iota(jnp.int32, (rows, TAIL), 1)
    high = lax.reduce_precision(coef, 8, 7)
    tail = jnp.where(lane == 0, high, jnp.where(lane == 1, coef - high, 0.0)).astype(bf16)
    return sent, tail


def stage_kernel(place_ref, parts_ref, gain_ref, before_any, up_any, down_any, inv_any, x_any, *refs, group):
    weights, refs = refs[:16], refs[16 + 4 :]
    box_ref, boxes_any, low_any, grad_any, tail_any = refs[:5]
    before_ref, up_ref, down_ref, inv_ref, x_ref, full, weight, low_ref, grad_ref, tail_ref = refs[5:15]
    in_sems, w_sems, out_sems = refs[15:]
    m, ypos, core, zpos = place_ref[0], place_ref[1], place_ref[2], place_ref[3]
    width = x_ref.shape[1]
    width_all = full.shape[1]
    half = width // 2

    def started(source, target, sem):
        copy = pltpu.make_async_copy(source, target, sem)
        copy.start()
        return copy

    before_copy = started(before_any.at[:, m], before_ref, in_sems.at[0])
    up_copy = started(up_any.at[m], up_ref, in_sems.at[1])
    copies = []
    for piece in range(8):
        for side, base in enumerate((core * half, (1 - core) * half)):
            lanes = pl.ds(pl.multiple_of(base, 128), half)
            target = weight.at[pl.ds(piece * half, half), lanes]
            copies.append(started(weights[8 * side + piece], target, w_sems.at[piece, side]))
        if piece == 0:
            down_copy = started(down_any.at[m], down_ref, in_sems.at[2])
            inv_copy = started(inv_any.at[m], inv_ref, in_sems.at[3])
            x_copy = started(x_any.at[m], x_ref, in_sems.at[4])

    tail = parts_ref[:, :, width:].astype(f32)
    coef = jnp.sum(jnp.sum(tail, axis=0), axis=1, keepdims=True)
    before_copy.wait()
    up_copy.wait()
    low = None
    for part in range(4):
        fixed = parts_ref[part, :, :width].astype(f32) - coef * before_ref[part].astype(f32)
        fixed = fixed.astype(bf16)
        first = 2 * lax.rem(zpos - part + 4, 4) * half
        second = (2 * lax.rem(part - zpos + 4, 4) + 1) * half
        full[:, pl.ds(pl.multiple_of(first, 128), half)] = fixed[:, :half]
        full[:, pl.ds(pl.multiple_of(second, 128), half)] = fixed[:, half:]

        @pl.when(part == ypos)
        def _(fixed=fixed):
            grad_ref[...] = fixed

        term = lax.dot_general(
            fixed,
            up_ref[:, part * width : (part + 1) * width],
            contract_last,
            preferred_element_type=f32,
        )
        low = term if low is None else low + term
    grad_copy = started(grad_ref, grad_any.at[m], out_sems.at[0])
    low = own_group(low, group)
    low_ref[...] = low
    low_copy = started(low_ref, low_any.at[m], out_sems.at[1])
    down_copy.wait()
    total = low_rank_scale * lax.dot_general(
        low, down_ref[...], contract_inner, preferred_element_type=f32
    )
    for begin, end in ((0, 2), (2, 4), (4, 6), (6, 7), (7, 8)):
        for copy in copies[2 * begin : 2 * end]:
            copy.wait()
        span = slice(begin * half, end * half)
        total = total + lax.dot_general(
            full[:, span], weight[span], contract_inner, preferred_element_type=f32
        )
    inv_copy.wait()
    x_copy.wait()
    sent, tail = message(
        total, grad_ref[...], gain_ref[...], inv_ref[:, 0:1], x_ref[...], width_all
    )
    box_ref[:, :width] = sent
    box_ref[:, width:] = tail
    tail_ref[...] = tail
    box_copy = started(box_ref, boxes_any.at[m], out_sems.at[2])
    tail_copy = started(tail_ref, tail_any.at[m], out_sems.at[3])
    grad_copy.wait()
    low_copy.wait()
    box_copy.wait()
    tail_copy.wait()


def run_stage(place, parts, before, up, down, gain, inv, x, weights, kept):
    _, rows, width = x.shape
    width_all = 4 * width
    cols = up.shape[1]
    vmem = pl.BlockSpec(memory_space=pltpu.VMEM)
    any_space = pl.BlockSpec(memory_space=pl.ANY)
    inputs = [place, parts, gain, before, up, down, inv, x, *weights]
    return pl.pallas_call(
        functools.partial(stage_kernel, group=cols // 16),
        in_specs=[pl.BlockSpec(memory_space=pltpu.SMEM), vmem, vmem]
        + [any_space] * (len(inputs) + len(kept) - 3),
        out_specs=[vmem] + [any_space] * len(kept),
        scratch_shapes=[
            pltpu.VMEM((4, rows, width), bf16),
            pltpu.VMEM((cols, width_all), bf16),
            pltpu.VMEM((cols, width), bf16),
            pltpu.VMEM((rows, TAIL), f32),
            pltpu.VMEM((rows, width), bf16),
            pltpu.VMEM((rows, width_all), bf16),
            pltpu.VMEM((width_all, width), bf16),
            pltpu.VMEM((rows, cols), bf16),
            pltpu.VMEM((rows, width), bf16),
            pltpu.VMEM((rows, TAIL), bf16),
            pltpu.SemaphoreType.DMA((5,)),
            pltpu.SemaphoreType.DMA((8, 2)),
            pltpu.SemaphoreType.DMA((4,)),
        ],
        out_shape=[jax.ShapeDtypeStruct((rows, width + TAIL), bf16)]
        + [jax.ShapeDtypeStruct(k.shape, k.dtype) for k in kept],
        input_output_aliases={len(inputs) + i: 1 + i for i in range(len(kept))},
        compiler_params=pltpu.CompilerParams(vmem_limit_bytes=32 * 1024 * 1024),
        cost_estimate=pl.CostEstimate(
            flops=2 * rows * width * width_all, bytes_accessed=2 * width * width_all, transcendentals=0
        ),
        name="stage",
    )(*inputs, *kept)


def local(
    section_inputs,
    out_grads,
    proj_weight,
    norm_gain,
    adapter_down,
    adapter_up,
    tenant_ids,
    slot_table,
):
    sec = lax.axis_index("s")
    ypos = lax.axis_index("y")
    core = lax.axis_index("c")
    micro = section_inputs.shape[1]
    width_all = section_inputs.shape[3]
    half = proj_weight.shape[1]
    width = 2 * half
    toks = section_inputs.shape[2] // 2
    rank = adapter_down.shape[3]
    rows_all = micro * toks
    group = micro // CHUNKS
    rows = group * toks
    multiplier = low_rank_scale / (toks * 2 * lax.axis_size("z"))

    zpos = lax.axis_index("z")
    x_tokens = lax.dynamic_slice_in_dim(section_inputs[0], core * toks, toks, 1)
    x_y = lax.dynamic_slice_in_dim(x_tokens, ypos * width, width, 2).reshape(rows_all, width)
    x_moved = lax.ppermute(x_y, "s", EVERY)
    first = proj_weight[0][:, :half].T
    second = proj_weight[0][:, half:].T
    empty = (
        jnp.zeros((CHUNKS, rows, width + TAIL), bf16),
        jnp.zeros((CHUNKS, rows, group * rank), bf16),
        jnp.zeros((CHUNKS, rows, width), bf16),
        jnp.zeros((CHUNKS, rows, TAIL), bf16),
    )
    x_moved, first, second, norm_gain, adapter_down, x_tokens, x_y, empty = lax.optimization_barrier(
        (x_moved, first, second, norm_gain, adapter_down, x_tokens, x_y, empty)
    )
    right_1 = lax.ppermute(first, ("s", "z"), RIGHT)
    left_1 = lax.ppermute(second, ("s", "z"), LEFT)

    x_f = x_tokens.reshape(rows_all, width_all).astype(f32)
    inv_rms = lax.rsqrt(jnp.mean(x_f * x_f, axis=-1, keepdims=True) + norm_eps)
    normed_y = x_y.astype(f32) * inv_rms
    x_before = lax.cond(
        sec == 15, lambda x: jnp.zeros((4,) + x.shape, x.dtype), spread, x_moved
    )
    gain_y = both_cores(norm_gain, 1)
    down_y = both_cores(adapter_down[0], 1)
    h_y = (normed_y * gain_y).astype(bf16)

    iota = jnp.arange(micro, dtype=jnp.int32)
    tenant_hot = tenant_ids[:, None] == iota[None, :]
    slot_ids = jnp.sum(jnp.where(tenant_hot, slot_table[0][None, :], 0), axis=1)
    down_sel = down_y[slot_ids]
    up_sel = adapter_up[0][slot_ids]
    low_part = jnp.einsum(
        "mtd,mdr->mtr", h_y.reshape(micro, toks, width), down_sel, preferred_element_type=f32
    )

    def extra(args):
        h_y, low_part = args
        low_in = lax.psum(low_part, "y").astype(bf16)
        return lax.all_gather(h_y, "z"), lax.all_gather(low_in, "z")

    x_before = x_before.reshape(4, CHUNKS, rows, width)
    x_chunk = x_y.reshape(CHUNKS, rows, width)
    inv_chunk = jnp.broadcast_to(inv_rms.reshape(CHUNKS, rows, 1), (CHUNKS, rows, TAIL))
    down_chunk = down_sel.transpose(0, 2, 1).reshape(CHUNKS, group * rank, width)
    up_chunk = up_sel.reshape(CHUNKS, group * rank, width_all)

    def top(args):
        out_grads, first, second, _ = args
        shard = jnp.concatenate([first, second], 0)
        shard_x = lax.ppermute(shard, ("s", "c"), TOP_SWAP)
        grad = lax.dynamic_slice_in_dim(out_grads, core * toks, toks, 1)
        low = jnp.einsum("mtd,mrd->mtr", grad, up_sel, preferred_element_type=f32).astype(bf16)
        adapt = jnp.einsum("mtr,mdr->mtd", low, down_sel, preferred_element_type=f32)
        grad = grad.reshape(rows_all, width_all)
        blocks = jnp.stack([grad[:, i * width : (i + 1) * width] for i in range(4)])
        blocks = lax.all_to_all(blocks, "z", 0, 0).reshape(4 * rows_all, width)
        mine, theirs = (
            lax.dot_general(blocks, w, contract_inner, preferred_element_type=f32).astype(bf16)
            for w in (shard, shard_x)
        )
        terms = jnp.concatenate(
            [jnp.where(core == 0, mine, theirs), jnp.where(core == 0, theirs, mine)], 1
        )
        terms = lax.all_to_all(terms.reshape(4, rows_all, width), "z", 0, 0)
        total = jnp.sum(terms.astype(f32), axis=0)
        total = total + low_rank_scale * adapt.reshape(rows_all, width)
        grad_y = lax.dynamic_slice_in_dim(grad, ypos * width, width, 1)
        sent, tail = message(total, grad_y, gain_y, inv_rms, x_y, width_all)
        boxes = jnp.concatenate([sent, tail], 1).reshape(CHUNKS, rows, width + TAIL)
        member = jnp.arange(rows_all)[:, None] // toks % group == jnp.arange(group)[None, :]
        low = jnp.where(member[:, :, None], low.reshape(rows_all, 1, rank), 0)
        low = low.astype(bf16).reshape(CHUNKS, rows, group * rank)
        tail = tail.reshape(CHUNKS, rows, TAIL)
        return boxes, low, grad_y.reshape(CHUNKS, rows, width), tail

    def swapped(value):
        return lax.ppermute(value, ("s", "c"), PAIRS)

    ready = (x_before, x_chunk, inv_chunk, down_chunk, up_chunk, gain_y, h_y, low_part)
    right_1, left_1, ready = lax.optimization_barrier((right_1, left_1, ready))
    kept = lax.cond(sec == 15, top, lambda args: args[3], (out_grads, first, second, empty))
    boxes_top = lax.ppermute(kept[0], "s", [(15, 14)])
    right_2 = lax.ppermute(right_1, ("s", "z"), RIGHT)
    left_2 = lax.ppermute(left_1, ("s", "z"), LEFT)
    others = [swapped(w) for w in (right_1, left_1)]
    right_2, left_2, others, first, second = lax.optimization_barrier(
        (right_2, left_2, others, first, second)
    )
    right_3 = lax.ppermute(right_2, ("s", "z"), RIGHT)
    left_3 = lax.ppermute(left_2, ("s", "z"), LEFT)
    more = [swapped(w) for w in (first, second, right_2, left_2)]
    right_3, left_3, more, kept, boxes_top, ready = lax.optimization_barrier(
        (right_3, left_3, more, kept, boxes_top, ready)
    )
    x_before, x_chunk, inv_chunk, down_chunk, up_chunk, gain_y, h_y, low_part = ready
    last = [swapped(w) for w in (right_3, left_3)]
    weights = [first, second, right_1, left_1, right_2, left_2, right_3, left_3]
    weights = weights + more[:2] + others + more[2:] + last
    extras = lax.cond(
        sec <= 15 - AHEAD,
        extra,
        lambda args: (
            jnp.zeros((4, rows_all, width), bf16),
            jnp.zeros((4, micro, toks, rank), bf16),
        ),
        (h_y, low_part),
    )

    def pick(array, m):
        return lax.dynamic_index_in_dim(array, m, 0, keepdims=False)

    def step(u, state):
        box, kept = state
        t, m = u // CHUNKS, u % CHUNKS
        turn = 15 - t + m

        def computed(args):
            box, kept = args
            place = jnp.stack([m, ypos, core, zpos]).astype(jnp.int32)
            parts = lax.cond(
                sec == 15, lambda box: jnp.zeros((4,) + box.shape, box.dtype), spread, box
            )
            box, *kept = run_stage(
                place,
                parts,
                x_before,
                up_chunk,
                down_chunk,
                gain_y,
                inv_chunk,
                x_chunk,
                weights,
                kept,
            )
            return box, tuple(kept)

        box, kept = lax.cond(
            (sec == turn) & (sec < 15), computed, lambda args: args, (box, kept)
        )
        part = ((sec == turn) | (sec == turn - 1)) & (turn >= 1) & (turn <= 14)
        kind = jnp.where(part, jnp.where(turn % 2 == 1, 1, 2), 0)
        kind = jnp.where((turn == 15) & (sec == 14) & (m > 0), 3, kind)
        box = lax.switch(
            kind,
            [
                lambda box: box,
                lambda box: lax.ppermute(box, "s", ODD),
                lambda box: lax.ppermute(box, "s", EVEN),
                lambda box: pick(boxes_top, m),
            ],
            box,
        )
        return box, kept

    start = (pick(boxes_top, 0), kept)
    _, kept = lax.fori_loop(0, (15 + CHUNKS) * CHUNKS, step, start)
    boxes, low_all, grad_all, tail_all = kept
    low_all, h_y, low_part = lax.optimization_barrier((low_all, h_y, low_part))
    h_all, low_in_all = lax.cond(
        sec > 15 - AHEAD, lambda args: extra((h_y, low_part)), lambda args: args, extras
    )

    coefs = spread(tail_all)
    coef_sum = jnp.sum(coefs.astype(f32), axis=(0, -1))[..., None]
    new_grads = boxes[:, :, :width].astype(f32) - coef_sum * x_chunk.astype(f32)
    new_grads = new_grads.astype(bf16).reshape(micro, toks, width)
    keep = jnp.where(core == 0, new_grads[:, :, :half], new_grads[:, :, half:])
    give = jnp.where(core == 0, new_grads[:, :, half:], new_grads[:, :, :half])
    got = lax.ppermute(give, "c", SWAP)
    kept = jnp.concatenate(
        [jnp.where(core == 0, keep, got), jnp.where(core == 0, got, keep)], 1
    )

    both = jnp.concatenate(
        [
            grad_all.reshape(rows_all, width),
            jnp.pad(low_all.reshape(rows_all, group * rank), ((0, 0), (0, TAIL - group * rank))),
        ],
        1,
    )
    both = lax.all_gather(both, "z").reshape(4, micro, toks, width + TAIL)
    grads_z = both[..., :width]
    low_z = both[..., width : width + group * rank].reshape(4, micro, toks, group, rank)
    low_z = jnp.sum(low_z.astype(f32), axis=3).astype(bf16)
    hidden_z = h_all.reshape(4, micro, toks, width)
    down_part = multiplier * jnp.einsum(
        "zmtd,zmtr->mdr", hidden_z, low_z, preferred_element_type=f32
    )
    up_part = multiplier * jnp.einsum(
        "zmtr,zmtd->mrd", low_in_all, grads_z, preferred_element_type=f32
    )
    down_acc = half_sum(down_part, 1)
    up_acc = half_sum(up_part, 2)
    slot_hot = slot_ids[None, :] == iota[:, None]
    down_out = jnp.sum(jnp.where(slot_hot[:, :, None, None], down_acc[None], 0.0), axis=1)
    up_out = jnp.sum(jnp.where(slot_hot[:, :, None, None], up_acc[None], 0.0), axis=1)
    return (kept[None], down_out[None], up_out[None])


def solution(mesh):
    fine = Mesh(mesh.devices.reshape(16, 4, 2, 4), ("s", "y", "c", "z"))
    mp = ("y", "c")
    placed = (
        P("s", None, "z", None),
        P(None, "z", None),
        P("s", mp, "z"),
        P("s", mp),
        P("s", None, mp, None),
        P("s", None, None, None),
        P(),
        P("s", None),
    )
    return jax.shard_map(
        local,
        mesh=fine,
        in_specs=placed,
        out_specs=(
            P("s", None, "z", mp),
            P("s", None, mp, None),
            P("s", None, None, mp),
        ),
        check_vma=False,
    )
```

```python
import functools

import jax
import jax.numpy as jnp
from jax import lax
from jax.experimental import pallas as pl
from jax.experimental.pallas import tpu as pltpu
from jax.sharding import Mesh, PartitionSpec as P

norm_eps = 1e-05
low_rank_scale = 2.0
CHUNKS = 2
TAIL = 128
SWAP = [(0, 1), (1, 0)]
ODD = [(s, s - 1) for s in range(15, 0, -2)]
EVEN = [(s, s - 1) for s in range(14, 0, -2)]
EVERY = [(s, s - 1) for s in range(15, 0, -1)]
f32 = jnp.float32
bf16 = jnp.bfloat16
contract_last = (((1,), (1,)), ((), ()))
contract_inner = (((1,), (0,)), ((), ()))
AHEAD = 3
TOP_SWAP = [(30, 31), (31, 30)]
RIGHT = [(4 * s + z, 4 * s + (z + 1) % 4) for s in range(15) for z in range(4)]
LEFT = [(4 * s + z, 4 * s + (z + 3) % 4) for s in range(15) for z in range(4)]
PAIRS = [(2 * s + c, 2 * s + 1 - c) for s in range(15) for c in range(2)]


def both_cores(value, axis):
    core = lax.axis_index("c")
    other = lax.ppermute(value, "c", SWAP)
    low = jnp.where(core == 0, value, other)
    high = jnp.where(core == 0, other, value)
    return jnp.concatenate([low, high], axis)


def half_sum(value, axis):
    core = lax.axis_index("c")
    width = value.shape[axis] // 2
    low = lax.slice_in_dim(value, 0, width, axis=axis)
    high = lax.slice_in_dim(value, width, 2 * width, axis=axis)
    mine = jnp.where(core == 0, low, high)
    theirs = jnp.where(core == 0, high, low)
    return mine + lax.ppermute(theirs, "c", SWAP)


def spread(value):
    sent = jnp.broadcast_to(value[None], (4,) + value.shape)
    return lax.all_to_all(sent, "y", 0, 0)


def own_group(low, group):
    rows, cols = low.shape
    row_group = lax.broadcasted_iota(jnp.int32, low.shape, 0) // (rows // group)
    col_group = lax.broadcasted_iota(jnp.int32, low.shape, 1) // (cols // group)
    return jnp.where(row_group == col_group, low, 0.0).astype(bf16)


def message(total, grad_y, gain, inv, x, width_all):
    rows, width = total.shape
    normed_grad = (total * gain).astype(bf16).astype(f32)
    sent = (grad_y.astype(f32) + inv * normed_grad).astype(bf16)
    coef = jnp.sum(normed_grad * x.astype(f32), axis=1, keepdims=True)
    coef = coef * (inv * inv * inv / width_all)
    lane = lax.broadcasted_iota(jnp.int32, (rows, TAIL), 1)
    high = lax.reduce_precision(coef, 8, 7)
    tail = jnp.where(lane == 0, high, jnp.where(lane == 1, coef - high, 0.0)).astype(bf16)
    return sent, tail


def stage_kernel(place_ref, parts_ref, gain_ref, before_any, up_any, down_any, inv_any, x_any, *refs, group):
    weights, refs = refs[:16], refs[16 + 4 :]
    box_any, boxes_any, low_any, grad_any, tail_any = refs[:5]
    before_ref, up_ref, down_ref, inv_ref, x_ref, full, weight, low_ref, grad_ref, tail_ref = refs[5:15]
    box_ref, in_sems, w_sems, out_sems = refs[15:]
    m, ypos, core, zpos = place_ref[0], place_ref[1], place_ref[2], place_ref[3]
    width = x_ref.shape[1]
    width_all = full.shape[1]
    half = width // 2

    def started(source, target, sem):
        copy = pltpu.make_async_copy(source, target, sem)
        copy.start()
        return copy

    before_copy = started(before_any.at[:, m], before_ref, in_sems.at[0])
    up_copy = started(up_any.at[m], up_ref, in_sems.at[1])
    copies = []
    for piece in range(8):
        for side, base in enumerate((core * half, (1 - core) * half)):
            lanes = pl.ds(pl.multiple_of(base, 128), half)
            target = weight.at[pl.ds(piece * half, half), lanes]
            copies.append(started(weights[8 * side + piece], target, w_sems.at[piece, side]))
        if piece == 0:
            down_copy = started(down_any.at[m], down_ref, in_sems.at[2])
            inv_copy = started(inv_any.at[m], inv_ref, in_sems.at[3])
            x_copy = started(x_any.at[m], x_ref, in_sems.at[4])

    tail = parts_ref[:, :, width:].astype(f32)
    coef = jnp.sum(jnp.sum(tail, axis=0), axis=1, keepdims=True)
    before_copy.wait()
    up_copy.wait()
    low = None
    for part in range(4):
        fixed = parts_ref[part, :, :width].astype(f32) - coef * before_ref[part].astype(f32)
        fixed = fixed.astype(bf16)
        first = 2 * lax.rem(zpos - part + 4, 4) * half
        second = (2 * lax.rem(part - zpos + 4, 4) + 1) * half
        full[:, pl.ds(pl.multiple_of(first, 128), half)] = fixed[:, :half]
        full[:, pl.ds(pl.multiple_of(second, 128), half)] = fixed[:, half:]

        @pl.when(part == ypos)
        def _(fixed=fixed):
            grad_ref[...] = fixed

        term = lax.dot_general(
            fixed,
            up_ref[:, part * width : (part + 1) * width],
            contract_last,
            preferred_element_type=f32,
        )
        low = term if low is None else low + term
    grad_copy = started(grad_ref, grad_any.at[m], out_sems.at[0])
    low = own_group(low, group)
    low_ref[...] = low
    low_copy = started(low_ref, low_any.at[m], out_sems.at[1])
    down_copy.wait()
    total = low_rank_scale * lax.dot_general(
        low, down_ref[...], contract_inner, preferred_element_type=f32
    )
    for begin, end in ((0, 2), (2, 4), (4, 6), (6, 7), (7, 8)):
        for copy in copies[2 * begin : 2 * end]:
            copy.wait()
        span = slice(begin * half, end * half)
        total = total + lax.dot_general(
            full[:, span], weight[span], contract_inner, preferred_element_type=f32
        )
    inv_copy.wait()
    x_copy.wait()
    sent, tail = message(
        total, grad_ref[...], gain_ref[...], inv_ref[:, 0:1], x_ref[...], width_all
    )
    box_ref[:, :width] = sent
    box_ref[:, width:] = tail
    tail_ref[...] = tail
    out_copy = started(box_ref, box_any, out_sems.at[4])
    box_copy = started(box_ref, boxes_any.at[m], out_sems.at[2])
    tail_copy = started(tail_ref, tail_any.at[m], out_sems.at[3])
    grad_copy.wait()
    low_copy.wait()
    box_copy.wait()
    tail_copy.wait()
    out_copy.wait()


def run_stage(place, parts, before, up, down, gain, inv, x, weights, kept):
    _, rows, width = x.shape
    width_all = 4 * width
    cols = up.shape[1]
    vmem = pl.BlockSpec(memory_space=pltpu.VMEM)
    any_space = pl.BlockSpec(memory_space=pl.ANY)
    inputs = [place, parts, gain, before, up, down, inv, x, *weights]
    return pl.pallas_call(
        functools.partial(stage_kernel, group=cols // 16),
        in_specs=[pl.BlockSpec(memory_space=pltpu.SMEM), vmem, vmem]
        + [any_space] * (len(inputs) + len(kept) - 3),
        out_specs=[any_space] * (1 + len(kept)),
        scratch_shapes=[
            pltpu.VMEM((4, rows, width), bf16),
            pltpu.VMEM((cols, width_all), bf16),
            pltpu.VMEM((cols, width), bf16),
            pltpu.VMEM((rows, TAIL), f32),
            pltpu.VMEM((rows, width), bf16),
            pltpu.VMEM((rows, width_all), bf16),
            pltpu.VMEM((width_all, width), bf16),
            pltpu.VMEM((rows, cols), bf16),
            pltpu.VMEM((rows, width), bf16),
            pltpu.VMEM((rows, TAIL), bf16),
            pltpu.VMEM((rows, width + TAIL), bf16),
            pltpu.SemaphoreType.DMA((5,)),
            pltpu.SemaphoreType.DMA((8, 2)),
            pltpu.SemaphoreType.DMA((5,)),
        ],
        out_shape=[jax.ShapeDtypeStruct((rows, width + TAIL), bf16)]
        + [jax.ShapeDtypeStruct(k.shape, k.dtype) for k in kept],
        input_output_aliases={len(inputs) + i: 1 + i for i in range(len(kept))},
        compiler_params=pltpu.CompilerParams(vmem_limit_bytes=32 * 1024 * 1024),
        cost_estimate=pl.CostEstimate(
            flops=2 * rows * width * width_all, bytes_accessed=2 * width * width_all, transcendentals=0
        ),
        name="stage",
    )(*inputs, *kept)


def local(
    section_inputs,
    out_grads,
    proj_weight,
    norm_gain,
    adapter_down,
    adapter_up,
    tenant_ids,
    slot_table,
):
    sec = lax.axis_index("s")
    ypos = lax.axis_index("y")
    core = lax.axis_index("c")
    micro = section_inputs.shape[1]
    width_all = section_inputs.shape[3]
    half = proj_weight.shape[1]
    width = 2 * half
    toks = section_inputs.shape[2] // 2
    rank = adapter_down.shape[3]
    rows_all = micro * toks
    group = micro // CHUNKS
    rows = group * toks
    multiplier = low_rank_scale / (toks * 2 * lax.axis_size("z"))

    zpos = lax.axis_index("z")
    x_tokens = lax.dynamic_slice_in_dim(section_inputs[0], core * toks, toks, 1)
    x_y = lax.dynamic_slice_in_dim(x_tokens, ypos * width, width, 2).reshape(rows_all, width)
    x_moved = lax.ppermute(x_y, "s", EVERY)
    first = proj_weight[0][:, :half].T
    second = proj_weight[0][:, half:].T
    empty = (
        jnp.zeros((CHUNKS, rows, width + TAIL), bf16),
        jnp.zeros((CHUNKS, rows, group * rank), bf16),
        jnp.zeros((CHUNKS, rows, width), bf16),
        jnp.zeros((CHUNKS, rows, TAIL), bf16),
    )
    x_moved, first, second, norm_gain, adapter_down, x_tokens, x_y, empty = lax.optimization_barrier(
        (x_moved, first, second, norm_gain, adapter_down, x_tokens, x_y, empty)
    )
    right_1 = lax.ppermute(first, ("s", "z"), RIGHT)
    left_1 = lax.ppermute(second, ("s", "z"), LEFT)

    x_f = x_tokens.reshape(rows_all, width_all).astype(f32)
    inv_rms = lax.rsqrt(jnp.mean(x_f * x_f, axis=-1, keepdims=True) + norm_eps)
    normed_y = x_y.astype(f32) * inv_rms
    x_before = lax.cond(
        sec == 15, lambda x: jnp.zeros((4,) + x.shape, x.dtype), spread, x_moved
    )
    gain_y = both_cores(norm_gain, 1)
    down_y = both_cores(adapter_down[0], 1)
    h_y = (normed_y * gain_y).astype(bf16)

    iota = jnp.arange(micro, dtype=jnp.int32)
    tenant_hot = tenant_ids[:, None] == iota[None, :]
    slot_ids = jnp.sum(jnp.where(tenant_hot, slot_table[0][None, :], 0), axis=1)
    down_sel = down_y[slot_ids]
    up_sel = adapter_up[0][slot_ids]
    low_part = jnp.einsum(
        "mtd,mdr->mtr", h_y.reshape(micro, toks, width), down_sel, preferred_element_type=f32
    )

    def extra(args):
        h_y, low_part = args
        low_in = lax.psum(low_part, "y").astype(bf16)
        return lax.all_gather(h_y, "z"), lax.all_gather(low_in, "z")

    x_before = x_before.reshape(4, CHUNKS, rows, width)
    x_chunk = x_y.reshape(CHUNKS, rows, width)
    inv_chunk = jnp.broadcast_to(inv_rms.reshape(CHUNKS, rows, 1), (CHUNKS, rows, TAIL))
    down_chunk = down_sel.transpose(0, 2, 1).reshape(CHUNKS, group * rank, width)
    up_chunk = up_sel.reshape(CHUNKS, group * rank, width_all)

    def top(args):
        out_grads, first, second, _ = args
        shard = jnp.concatenate([first, second], 0)
        shard_x = lax.ppermute(shard, ("s", "c"), TOP_SWAP)
        grad = lax.dynamic_slice_in_dim(out_grads, core * toks, toks, 1)
        low = jnp.einsum("mtd,mrd->mtr", grad, up_sel, preferred_element_type=f32).astype(bf16)
        adapt = jnp.einsum("mtr,mdr->mtd", low, down_sel, preferred_element_type=f32)
        grad = grad.reshape(rows_all, width_all)
        blocks = jnp.stack([grad[:, i * width : (i + 1) * width] for i in range(4)])
        blocks = lax.all_to_all(blocks, "z", 0, 0).reshape(4 * rows_all, width)
        mine, theirs = (
            lax.dot_general(blocks, w, contract_inner, preferred_element_type=f32).astype(bf16)
            for w in (shard, shard_x)
        )
        terms = jnp.concatenate(
            [jnp.where(core == 0, mine, theirs), jnp.where(core == 0, theirs, mine)], 1
        )
        terms = lax.all_to_all(terms.reshape(4, rows_all, width), "z", 0, 0)
        total = jnp.sum(terms.astype(f32), axis=0)
        total = total + low_rank_scale * adapt.reshape(rows_all, width)
        grad_y = lax.dynamic_slice_in_dim(grad, ypos * width, width, 1)
        sent, tail = message(total, grad_y, gain_y, inv_rms, x_y, width_all)
        boxes = jnp.concatenate([sent, tail], 1).reshape(CHUNKS, rows, width + TAIL)
        member = jnp.arange(rows_all)[:, None] // toks % group == jnp.arange(group)[None, :]
        low = jnp.where(member[:, :, None], low.reshape(rows_all, 1, rank), 0)
        low = low.astype(bf16).reshape(CHUNKS, rows, group * rank)
        tail = tail.reshape(CHUNKS, rows, TAIL)
        return boxes, low, grad_y.reshape(CHUNKS, rows, width), tail

    def swapped(value):
        return lax.ppermute(value, ("s", "c"), PAIRS)

    ready = (x_before, x_chunk, inv_chunk, down_chunk, up_chunk, gain_y, h_y, low_part)
    right_1, left_1, ready = lax.optimization_barrier((right_1, left_1, ready))
    kept = lax.cond(sec == 15, top, lambda args: args[3], (out_grads, first, second, empty))
    boxes_top = lax.ppermute(kept[0], "s", [(15, 14)])
    right_2 = lax.ppermute(right_1, ("s", "z"), RIGHT)
    left_2 = lax.ppermute(left_1, ("s", "z"), LEFT)
    others = [swapped(w) for w in (right_1, left_1)]
    right_2, left_2, others, first, second = lax.optimization_barrier(
        (right_2, left_2, others, first, second)
    )
    right_3 = lax.ppermute(right_2, ("s", "z"), RIGHT)
    left_3 = lax.ppermute(left_2, ("s", "z"), LEFT)
    more = [swapped(w) for w in (first, second, right_2, left_2)]
    right_3, left_3, more, kept, boxes_top, ready = lax.optimization_barrier(
        (right_3, left_3, more, kept, boxes_top, ready)
    )
    x_before, x_chunk, inv_chunk, down_chunk, up_chunk, gain_y, h_y, low_part = ready
    last = [swapped(w) for w in (right_3, left_3)]
    weights = [first, second, right_1, left_1, right_2, left_2, right_3, left_3]
    weights = weights + more[:2] + others + more[2:] + last
    extras = lax.cond(
        sec <= 15 - AHEAD,
        extra,
        lambda args: (
            jnp.zeros((4, rows_all, width), bf16),
            jnp.zeros((4, micro, toks, rank), bf16),
        ),
        (h_y, low_part),
    )

    def pick(array, m):
        return lax.dynamic_index_in_dim(array, m, 0, keepdims=False)

    def step(u, state):
        box, kept = state
        t, m = u // CHUNKS, u % CHUNKS
        turn = 15 - t + m

        def computed(args):
            box, kept = args
            place = jnp.stack([m, ypos, core, zpos]).astype(jnp.int32)
            parts = lax.cond(
                sec == 15, lambda box: jnp.zeros((4,) + box.shape, box.dtype), spread, box
            )
            box, *kept = run_stage(
                place,
                parts,
                x_before,
                up_chunk,
                down_chunk,
                gain_y,
                inv_chunk,
                x_chunk,
                weights,
                kept,
            )
            return box, tuple(kept)

        box, kept = lax.cond(
            (sec == turn) & (sec < 15), computed, lambda args: args, (box, kept)
        )
        part = ((sec == turn) | (sec == turn - 1)) & (turn >= 1) & (turn <= 14)
        kind = jnp.where(part, jnp.where(turn % 2 == 1, 1, 2), 0)
        kind = jnp.where((turn == 15) & (sec == 14) & (m > 0), 3, kind)
        box = lax.switch(
            kind,
            [
                lambda box: box,
                lambda box: lax.ppermute(box, "s", ODD),
                lambda box: lax.ppermute(box, "s", EVEN),
                lambda box: pick(boxes_top, m),
            ],
            box,
        )
        return box, kept

    start = (pick(boxes_top, 0), kept)
    _, kept = lax.fori_loop(0, (15 + CHUNKS) * CHUNKS, step, start)
    boxes, low_all, grad_all, tail_all = kept
    low_all, h_y, low_part = lax.optimization_barrier((low_all, h_y, low_part))
    h_all, low_in_all = lax.cond(
        sec > 15 - AHEAD, lambda args: extra((h_y, low_part)), lambda args: args, extras
    )

    coefs = spread(tail_all)
    coef_sum = jnp.sum(coefs.astype(f32), axis=(0, -1))[..., None]
    new_grads = boxes[:, :, :width].astype(f32) - coef_sum * x_chunk.astype(f32)
    new_grads = new_grads.astype(bf16).reshape(micro, toks, width)
    keep = jnp.where(core == 0, new_grads[:, :, :half], new_grads[:, :, half:])
    give = jnp.where(core == 0, new_grads[:, :, half:], new_grads[:, :, :half])
    got = lax.ppermute(give, "c", SWAP)
    kept = jnp.concatenate(
        [jnp.where(core == 0, keep, got), jnp.where(core == 0, got, keep)], 1
    )

    both = jnp.concatenate(
        [
            grad_all.reshape(rows_all, width),
            jnp.pad(low_all.reshape(rows_all, group * rank), ((0, 0), (0, TAIL - group * rank))),
        ],
        1,
    )
    both = lax.all_gather(both, "z").reshape(4, micro, toks, width + TAIL)
    grads_z = both[..., :width]
    low_z = both[..., width : width + group * rank].reshape(4, micro, toks, group, rank)
    low_z = jnp.sum(low_z.astype(f32), axis=3).astype(bf16)
    hidden_z = h_all.reshape(4, micro, toks, width)
    down_part = multiplier * jnp.einsum(
        "zmtd,zmtr->mdr", hidden_z, low_z, preferred_element_type=f32
    )
    up_part = multiplier * jnp.einsum(
        "zmtr,zmtd->mrd", low_in_all, grads_z, preferred_element_type=f32
    )
    down_acc = half_sum(down_part, 1)
    up_acc = half_sum(up_part, 2)
    slot_hot = slot_ids[None, :] == iota[:, None]
    down_out = jnp.sum(jnp.where(slot_hot[:, :, None, None], down_acc[None], 0.0), axis=1)
    up_out = jnp.sum(jnp.where(slot_hot[:, :, None, None], up_acc[None], 0.0), axis=1)
    return (kept[None], down_out[None], up_out[None])


def solution(mesh):
    fine = Mesh(mesh.devices.reshape(16, 4, 2, 4), ("s", "y", "c", "z"))
    mp = ("y", "c")
    placed = (
        P("s", None, "z", None),
        P(None, "z", None),
        P("s", mp, "z"),
        P("s", mp),
        P("s", None, mp, None),
        P("s", None, None, None),
        P(),
        P("s", None),
    )
    return jax.shard_map(
        local,
        mesh=fine,
        in_specs=placed,
        out_specs=(
            P("s", None, "z", mp),
            P("s", None, mp, None),
            P("s", None, None, mp),
        ),
        check_vma=False,
    )
```
